32 devices in a mesh: gx: 4 (over z), gy: 8 (over y, x, core).
Axes of the slice: x: 2, y: 2, z: 4, core: 2. Of those that a mesh axis runs over, the one named last changes fastest.
Arguments:
- tokens: bfloat16 [8192, 1152], P('gy'), may hold values from -6 to 6
- parents: int32 [32], replicated, may hold values from -1 to 23, as said below
- w_query: bfloat16 [1152, 1024], P('gy', 'gx'), may hold values from -0.1875 to 0.1875
- w_key: bfloat16 [1152, 256], P(('gx', 'gy')), may hold values from -0.1875 to 0.1875
- w_value: bfloat16 [1152, 256], P(('gx', 'gy')), may hold values from -0.1875 to 0.1875
- w_out: bfloat16 [1024, 1152], P('gx', 'gy'), may hold values from -0.1875 to 0.1875
- w_gate: bfloat16 [1152, 6912], P('gy', 'gx'), may hold values from -0.1875 to 0.1875
- w_up: bfloat16 [1152, 6912], P('gy', 'gx'), may hold values from -0.1875 to 0.1875
- w_down: bfloat16 [6912, 1152], P('gx', 'gy'), may hold values from -0.078125 to 0.078125
- g_attn_in: bfloat16 [1152], P('gy'), may hold values from 0.25 to 1.75
- g_attn_out: bfloat16 [1152], P('gy'), may hold values from 0.25 to 1.75
- g_ffn_in: bfloat16 [1152], P('gy'), may hold values from 0.25 to 1.75
- g_ffn_out: bfloat16 [1152], P('gy'), may hold values from 0.25 to 1.75
- g_query: bfloat16 [256], P('gy'), may hold values from 0.25 to 1.75
- g_key: bfloat16 [256], P('gy'), may hold values from 0.25 to 1.75
- cotangent: bfloat16 [8192, 1152], P('gy'), may hold values from -6 to 6
Outputs:
- output: bfloat16 [8192, 1152], P('gy')
- grad_tokens: float32 [8192, 1152], P('gy')
- grad_g_attn_in: float32 [1152], P('gy')
- grad_g_attn_out: float32 [1152], P('gy')
- grad_g_ffn_in: float32 [1152], P('gy')
- grad_g_ffn_out: float32 [1152], P('gy')
- grad_g_query: float32 [256], P('gy')
- grad_g_key: float32 [256], P('gy')
- grad_w_query: float32 [1152, 1024], P('gy', 'gx')
- grad_w_key: float32 [1152, 256], P(('gx', 'gy'))
- grad_w_value: float32 [1152, 256], P(('gx', 'gy'))
- grad_w_out: float32 [1024, 1152], P('gx', 'gy')
- grad_w_gate: float32 [1152, 6912], P('gy', 'gx')
- grad_w_up: float32 [1152, 6912], P('gy', 'gx')
- grad_w_down: float32 [6912, 1152], P('gx', 'gy')
The draws below stay inside these ranges and needn't reach their ends.
Inputs may be any that keep to these rules, and one draw needn't show every extreme that they name: Segments come in trees of 16, aligned runs of 16 segment numbers. In each run, the first 4 form a chain in some order whose first has parent -1, the next 4 all have the chain's last as parent, and the last 8 have the middle 4 as parents, two each. Parents are global segment numbers.
All inputs are finite; a program needn't handle non-finite values.
Results may differ from the reference program's by a relative error of at most 0.022.
Values may be sent and summed in bfloat16 or wider, within the bound.
No kernel may reach another device: no remote copies, remote signals or barrier semaphores. Data moves between devices by JAX's collectives and lax.ppermute only.
A program may use at most 192 MiB of HBM per device.

```python
import jax
import jax.numpy as jnp
from jax import lax

D = 1152
H = 4
HD = 256
FF = 6912
WIN = 512
SEG = 256
TREES = 2
TOKENS = 8192
NANC = 2


def draw_parents(key, part):
    tree_keys = jax.random.split(key, TREES)

    def one_tree(tree_key, tree_number):
        trunk_key, leaf_key = jax.random.split(tree_key)
        trunk_order = jax.random.permutation(trunk_key, 4).astype(jnp.int32)
        leaf_order = jax.random.permutation(leaf_key, 8).astype(jnp.int32)
        tree_base = 16 * tree_number
        trunk_chain = tree_base + trunk_order
        previous = jnp.concatenate([jnp.full((1,), -1, jnp.int32), trunk_chain[:3]])
        trunk_parent = jnp.zeros((4,), jnp.int32).at[trunk_order].set(previous)
        branch_parent = jnp.zeros((4,), jnp.int32) + trunk_chain[3]
        leaf_parent = tree_base + 4 + leaf_order // 2
        return jnp.concatenate([trunk_parent, branch_parent, leaf_parent])
    tables = jax.vmap(one_tree)(tree_keys, jnp.arange(TREES, dtype=jnp.int32))
    return tables.reshape(-1).astype(jnp.int32)


def steps_of(key, dims, cuts, low, top_value):
    factor_of = 1.0
    for dim, blocks in cuts:
        steps = jax.random.uniform(jax.random.fold_in(jax.random.fold_in(key, 6), dim), (blocks,), jnp.float32, low / len(cuts), top_value / len(cuts))
        factor_of = factor_of * jnp.repeat(jnp.exp(steps), dims[dim] // blocks).reshape((-1,) + (1,) * (len(dims) - 1 - dim))
    return factor_of


def noise(own_key, extent, deviation, limit, pieces=(), kind=jnp.bfloat16):
    level = steps_of(own_key, extent, pieces, -0.22, 0.18) if pieces else 1.0
    values = jax.random.normal(own_key, extent, jnp.float32) * deviation * level
    return jnp.minimum(jnp.maximum(values, -limit), limit).astype(kind)


def setup_inputs(seed: int = 0) -> dict:
    splits = jax.random.split(jax.random.key(seed), 17)
    return {
        "tokens": noise(splits[0], (TOKENS, D), 1.0, 6.0, ((0, 8),)),
        "parents": draw_parents(jax.random.fold_in(splits[16], 71), 0),
        "w_query": noise(splits[2], (D, H * HD), D ** -0.5, 0.1875, ((0, 8), (1, 4))),
        "w_key": noise(splits[3], (D, HD), D ** -0.5, 0.1875, ((0, 32),)),
        "w_value": noise(splits[4], (D, HD), D ** -0.5, 0.1875, ((0, 32),)),
        "w_out": noise(splits[5], (H * HD, D), (H * HD) ** -0.5, 0.1875, ((0, 4), (1, 8))),
        "w_gate": noise(splits[6], (D, FF), D ** -0.5, 0.1875, ((0, 8), (1, 4))),
        "w_up": noise(splits[7], (D, FF), D ** -0.5, 0.1875, ((0, 8), (1, 4))),
        "w_down": noise(splits[8], (FF, D), FF ** -0.5, 0.078125, ((0, 4), (1, 8))),
        "g_attn_in": jnp.clip(1.0 + 0.15 * jax.random.normal(splits[9], (D,), jnp.float32), 0.25, 1.75).astype(jnp.bfloat16),
        "g_attn_out": jnp.clip(1.0 + 0.15 * jax.random.normal(splits[10], (D,), jnp.float32), 0.25, 1.75).astype(jnp.bfloat16),
        "g_ffn_in": jnp.clip(1.0 + 0.15 * jax.random.normal(splits[11], (D,), jnp.float32), 0.25, 1.75).astype(jnp.bfloat16),
        "g_ffn_out": jnp.clip(1.0 + 0.15 * jax.random.normal(splits[12], (D,), jnp.float32), 0.25, 1.75).astype(jnp.bfloat16),
        "g_query": jnp.clip(1.0 + 0.15 * jax.random.normal(splits[13], (HD,), jnp.float32), 0.25, 1.75).astype(jnp.bfloat16),
        "g_key": jnp.clip(1.0 + 0.15 * jax.random.normal(splits[14], (HD,), jnp.float32), 0.25, 1.75).astype(jnp.bfloat16),
        "cotangent": noise(splits[15], (TOKENS, D), 1.0, 6.0, ((0, 8),)),
    }


EPSILON = 1e-06
MASKED = -1e+30
HIGH = lax.Precision.HIGHEST

@jax.custom_vjp
def low(v):
    return lax.optimization_barrier(v.astype(jnp.bfloat16)).astype(jnp.float32)

@jax.custom_vjp
def low_back(v):
    return v

def low_keep(v):
    return (low(v), None)

def low_pass(kept, grad):
    return (grad,)

def back_keep(v):
    return (v, None)

def back_low(kept, grad):
    return (low(grad),)
low.defvjp(low_keep, low_pass)
low_back.defvjp(back_keep, back_low)

def matmul(left_side, right_side):
    return jnp.dot(left_side, right_side, precision=HIGH, preferred_element_type=jnp.float32)

def rms_norm(values, gain):
    return values * lax.rsqrt(lax.optimization_barrier(jnp.mean(values * values, axis=-1, keepdims=True)) + EPSILON) * gain

def angles(depth, head_width):
    half_width = head_width // 2
    rates = 10000.0 ** (-jnp.arange(half_width, dtype=jnp.float32) / half_width)
    turned = depth.astype(jnp.float32)[:, None] * rates[None, :]
    return (jnp.cos(turned), jnp.sin(turned))

def rotate(values, cos_table, sin_table):
    half_width = values.shape[-1] // 2
    first_half = values[..., :half_width]
    second_half = values[..., half_width:]
    return jnp.concatenate([first_half * cos_table - second_half * sin_table, second_half * cos_table + first_half * sin_table], axis=-1)

def ancestry(parents, levels):
    lineage = []
    current = parents
    seg_level = jnp.zeros_like(parents)
    for level_step in range(5):
        lineage.append(current)
        seg_level = seg_level + (current >= 0).astype(jnp.int32)
        current = jnp.where(current >= 0, jnp.take(parents, jnp.maximum(current, 0)), -1)
    while len(lineage) < levels:
        lineage.append(jnp.full_like(parents, -1))
    return (seg_level, jnp.stack(lineage[:levels], axis=1))

def path_mask(level_query, level_key, alive_slot, seg_len, window):
    offsets = jnp.arange(seg_len, dtype=jnp.int32)
    depth_query = level_query[:, None] * seg_len + offsets[None, :]
    depth_key = level_key[:, :, None] * seg_len + offsets[None, None, :]
    distance = depth_query[:, :, None, None] - depth_key[:, None, :, :]
    visible = alive_slot[:, None, :, None] & (distance >= 0) & (distance < window)
    return visible.reshape(level_query.shape[0], seg_len, -1)

def tree_attention(queries, key_rows, value_rows, seg_level, lineage):
    seg_count = queries.shape[0]
    own_slot = jnp.arange(seg_count, dtype=jnp.int32)[:, None]
    slots = jnp.concatenate([own_slot, lineage], axis=1)
    alive_slot = slots >= 0
    picked = jnp.maximum(slots, 0).reshape(-1)
    keys_used = jnp.take(key_rows, picked, axis=0).reshape(seg_count, -1, HD)
    values_used = jnp.take(value_rows, picked, axis=0).reshape(seg_count, -1, HD)
    visible = path_mask(seg_level, jnp.take(seg_level, picked).reshape(seg_count, -1), alive_slot, SEG, WIN)
    scores = low_back(jnp.einsum('sqhd,skd->shqk', queries, keys_used, precision=HIGH) * HD ** (-0.5))
    scores = jnp.where(visible[:, None], scores, MASKED)
    row_max = lax.optimization_barrier(jnp.max(scores, axis=-1, keepdims=True))
    weights = jnp.exp(scores - row_max)
    soft_weights = weights / lax.optimization_barrier(jnp.sum(weights, axis=-1, keepdims=True))
    return jnp.einsum('shqk,skd->sqhd', low(soft_weights), values_used, precision=HIGH)

def tree_block(residual, local_table, weights):
    w_query, w_key, w_value, w_out, w_gate, w_up, w_down, gain_in, gain_post, gain_ffn, gain_last, gain_query, gain_key = weights
    seg_count = local_table.shape[0]
    seg_level, lineage = ancestry(local_table, NANC)
    offsets = jnp.arange(SEG, dtype=jnp.int32)
    depth = (seg_level[:, None] * SEG + offsets[None, :]).reshape(-1)
    cos_table, sin_table = angles(depth, HD)
    normed = low(rms_norm(residual, gain_in))
    query_raw = low_back(matmul(normed, w_query)).reshape(-1, H, HD)
    key_raw = low_back(matmul(normed, w_key))
    value_used = low(low_back(matmul(normed, w_value)))
    query_used = low(rotate(rms_norm(query_raw, gain_query), cos_table[:, None], sin_table[:, None]))
    key_used = low(rotate(rms_norm(key_raw, gain_key), cos_table, sin_table))
    heads_out = tree_attention(query_used.reshape(seg_count, SEG, H, HD), key_used.reshape(seg_count, SEG, HD), value_used.reshape(seg_count, SEG, HD), seg_level, lineage)
    heads_low = low(low_back(heads_out.reshape(-1, H * HD)))
    attn_total = low_back(matmul(heads_low, w_out))
    mid_residual = residual + rms_norm(attn_total, gain_post)
    normed_ffn = low(rms_norm(mid_residual, gain_ffn))
    gate_proj = low_back(matmul(normed_ffn, w_gate))
    up_proj = low_back(matmul(normed_ffn, w_up))
    hidden = low(jax.nn.gelu(gate_proj, approximate=True) * up_proj)
    ffn_total = low_back(matmul(hidden, w_down))
    return mid_residual + rms_norm(ffn_total, gain_last)

def forward(parents, residual, *weights):
    tree_rows = residual.reshape(TREES, 16 * SEG, D)
    tree_base = 16 * jnp.arange(TREES, dtype=jnp.int32)[:, None]
    tables = parents.reshape(TREES, 16)
    local_table = jnp.where(tables >= 0, tables - tree_base, -1)

    def one_tree(tree_item):
        return tree_block(tree_item[0], tree_item[1], weights)
    outputs = lax.map(jax.checkpoint(one_tree), (tree_rows, local_table))
    return outputs.reshape(TOKENS, D)

def reference(tokens, parents, w_query, w_key, w_value, w_out, w_gate, w_up, w_down, g_attn_in, g_attn_out, g_ffn_in, g_ffn_out, g_query, g_key, cotangent):
    floats = [item_array.astype(jnp.float32) for item_array in (tokens, w_query, w_key, w_value, w_out, w_gate, w_up, w_down, g_attn_in, g_attn_out, g_ffn_in, g_ffn_out, g_query, g_key)]

    def run_layer(*values):
        return forward(parents, *values)
    result, pull_back = jax.vjp(run_layer, *floats)
    grads = pull_back(cotangent.astype(jnp.float32))
    return (result.astype(jnp.bfloat16), grads[0], grads[8], grads[9], grads[10], grads[11], grads[12], grads[13], grads[1], grads[2], grads[3], grads[4], grads[5], grads[6], grads[7])
```

```python
import math

import jax
import jax.numpy as jnp
from jax import lax
from jax.experimental import pallas as pl
from jax.experimental.pallas import tpu as pltpu
from jax.sharding import Mesh
from jax.sharding import PartitionSpec as P

SEG = 256
EPSILON = 1e-06
MASKED = -1e30
PLANE = ("gb", "ga", "gc")
SWAP = [(0, 1), (1, 0)]
F32 = jnp.float32
BF16 = jnp.bfloat16


def rms_norm(values, gain):
    return values * lax.rsqrt(jnp.mean(values * values, axis=-1, keepdims=True) + EPSILON) * gain


def norm_back(values, gain, incoming):
    r = lax.rsqrt(jnp.mean(values * values, axis=-1, keepdims=True) + EPSILON)
    scaled = gain * incoming
    inner = jnp.mean(values * scaled, axis=-1, keepdims=True)
    return r * scaled - values * (r * r * r) * inner, incoming * values * r


def rotate(values, cos_table, sin_table):
    half_width = values.shape[-1] // 2
    a, b = values[..., :half_width], values[..., half_width:]
    return jnp.concatenate([a * cos_table - b * sin_table, b * cos_table + a * sin_table], axis=-1)


def dot(a, b, dims=(1, 0)):
    return lax.dot_general(
        a, b, (((dims[0],), (dims[1],)), ((), ())), preferred_element_type=F32
    )


def swap(x, axis):
    return lax.ppermute(x, axis, SWAP)


def across(x, distance):
    return lax.ppermute(x, "gx", [(i, i ^ distance) for i in range(4)])


def place(pieces, slots, count):
    rows, width = pieces[0].shape[-2:]
    shape = jax.ShapeDtypeStruct((count, rows, width), pieces[0].dtype)

    def kernel(slot_ref, *refs):
        ins, (out, held, sems) = refs[: len(pieces)], refs[len(pieces) :]
        loads = [
            pltpu.make_async_copy(ref, held.at[i], sems.at[0, i]) for i, ref in enumerate(ins)
        ]
        stores = [
            pltpu.make_async_copy(held.at[i], out.at[slot_ref[i]], sems.at[1, i])
            for i in range(len(pieces))
        ]
        for load in loads:
            load.start()
        for load, store in zip(loads, stores):
            load.wait()
            store.start()
        for store in stores:
            store.wait()

    return pl.pallas_call(
        kernel,
        out_shape=shape,
        in_specs=[pl.BlockSpec(memory_space=pltpu.SMEM)]
        + [pl.BlockSpec(memory_space=pl.ANY)] * len(pieces),
        out_specs=pl.BlockSpec(memory_space=pl.ANY),
        scratch_shapes=[
            pltpu.VMEM((len(pieces), rows, width), pieces[0].dtype),
            pltpu.SemaphoreType.DMA((2, len(pieces))),
        ],
        compiler_params=pltpu.CompilerParams(vmem_limit_bytes=32 * 2**20),
    )(slots, *pieces)


def plane_gather(x):
    if lax.axis_size("ga") != 2:
        return lax.all_gather(x, PLANE, axis=0)
    half = x.shape[0] // 32 * 16
    from_x, from_y = swap(x, "ga"), swap(x, "gb")
    diagonal = jnp.concatenate([swap(from_y[:half], "ga"), swap(from_x[half:], "gb")], axis=0)
    mine = [x, from_x, from_y, diagonal]
    theirs = [swap(piece, "gc") for piece in mine]
    here = lax.axis_index(PLANE)
    slots = jnp.array([0, 2, 4, 6, 1, 3, 5, 7], jnp.int32) ^ here
    return place(mine + theirs, slots, 8)


def plane_scatter(g):
    if lax.axis_size("ga") != 2:
        return lax.psum_scatter(g, PLANE, scatter_dimension=0).astype(F32)
    y, x, c = [lax.axis_index(name) for name in PLANE]
    g = g.reshape((4, 2) + g.shape[1:])

    def pick(values, index, axis):
        return lax.dynamic_index_in_dim(values, index, axis, keepdims=False)

    received = swap(pick(g, 1 - c, 1), "gc")

    def chip(number):
        return pick(pick(g, c, 1), number, 0).astype(F32) + pick(received, number, 0).astype(F32)

    here, by_x, by_y, far = [
        chip(n) for n in (2 * y + x, 2 * y + 1 - x, 2 * (1 - y) + x, 2 * (1 - y) + 1 - x)
    ]
    far = far.astype(BF16)
    half = g.shape[2] // 32 * 16
    got_first = swap(far[:half], "ga")
    got_second = swap(far[half:], "gb")
    send_x = jnp.concatenate([by_x[:half], by_x[half:] + got_second.astype(F32)], axis=0)
    send_y = jnp.concatenate([by_y[:half] + got_first.astype(F32), by_y[half:]], axis=0)
    return here + swap(send_x.astype(BF16), "ga").astype(F32) + swap(
        send_y.astype(BF16), "gb"
    ).astype(F32)


def glu(gate, up):
    return jax.nn.gelu(gate, approximate=True) * up


def body(
    tokens,
    parents,
    w_query,
    w_key,
    w_value,
    w_out,
    w_gate,
    w_up,
    w_down,
    g_attn_in,
    g_attn_out,
    g_ffn_in,
    g_ffn_out,
    g_query,
    g_key,
    cotangent,
):
    column = lax.axis_index(PLANE)
    columns = lax.axis_size(PLANE)
    plane = lax.axis_index("gx")
    planes = lax.axis_size("gx")
    width = tokens.shape[1]
    head_width = w_key.shape[1]
    heads = planes * w_query.shape[1] // head_width
    block, small = w_query.shape[0], w_key.shape[0]
    gains_len = 4 * block + 2 * g_query.shape[0]
    gain_rows = -(-gains_len // (2 * head_width))
    used = block + small + gain_rows
    pack_rows = -(-used // 16) * 16
    pack_width = 2 * head_width

    ffn_mine = jnp.concatenate([w_gate, w_up, w_down.T], axis=0)
    ffn_theirs = across(ffn_mine, 2)
    gains = jnp.concatenate([g_attn_in, g_attn_out, g_ffn_in, g_ffn_out, g_query, g_key])
    gains = jnp.pad(gains, (0, gain_rows * pack_width - gains_len)).reshape(gain_rows, pack_width)
    pack = jnp.concatenate(
        [
            jnp.concatenate([w_query, w_out.T], axis=1),
            jnp.concatenate([w_key, w_value], axis=1),
            gains,
            jnp.zeros((pack_rows - used, pack_width), BF16),
        ],
        axis=0,
    )
    pack = lax.all_gather(pack, "gx", axis=0, tiled=True)
    pack = plane_gather(pack).reshape(columns, planes, pack_rows, pack_width)

    def from_blocks(blocks):
        return blocks.transpose(0, 2, 1, 3).reshape(columns * block, -1)

    wq = from_blocks(pack[:, :, :block, :head_width])
    wo_t = from_blocks(pack[:, :, :block, head_width:])
    wkv = pack[:, :, block : block + small].transpose(1, 0, 2, 3).reshape(width, pack_width)
    gains = pack[:, 0, block + small : used].reshape(columns, -1)[:, :gains_len].astype(F32)
    gain_in, gain_post, gain_ffn, gain_last = [
        gains[:, i * block : (i + 1) * block].reshape(-1) for i in range(4)
    ]
    gain_query, gain_key = [
        gains[:, 4 * block + i * g_query.shape[0] :][:, : g_query.shape[0]].reshape(-1)
        for i in range(2)
    ]

    def ffn_weights(mine):
        stacked = plane_gather(mine).reshape(columns, 3, block, -1)
        return [stacked[:, i].reshape(width, -1) for i in range(3)]

    quarters = [ffn_weights(ffn_mine), ffn_weights(ffn_theirs)]

    def parent_of(segment):
        found = lax.dynamic_index_in_dim(parents, jnp.maximum(segment, 0), 0, keepdims=False)
        return jnp.where(segment >= 0, found, -1)

    def level_of(segment):
        level = jnp.int32(0)
        for _ in range(5):
            segment = parent_of(segment)
            level = level + (segment >= 0).astype(jnp.int32)
        return level

    first = 4 * column
    role = column % 4
    own = first + plane
    own_a = parent_of(own)
    own_b = parent_of(own_a)

    def later(distance):
        return jnp.minimum(own + 4 * distance, parents.shape[0] - 1)

    a1, a2 = parent_of(later(1)), parent_of(later(2))
    b1, b2 = parent_of(a1), parent_of(a2)

    def local(segment):
        return jnp.clip(segment - first, 0, 3)

    pick_1 = local(a1)
    pick_2 = local(jnp.where(role == 0, b2, a2))
    pick_3 = local(b1)
    pick_a, pick_b = local(own_a), local(own_b)
    trees = range(columns // 4)
    route_1 = [(4 * t + i, 4 * t + i + 1) for t in trees for i in (0, 1)]
    route_2 = [(4 * t + i, 4 * t + i + 2) for t in trees for i in (0, 1)]
    route_3 = [(4 * t + i, 4 * t + i + 1) for t in trees for i in (0, 2)]

    def send(x, route):
        return lax.ppermute(x, PLANE, route)

    def send_back(x, route):
        return lax.ppermute(x, PLANE, [(b, a) for a, b in route])

    levels = jnp.stack([level_of(first + i) for i in range(4)])
    depth = (levels[:, None] * SEG + jnp.arange(SEG, dtype=jnp.int32)[None, :]).reshape(-1)
    half_width = head_width // 2
    rates = 10000.0 ** (-jnp.arange(half_width, dtype=F32) / half_width)
    turned = depth.astype(F32)[:, None] * rates[None, :]
    cos_table, sin_table = jnp.cos(turned), jnp.sin(turned)

    def own_rows(x):
        return lax.dynamic_slice_in_dim(x, plane * SEG, SEG, 0)

    def pair_rows(x):
        other = lax.dynamic_slice_in_dim(x, (plane ^ 1) * SEG, SEG, 0)
        return jnp.concatenate([own_rows(x), other], axis=0)

    residual = tokens.astype(F32)
    normed = rms_norm(residual, gain_in).astype(BF16)
    normed_own = own_rows(normed)
    kv_raw = dot(normed, wkv)
    key_raw = kv_raw[:, :head_width]
    key_used = rotate(rms_norm(key_raw, gain_key), cos_table, sin_table).astype(BF16)
    pairs = jnp.concatenate([key_used, kv_raw[:, head_width:].astype(BF16)], axis=1)

    def segment_of(x, number):
        return lax.dynamic_slice_in_dim(x, number * SEG, SEG, 0)

    got_1 = send(segment_of(pairs, pick_1), route_1)
    got_2 = send(segment_of(pairs, pick_2), route_2)
    got_3 = send(jnp.where(role == 2, got_2, segment_of(pairs, pick_3)), route_3)
    slot_a = jnp.where(
        role == 0, segment_of(pairs, pick_a), jnp.where(role == 3, got_2, got_1)
    )
    slot_b = jnp.where(
        role == 0, segment_of(pairs, pick_b), jnp.where(role == 2, got_2, got_3)
    )
    slots = jnp.concatenate([own_rows(pairs), slot_a, slot_b], axis=0)
    keys, values = slots[:, :head_width], slots[:, head_width:]
    cos_own, sin_own = own_rows(cos_table)[:, None], own_rows(sin_table)[:, None]
    query_raw = dot(normed_own, wq).reshape(SEG, heads, head_width)
    queries = rotate(rms_norm(query_raw, gain_query), cos_own, sin_own).astype(BF16)
    offset = jnp.arange(SEG, dtype=jnp.int32)
    at_query, at_key = offset[:, None], offset[None, :]
    visible = jnp.concatenate(
        [
            at_key <= at_query,
            jnp.broadcast_to(own_a >= 0, (SEG, SEG)),
            (at_key > at_query) & (own_b >= 0),
        ],
        axis=1,
    )
    score_scale = head_width ** (-0.5)
    scores = jnp.einsum("qhd,kd->hqk", queries, keys, preferred_element_type=F32) * score_scale
    scores = jnp.where(visible[None], scores, MASKED)
    weights = jnp.exp(scores - jnp.max(scores, axis=-1, keepdims=True))
    probs = weights / jnp.sum(weights, axis=-1, keepdims=True)
    probs_low = probs.astype(BF16)
    heads_low = jnp.einsum("hqk,kd->qhd", probs_low, values, preferred_element_type=F32)
    heads_low = heads_low.reshape(SEG, -1).astype(BF16)

    heads_pair = jnp.concatenate([heads_low, across(heads_low, 1)], axis=0)
    attn = dot(heads_pair, wo_t, (1, 1))
    upstream = pair_rows(cotangent).astype(F32)
    mid = pair_rows(residual) + rms_norm(attn, gain_post)
    normed_ffn = rms_norm(mid, gain_ffn).astype(BF16)
    parts = []
    ffn_part = 0.0
    for gate_w, up_w, down_w in quarters:
        gate, up = dot(normed_ffn, gate_w), dot(normed_ffn, up_w)
        hidden = glu(gate, up).astype(BF16)
        parts.append((gate, up, hidden))
        ffn_part = ffn_part + dot(hidden, down_w, (1, 1))
    ffn_own = ffn_part[:SEG] + across(ffn_part[SEG:].astype(BF16), 1).astype(F32)
    ffn = jnp.concatenate([ffn_own, across(ffn_own.astype(BF16), 1).astype(F32)], axis=0)
    output = (mid[:SEG] + rms_norm(ffn_own, gain_last)).astype(BF16)
    output = lax.all_gather(output, "gx", axis=0, tiled=True)

    d_ffn, d_gain_last = norm_back(ffn, gain_last, upstream)
    d_ffn_low = d_ffn.astype(BF16)
    back = 0.0
    ffn_grads = []
    for (gate, up, hidden), (gate_w, up_w, down_w) in zip(parts, quarters):
        d_hidden = dot(d_ffn_low, down_w)
        d_gate, d_up = jax.vjp(glu, gate, up)[1](d_hidden)
        d_gate, d_up = d_gate.astype(BF16), d_up.astype(BF16)
        back = back + dot(d_gate, gate_w, (1, 1)) + dot(d_up, up_w, (1, 1))
        made = [
            dot(normed_ffn, d_gate, (0, 0)),
            dot(normed_ffn, d_up, (0, 0)),
            dot(d_ffn_low, hidden, (0, 0)),
        ]
        made = [m.astype(BF16).reshape(columns, block, -1) for m in made]
        ffn_grads.append(jnp.concatenate(made, axis=1))
    d_normed_ffn = back[:SEG] + across(back[SEG:].astype(BF16), 1).astype(F32)
    grads_theirs = plane_scatter(ffn_grads[1])
    grads_mine = plane_scatter(ffn_grads[0])
    ffn_grad = grads_mine + across(grads_theirs.astype(BF16), 2).astype(F32)

    d_mid_add, d_gain_ffn = norm_back(mid[:SEG], gain_ffn, d_normed_ffn)
    d_mid = upstream[:SEG] + d_mid_add
    d_attn, d_gain_post = norm_back(attn[:SEG], gain_post, d_mid)
    d_attn_low = d_attn.astype(BF16)
    grad_out_t = dot(d_attn_low, heads_low, (0, 0))
    d_heads = dot(d_attn_low, wo_t).astype(BF16).reshape(SEG, heads, head_width)
    d_probs = jnp.einsum("qhd,kd->hqk", d_heads, values, preferred_element_type=F32)
    d_scores = probs * (d_probs - jnp.sum(d_probs * probs, axis=-1, keepdims=True))
    d_scores = d_scores.astype(BF16)
    d_keys = jnp.einsum("hqk,qhd->kd", d_scores, queries, preferred_element_type=F32)
    d_values = jnp.einsum("hqk,qhd->kd", probs_low, d_heads, preferred_element_type=F32)
    d_slots = jnp.concatenate([d_keys * score_scale, d_values], axis=1)
    d_self, d_a, d_b = d_slots[:SEG], d_slots[SEG : 2 * SEG], d_slots[2 * SEG :]
    back_1 = send_back(d_a.astype(BF16), route_1)
    back_3 = send_back(d_b.astype(BF16), route_3)
    d_b_far = jnp.where(role == 2, d_b + back_3.astype(F32), 0.0)
    back_2 = send_back(jnp.where(role == 3, d_a, d_b_far).astype(BF16), route_2)
    near = role == 0
    terms = [
        (plane, d_self),
        (jnp.where(near & (own_a >= 0), pick_a, -1), d_a),
        (jnp.where(near & (own_b >= 0), pick_b, -1), d_b),
        (jnp.where(role <= 1, pick_1, -1), back_1.astype(F32)),
        (jnp.where(role <= 1, pick_2, -1), back_2.astype(F32)),
        (jnp.where(near, pick_3, -1), back_3.astype(F32)),
    ]
    d_window = jnp.concatenate(
        [sum(jnp.where(at == i, term, 0.0) for at, term in terms) for i in range(4)], axis=0
    )
    d_own = lax.psum_scatter(
        d_window.astype(BF16), "gx", scatter_dimension=0, tiled=True
    ).astype(F32)
    d_queries = jnp.einsum("hqk,kd->qhd", d_scores, keys, preferred_element_type=F32)
    d_query_raw, d_gain_query = norm_back(
        query_raw, gain_query, rotate(d_queries * score_scale, cos_own, -sin_own)
    )
    d_key_raw, d_gain_key = norm_back(
        own_rows(key_raw),
        gain_key,
        rotate(d_own[:, :head_width], cos_own[:, 0], -sin_own[:, 0]),
    )
    d_query_low = d_query_raw.reshape(SEG, -1).astype(BF16)
    d_kv_low = jnp.concatenate([d_key_raw, d_own[:, head_width:]], axis=1).astype(BF16)
    d_normed = dot(d_query_low, wq, (1, 1)) + dot(d_kv_low, wkv, (1, 1))
    d_res_add, d_gain_in = norm_back(own_rows(residual), gain_in, d_normed)
    grad_tokens = lax.all_gather(
        (d_mid + d_res_add).astype(BF16), "gx", axis=0, tiled=True
    ).astype(F32)

    def to_blocks(grad):
        return grad.astype(BF16).reshape(columns, block, planes, -1).transpose(0, 2, 1, 3)

    grad_query = to_blocks(dot(normed_own, d_query_low, (0, 0)))
    grad_out = to_blocks(grad_out_t)
    grad_kv = dot(normed_own, d_kv_low, (0, 0)).astype(BF16)
    grad_kv = grad_kv.reshape(planes, columns, small, -1).transpose(1, 0, 2, 3)
    gain_sums = [
        d_gain_in.sum(0),
        d_gain_post.sum(0),
        d_gain_ffn.sum(0),
        d_gain_last[:SEG].sum(0),
        d_gain_query.sum((0, 1)),
        d_gain_key.sum(0),
    ]
    gain_sums = jnp.concatenate([g.reshape(columns, -1) for g in gain_sums], axis=1).astype(BF16)
    gain_sums = jnp.pad(gain_sums, ((0, 0), (0, gain_rows * pack_width - gains_len)))
    gain_sums = jnp.broadcast_to(
        gain_sums.reshape(columns, 1, gain_rows, pack_width),
        (columns, planes, gain_rows, pack_width),
    )
    grads = jnp.concatenate(
        [
            jnp.concatenate([grad_query, grad_out], axis=3),
            grad_kv,
            gain_sums,
            jnp.zeros((columns, planes, pack_rows - used, pack_width), BF16),
        ],
        axis=2,
    )
    grads = plane_scatter(grads.reshape(columns, planes * pack_rows, pack_width))
    gain_grads = lax.all_gather(
        grads[block + small : used].astype(BF16), "gx", axis=0
    ).astype(F32).sum(0).reshape(-1)
    grads = lax.psum_scatter(
        grads.astype(BF16), "gx", scatter_dimension=0, tiled=True
    ).astype(F32)
    return (
        output,
        grad_tokens,
        gain_grads[:block],
        gain_grads[block : 2 * block],
        gain_grads[2 * block : 3 * block],
        gain_grads[3 * block : 4 * block],
        gain_grads[4 * block : 4 * block + g_query.shape[0]],
        gain_grads[4 * block + g_query.shape[0] : gains_len],
        grads[:block, :head_width],
        grads[block : block + small, :head_width],
        grads[block : block + small, head_width:],
        grads[:block, head_width:].T,
        ffn_grad[:block],
        ffn_grad[block : 2 * block],
        ffn_grad[2 * block :].T,
    )


def solution(mesh):
    side = math.isqrt(mesh.shape["gy"] // 2)
    split = Mesh(mesh.devices.reshape(mesh.shape["gx"], side, side, 2), ("gx",) + PLANE)
    whole = ("gx",) + PLANE
    return jax.shard_map(
        body,
        mesh=split,
        in_specs=(
            P(PLANE, None),
            P(),
            P(PLANE, "gx"),
            P(whole, None),
            P(whole, None),
            P("gx", PLANE),
            P(PLANE, "gx"),
            P(PLANE, "gx"),
            P("gx", PLANE),
            P(PLANE),
            P(PLANE),
            P(PLANE),
            P(PLANE),
            P(PLANE),
            P(PLANE),
            P(PLANE, None),
        ),
        out_specs=(
            P(PLANE, None),
            P(PLANE, None),
            P(PLANE),
            P(PLANE),
            P(PLANE),
            P(PLANE),
            P(PLANE),
            P(PLANE),
            P(PLANE, "gx"),
            P(whole, None),
            P(whole, None),
            P("gx", PLANE),
            P(PLANE, "gx"),
            P(PLANE, "gx"),
            P("gx", PLANE),
        ),
        check_vma=False,
    )
```

```python
import math

import jax
import jax.numpy as jnp
from jax import lax
from jax.experimental import pallas as pl
from jax.experimental.pallas import tpu as pltpu
from jax.sharding import Mesh
from jax.sharding import PartitionSpec as P

SEG = 256
EPSILON = 1e-06
MASKED = -1e30
PLANE = ("gb", "ga", "gc")
SWAP = [(0, 1), (1, 0)]
F32 = jnp.float32
BF16 = jnp.bfloat16


def rms_norm(values, gain):
    return values * lax.rsqrt(jnp.mean(values * values, axis=-1, keepdims=True) + EPSILON) * gain


def norm_back(values, gain, incoming):
    r = lax.rsqrt(jnp.mean(values * values, axis=-1, keepdims=True) + EPSILON)
    scaled = gain * incoming
    inner = jnp.mean(values * scaled, axis=-1, keepdims=True)
    return r * scaled - values * (r * r * r) * inner, incoming * values * r


def rotate(values, cos_table, sin_table):
    half_width = values.shape[-1] // 2
    a, b = values[..., :half_width], values[..., half_width:]
    return jnp.concatenate([a * cos_table - b * sin_table, b * cos_table + a * sin_table], axis=-1)


def dot(a, b, dims=(1, 0)):
    return lax.dot_general(
        a, b, (((dims[0],), (dims[1],)), ((), ())), preferred_element_type=F32
    )


def swap(x, axis):
    return lax.ppermute(x, axis, SWAP)


def across(x, distance):
    return lax.ppermute(x, "gx", [(i, i ^ distance) for i in range(4)])


def tie(*values):
    return lax.optimization_barrier(values)


def cost(microseconds):
    flops = int(microseconds * 0.6 * 1.15e9)
    return pl.CostEstimate(flops=flops, bytes_accessed=0, transcendentals=0)


def whole(array_or_space):
    return pl.BlockSpec(memory_space=array_or_space)


def params(mib):
    return pltpu.CompilerParams(vmem_limit_bytes=mib * 2**20)


def square():
    return lax.axis_size("ga") == 2


def halves(x):
    half = x.shape[0] // 32 * 16 or x.shape[0] // 2
    return x[:half], x[half:]


def send_near(x):
    return swap(x, "ga"), swap(x, "gb")


def send_far(from_x, from_y):
    return swap(halves(from_y)[0], "ga"), swap(halves(from_x)[1], "gb")


def collect(pieces, rows):
    count = len(pieces)
    starts = [0, rows, 2 * rows, 3 * rows, 3 * rows + pieces[3].shape[0]]
    shape = (4 * rows,) + pieces[0].shape[1:]

    def kernel(*refs):
        ins, (out, held, sems) = refs[:count], refs[count:]
        spots = [pl.ds(start, piece.shape[0]) for start, piece in zip(starts, pieces)]
        loads = [
            pltpu.make_async_copy(ref, held.at[spot], sems.at[0, i])
            for i, (ref, spot) in enumerate(zip(ins, spots))
        ]
        stores = [
            pltpu.make_async_copy(held.at[spot], out.at[spot], sems.at[1, i])
            for i, spot in enumerate(spots)
        ]
        for load in loads:
            load.start()
        for load, store in zip(loads, stores):
            load.wait()
            store.start()
        for store in stores:
            store.wait()

    return pl.pallas_call(
        kernel,
        out_shape=jax.ShapeDtypeStruct(shape, pieces[0].dtype),
        in_specs=[whole(pl.ANY)] * count,
        out_specs=whole(pl.ANY),
        scratch_shapes=[pltpu.VMEM(shape, pieces[0].dtype), pltpu.SemaphoreType.DMA((2, count))],
        compiler_params=params(24),
        cost_estimate=cost(4),
    )(*pieces)


def chip_slots():
    here = lax.axis_index(PLANE)
    return jnp.array([0, 2, 4, 6, 1, 3, 5, 7], jnp.int32) ^ here


def unpack(pieces, block, head_width, gain_spot, gain_rows):
    four, rows, width = pieces[0].shape
    planes = four // 4
    rest = rows - block
    small = block // planes
    count = len(pieces)
    jobs = [(i, 4 * chip + h, 4 * i + chip, h) for i in range(2) for chip in range(4) for h in range(planes)]

    def kernel(slot_ref, *refs):
        ins, (wq, wo, wkv, gains, other, sems) = refs[:count], refs[count:]
        copies = []
        for n, (i, j, at_slot, h) in enumerate(jobs):
            slot = slot_ref[at_slot]
            at = pl.ds(pl.multiple_of(slot * block, 16), block)
            to = pl.ds(h * head_width, head_width)
            parts = [
                (ins[i].at[j, pl.ds(0, block), pl.ds(0, head_width)], wq.at[at, to]),
                (ins[i].at[j, pl.ds(0, block), pl.ds(head_width, head_width)], wo.at[at, to]),
                (ins[i].at[j, pl.ds(block, rest), :], other.at[slot, h]),
            ]
            copies += [
                pltpu.make_async_copy(a, b, sems.at[n, m]) for m, (a, b) in enumerate(parts)
            ]
        for copy in copies:
            copy.start()
        for copy in copies:
            copy.wait()
        for c in range(8):
            gains[c] = other[c, 0, gain_spot : gain_spot + gain_rows, :]
        for h in range(planes):
            wkv[h * 8 * small : (h + 1) * 8 * small] = jnp.concatenate(
                [other[c, h, :small, :].astype(F32) for c in range(8)], axis=0
            ).astype(BF16)

    matrix = jax.ShapeDtypeStruct((8 * block, planes * head_width), BF16)
    return pl.pallas_call(
        kernel,
        out_shape=[
            matrix,
            matrix,
            jax.ShapeDtypeStruct((8 * block, width), BF16),
            jax.ShapeDtypeStruct((8, gain_rows, width), BF16),
        ],
        in_specs=[whole(pltpu.SMEM)] + [whole(pl.ANY)] * count,
        out_specs=[whole(pltpu.VMEM)] * 4,
        scratch_shapes=[
            pltpu.VMEM((8, planes, rest, width), BF16),
            pltpu.SemaphoreType.DMA((len(jobs), 3)),
        ],
        compiler_params=params(24),
        cost_estimate=cost(4.3),
    )(chip_slots(), *pieces)


def core_rows(ref, core, block):
    return jnp.concatenate(
        [ref[pl.ds(pl.multiple_of((2 * k + core) * block, 16), block), :] for k in range(4)],
        axis=0,
    )


def ffn_weight_grads(core, normed_t, d_ffn_t, d_gate, d_up, hidden, block):
    units = d_gate.shape[1]

    def kernel(core_ref, normed_ref, d_ffn_ref, gate_ref, up_ref, hidden_ref, out):
        m = pl.program_id(0)

        def run(left, right):
            rows = core_rows(left, core_ref[0], block)
            for n in range(0, units, 256):
                w = min(256, units - n)
                made = dot(rows, right[:, n : n + w]).astype(BF16)
                out[:, :, n : n + w] = made.reshape(4, block, w)

        for number, (left, right) in enumerate(
            ((normed_ref, gate_ref), (normed_ref, up_ref), (d_ffn_ref, hidden_ref))
        ):
            pl.when(m == number)(lambda left=left, right=right: run(left, right))

    def full(x):
        return pl.BlockSpec(x.shape, lambda m, c: (0, 0))

    ins = (normed_t, d_ffn_t, d_gate, d_up, hidden)
    return pl.pallas_call(
        kernel,
        grid_spec=pltpu.PrefetchScalarGridSpec(
            num_scalar_prefetch=1,
            grid=(3,),
            in_specs=[full(x) for x in ins],
            out_specs=pl.BlockSpec((4, block, units), lambda m, c: (0, m, 0)),
        ),
        out_shape=jax.ShapeDtypeStruct((4, 3 * block, units), BF16),
        compiler_params=params(48),
        cost_estimate=cost(6.7),
    )(core.reshape(1), *ins)


def attention_weight_grads(core, normed_t, d_query, d_attn_t, heads_low, other, block, planes):
    head_width = d_query.shape[1] // planes
    more = other.shape[1] // planes
    rows_all = block + more

    def kernel(core_ref, normed_ref, query_ref, d_attn_ref, heads_ref, other_ref, out):
        for half, (left, right) in enumerate(((normed_ref, query_ref), (d_attn_ref, heads_ref))):
            rows = core_rows(left, core_ref[0], block)
            for h in range(planes):
                made = dot(rows, right[:, h * head_width : (h + 1) * head_width]).astype(BF16)
                out[:, h * rows_all : h * rows_all + block, half * head_width : (half + 1) * head_width] = (
                    made.reshape(4, block, head_width)
                )
        for chip in range(4):
            for h in range(planes):
                out[chip, h * rows_all + block : (h + 1) * rows_all] = other_ref[
                    2 * chip + core_ref[0], h * more : (h + 1) * more
                ]

    return pl.pallas_call(
        kernel,
        out_shape=jax.ShapeDtypeStruct((4, planes * rows_all, 2 * head_width), BF16),
        in_specs=[whole(pltpu.SMEM)] + [whole(pltpu.VMEM)] * 5,
        out_specs=whole(pltpu.VMEM),
        compiler_params=params(32),
        cost_estimate=cost(2.5),
    )(core.reshape(1), normed_t, d_query, d_attn_t, heads_low, other)


class Scatter:
    def __init__(self, keep, received):
        y, x = lax.axis_index("gb"), lax.axis_index("ga")
        self.pick = lambda n: lax.dynamic_index_in_dim(keep, n, 0, keepdims=False).astype(
            F32
        ) + lax.dynamic_index_in_dim(received, n, 0, keepdims=False).astype(F32)
        self.here, self.x, self.y = 2 * y + x, 2 * y + 1 - x, 2 * (1 - y) + x
        self.far = 2 * (1 - y) + 1 - x

    def send_far(self):
        first, second = halves(self.pick(self.far).astype(BF16))
        return swap(first, "ga"), swap(second, "gb")

    def near_blocks(self, got_first, got_second):
        (x0, x1), (y0, y1) = halves(self.pick(self.x)), halves(self.pick(self.y))
        to_x = jnp.concatenate([x0, x1 + got_second.astype(F32)], axis=0)
        to_y = jnp.concatenate([y0 + got_first.astype(F32), y1], axis=0)
        return to_x.astype(BF16), to_y.astype(BF16)

    def send_near(self, got_first, got_second):
        to_x, to_y = self.near_blocks(got_first, got_second)
        return swap(to_x, "ga"), swap(to_y, "gb")

    def total(self, got_x, got_y):
        return self.pick(self.here) + got_x.astype(F32) + got_y.astype(F32)


def plane_scatter(g):
    if not square():
        return lax.psum_scatter(g, PLANE, scatter_dimension=0).astype(F32)
    c = lax.axis_index("gc")
    g = g.reshape((4, 2) + g.shape[1:])
    keep = lax.dynamic_index_in_dim(g, c, 1, keepdims=False)
    received = swap(lax.dynamic_index_in_dim(g, 1 - c, 1, keepdims=False), "gc")
    work = Scatter(keep, received)
    return work.total(*work.send_near(*work.send_far()))


GELU_A = 0.7978845608028654
GELU_B = 0.044715


def row_scale(values):
    return lax.rsqrt(jnp.mean(values * values, axis=-1, keepdims=True) + EPSILON)


def full(x):
    return pl.BlockSpec(x.shape, lambda *_: (0,) * len(x.shape))


def like(shape, dtype=F32):
    return jax.ShapeDtypeStruct(shape, dtype)


def prefetch_call(kernel, scalars, grid, ins, in_specs, outs, out_specs, scratch=(), mib=48, us=3):
    return pl.pallas_call(
        kernel,
        grid_spec=pltpu.PrefetchScalarGridSpec(
            num_scalar_prefetch=1,
            grid=grid,
            in_specs=in_specs,
            out_specs=out_specs,
            scratch_shapes=scratch,
        ),
        out_shape=outs,
        compiler_params=params(mib),
        cost_estimate=cost(us),
    )(scalars, *ins)


def flags_kernel(parents, spot):
    segments = parents.shape[0]

    def kernel(parents_ref, spot_ref, out):
        def parent_of(segment):
            found = parents_ref[jnp.maximum(segment, 0)]
            return jnp.where(segment >= 0, found, -1)

        column, plane = spot_ref[0], spot_ref[1]
        first = 4 * column
        own = first + plane

        def later(distance):
            return parent_of(jnp.minimum(own + 4 * distance, segments - 1))

        def local(segment):
            return jnp.clip(segment - first, 0, 3)

        role = lax.rem(column, 4)
        a, a1, a2 = parent_of(own), later(1), later(2)
        b, b1, b2 = parent_of(a), parent_of(a1), parent_of(a2)
        made = [
            role,
            plane,
            local(a),
            local(b),
            (a >= 0).astype(jnp.int32),
            (b >= 0).astype(jnp.int32),
            local(a1),
            local(jnp.where(role == 0, b2, a2)),
            local(b1),
        ]
        for i in range(4):
            segment, level = first + i, jnp.int32(0)
            for _ in range(5):
                segment = parent_of(segment)
                level = level + (segment >= 0).astype(jnp.int32)
            made.append(level)
        for i, value in enumerate(made):
            out[i] = value

    return pl.pallas_call(
        kernel,
        out_shape=like((13,), jnp.int32),
        in_specs=[whole(pltpu.SMEM)] * 2,
        out_specs=whole(pltpu.SMEM),
    )(parents, spot)


def key_value_kernel(flags, tokens, gain_in, wkv, gain_key, cos_table, sin_table):
    rows, width = tokens.shape
    head = wkv.shape[1] // 2
    half = head // 2

    def kernel(f, t_ref, gain_ref, w_ref, key_gain_ref, c_ref, s_ref, pairs, normed, raw, *sends):
        values = t_ref[...].astype(F32)
        low = (values * row_scale(values) * gain_ref[...]).astype(BF16)
        made = dot(low, w_ref[...])
        key = made[:, :head]
        scaled = key * row_scale(key) * key_gain_ref[...]
        pair = jnp.concatenate(
            [rotate(scaled, c_ref[...], s_ref[...]), made[:, head:]], axis=1
        ).astype(BF16)
        pairs[...] = pair
        for n in range(3):

            @pl.when(pl.program_id(0) == f[6 + n])
            def _(n=n):
                sends[n][...] = pair

        @pl.when(pl.program_id(0) == f[1])
        def _():
            normed[...] = low
            raw[...] = key

    def rows_of(x):
        return pl.BlockSpec((SEG, x), lambda i, p: (i, 0))

    return prefetch_call(
        kernel,
        flags,
        (rows // SEG,),
        (tokens, gain_in, wkv, gain_key, cos_table, sin_table),
        [rows_of(width), full(gain_in), full(wkv), full(gain_key), rows_of(half), rows_of(half)],
        [like((rows, 2 * head), BF16), like((SEG, width), BF16), like((SEG, head))]
        + [like((SEG, 2 * head), BF16)] * 3,
        [
            rows_of(2 * head),
            pl.BlockSpec((SEG, width), lambda i, p: (0, 0)),
            pl.BlockSpec((SEG, head), lambda i, p: (0, 0)),
        ]
        + [pl.BlockSpec((SEG, 2 * head), lambda i, p: (0, 0))] * 3,
        us=6,
    )


def query_kernel(plane, normed, wq, gain_query, cos_table, sin_table, head):
    width, total = wq.shape
    half = head // 2

    def kernel(plane_ref, n_ref, w_ref, gain_ref, c_ref, s_ref, query, raw):
        made = dot(n_ref[...], w_ref[...])
        raw[...] = made
        scaled = made * row_scale(made) * gain_ref[...]
        query[...] = rotate(scaled, c_ref[...], s_ref[...]).astype(BF16)

    by_head = pl.BlockSpec((SEG, head), lambda h, p: (0, h))
    table = pl.BlockSpec((SEG, half), lambda h, p: (p[0], 0))
    return prefetch_call(
        kernel,
        plane.reshape(1),
        (total // head,),
        (normed, wq, gain_query, cos_table, sin_table),
        [full(normed), pl.BlockSpec((width, head), lambda h, p: (0, h)), full(gain_query), table, table],
        [like((SEG, total), BF16), like((SEG, total))],
        [by_head, by_head],
        us=2.3,
    )


def visible_pairs(alive_a, alive_b):
    at_query = lax.broadcasted_iota(jnp.int32, (SEG, 3 * SEG), 0)
    spot = lax.broadcasted_iota(jnp.int32, (SEG, 3 * SEG), 1)
    own = (spot < SEG) & (spot <= at_query)
    above = (spot >= SEG) & (spot < 2 * SEG) & (alive_a > 0)
    top = (spot - 2 * SEG > at_query) & (alive_b > 0)
    return own | above | top


def softmax_of(query, keys, scale, alive_a, alive_b):
    scores = dot(query, keys, (1, 1)) * scale
    scores = jnp.where(visible_pairs(alive_a, alive_b), scores, MASKED)
    weights = jnp.exp(scores - jnp.max(scores, axis=-1, keepdims=True))
    return weights / jnp.sum(weights, axis=-1, keepdims=True)


def attention_kernel(flags, query, pairs, got_1, got_2, got_3):
    total = query.shape[1]
    head = pairs.shape[1] // 2

    def kernel(f, q_ref, pairs_ref, g1, g2, g3, heads, slots):
        @pl.when(pl.program_id(0) == 0)
        def _():
            role = f[0]

            def near(n):
                return pairs_ref[pl.ds(pl.multiple_of(n * SEG, SEG), SEG), :]

            slots[:SEG] = near(f[1])

            @pl.when(role == 0)
            def _():
                slots[SEG : 2 * SEG] = near(f[2])
                slots[2 * SEG :] = near(f[3])

            @pl.when(role == 1)
            def _():
                slots[SEG : 2 * SEG] = g1[...]
                slots[2 * SEG :] = g3[...]

            @pl.when(role == 2)
            def _():
                slots[SEG : 2 * SEG] = g1[...]
                slots[2 * SEG :] = g2[...]

            @pl.when(role == 3)
            def _():
                slots[SEG : 2 * SEG] = g2[...]
                slots[2 * SEG :] = g3[...]

        probs = softmax_of(q_ref[...], slots[:, :head], head**-0.5, f[4], f[5])
        heads[...] = dot(probs.astype(BF16), slots[:, head:]).astype(BF16)

    by_head = pl.BlockSpec((SEG, head), lambda h, f: (0, h))
    ins = (query, pairs, got_1, got_2, got_3)
    return prefetch_call(
        kernel,
        flags,
        (total // head,),
        ins,
        [by_head] + [full(x) for x in ins[1:]],
        [like((SEG, total), BF16), like((3 * SEG, 2 * head), BF16)],
        [by_head, pl.BlockSpec((3 * SEG, 2 * head), lambda h, f: (0, 0))],
        us=5.4,
    )


def middle_kernel(plane, heads_own, heads_got, wo_t, tokens, gain_post, gain_ffn):
    width, total = wo_t.shape

    def kernel(p, own, got, w_ref, t_ref, post_ref, gain_ref, attn, mid, normed):
        i = pl.program_id(0)

        def run(heads):
            made = dot(heads[...], w_ref[...], (1, 1))

            @pl.when(i == 0)
            def _():
                attn[...] = made

            middle = t_ref[...].astype(F32) + made * row_scale(made) * post_ref[...]
            mid[...] = middle
            normed[...] = (middle * row_scale(middle) * gain_ref[...]).astype(BF16)

        pl.when(i == 0)(lambda: run(own))
        pl.when(i == 1)(lambda: run(got))

    rows = pl.BlockSpec((SEG, width), lambda i, p: (i, 0))
    return prefetch_call(
        kernel,
        plane.reshape(1),
        (2,),
        (heads_own, heads_got, wo_t, tokens, gain_post, gain_ffn),
        [
            full(heads_own),
            full(heads_got),
            full(wo_t),
            pl.BlockSpec((SEG, width), lambda i, p: (p[0] ^ i, 0)),
            full(gain_post),
            full(gain_ffn),
        ],
        [like((SEG, width)), like((2 * SEG, width)), like((2 * SEG, width), BF16)],
        [pl.BlockSpec((SEG, width), lambda i, p: (0, 0)), rows, rows],
        us=4.5,
    )


def both_cores(pieces):
    return pieces + [(swap(piece, "gc"), row, slot + 1) for piece, row, slot in pieces]


class Blocks:
    def __init__(self, pieces, block):
        self.jobs = []
        if block is None:
            self.pieces = tuple(pieces)
            self.width, self.units = pieces[0].shape
            self.slots = jnp.zeros((1,), jnp.int32)
            self.jobs = [(m, 0, m, 0, self.width, None) for m in range(3)]
            return
        self.pieces = tuple(piece for piece, _, _ in pieces)
        self.units = self.pieces[0].shape[1]
        self.width = 8 * block
        here = lax.axis_index(PLANE)
        self.slots = jnp.array([slot for _, _, slot in pieces], jnp.int32)
        self.slots = (self.slots ^ here) * block
        for i, (piece, start, _) in enumerate(pieces):
            for m in range(3):
                low, high = max(start, m * block), min(start + piece.shape[0], (m + 1) * block)
                if low < high:
                    self.jobs.append((i, low - start, m, low - m * block, high - low, i))

    @classmethod
    def collected(cls, own, other, block):
        made = cls([(own, 0, 0), (other, 0, 1)], block)
        here = lax.axis_index(PLANE)
        made.slots = chip_slots() * block
        made.jobs = [
            (i, (3 * chip + m) * block, m, 0, block, 4 * i + chip)
            for i in range(2)
            for chip in range(4)
            for m in range(3)
        ]
        return made

    def scratch(self):
        return [
            pltpu.VMEM((3, self.width, self.units), BF16),
            pltpu.SemaphoreType.DMA((len(self.jobs),)),
        ]

    def copies(self, slots, refs, held, sems, matrix):
        made = []
        for n, (i, source, m, to, rows, slot) in enumerate(self.jobs):
            if m == matrix:
                base = 0 if slot is None else pl.multiple_of(slots[slot], 16)
                made.append(
                    pltpu.make_async_copy(
                        refs[i].at[pl.ds(source, rows)],
                        held.at[m, pl.ds(base + to, rows)],
                        sems.at[n],
                    )
                )
        return made


def ffn_forward_kernel(blocks, normed, part):
    rows, width = normed.shape
    units = blocks.units
    count = len(blocks.pieces)
    first = part is None

    def kernel(slots, n_ref, *refs):
        if not first:
            part_ref, refs = refs[0], refs[1:]
        pieces, (act, slope, hidden, out, held, sems) = refs[:count], refs[count:]
        start = pl.program_id(0) == 0

        def wait(m):
            @pl.when(start)
            def _():
                for copy in blocks.copies(slots, pieces, held, sems, m):
                    copy.wait()

        @pl.when(start)
        def _():
            for m in range(3):
                for copy in blocks.copies(slots, pieces, held, sems, m):
                    copy.start()

        left = n_ref[...]
        wait(0)
        gate = dot(left, held[0])
        wait(1)
        up = dot(left, held[1])
        square_gate = gate * gate
        turn = jnp.tanh(GELU_A * (gate + GELU_B * gate * square_gate))
        spread = 0.5 * (1.0 + turn)
        gelu = gate * spread
        bend = spread + 0.5 * gate * (1.0 - turn * turn) * (
            GELU_A * (1.0 + 3.0 * GELU_B * square_gate)
        )
        act[...] = gelu.astype(BF16)
        slope[...] = (up * bend).astype(BF16)
        low = (gelu * up).astype(BF16)
        hidden[...] = low
        wait(2)
        made = dot(low, held[2], (1, 1))
        out[...] = made if first else part_ref[...] + made

    by_rows = pl.BlockSpec((SEG, width), lambda i, s: (i, 0))
    by_units = pl.BlockSpec((SEG, units), lambda i, s: (i, 0))
    return prefetch_call(
        kernel,
        blocks.slots,
        (rows // SEG,),
        (normed,) + (() if first else (part,)) + blocks.pieces,
        [by_rows] + ([] if first else [by_rows]) + [whole(pl.ANY)] * count,
        [like((rows, units), BF16)] * 3 + [like((rows, width))],
        [by_units] * 3 + [by_rows],
        blocks.scratch(),
        mib=58,
        us=16,
    )


def ffn_backward_kernel(blocks, d_ffn, act, slope, back):
    rows, width = d_ffn.shape
    units = blocks.units
    count = len(blocks.pieces)
    first = back is None

    def kernel(slots, d_ref, act_ref, slope_ref, *refs):
        if not first:
            back_ref, refs = refs[0], refs[1:]
        pieces, (d_gate, d_up, out, held, sems) = refs[:count], refs[count:]
        start = pl.program_id(0) == 0

        def wait(m):
            @pl.when(start)
            def _():
                for copy in blocks.copies(slots, pieces, held, sems, m):
                    copy.wait()

        @pl.when(start)
        def _():
            for m in (2, 0, 1):
                for copy in blocks.copies(slots, pieces, held, sems, m):
                    copy.start()

        wait(2)
        d_hidden = dot(d_ref[...], held[2])
        to_gate = (d_hidden * slope_ref[...].astype(F32)).astype(BF16)
        to_up = (d_hidden * act_ref[...].astype(F32)).astype(BF16)
        d_gate[...] = to_gate
        d_up[...] = to_up
        wait(0)
        wait(1)
        made = dot(to_gate, held[0], (1, 1)) + dot(to_up, held[1], (1, 1))
        out[...] = made if first else back_ref[...] + made

    by_rows = pl.BlockSpec((SEG, width), lambda i, s: (i, 0))
    by_units = pl.BlockSpec((SEG, units), lambda i, s: (i, 0))
    return prefetch_call(
        kernel,
        blocks.slots,
        (rows // SEG,),
        (d_ffn, act, slope) + (() if first else (back,)) + blocks.pieces,
        [by_rows, by_units, by_units] + ([] if first else [by_rows]) + [whole(pl.ANY)] * count,
        [like((rows, units), BF16)] * 2 + [like((rows, width))],
        [by_units] * 2 + [by_rows],
        blocks.scratch(),
        mib=58,
        us=16,
    )


def ffn_end_kernel(plane, ffn_own, ffn_other, mid, cotangent, gain):
    rows, width = mid.shape

    def kernel(p, own_ref, other_ref, mid_ref, up_ref, gain_ref, d_out, d_turned, out, share):
        i = pl.program_id(0)
        g = gain_ref[...]

        def run(ref, own):
            ffn = ref[...].astype(F32)
            r = row_scale(ffn)
            incoming = up_ref[...].astype(F32)
            out[...] = (mid_ref[...] + ffn * r * g).astype(BF16)
            if own:
                share[...] = jnp.sum(incoming * ffn * r, axis=0, keepdims=True)
            scaled = g * incoming
            inner = jnp.mean(ffn * scaled, axis=-1, keepdims=True)
            made = (r * scaled - ffn * (r * r * r) * inner).astype(BF16)
            d_out[...] = made
            d_turned[...] = made.T

        pl.when(i == 0)(lambda: run(own_ref, True))
        pl.when(i == 1)(lambda: run(other_ref, False))

    once = pl.BlockSpec((SEG, width), lambda i, p: (0, 0))
    by_rows = pl.BlockSpec((SEG, width), lambda i, p: (i, 0))
    return prefetch_call(
        kernel,
        plane.reshape(1),
        (2,),
        (ffn_own, ffn_other, mid, cotangent, gain),
        [once, once, by_rows, pl.BlockSpec((SEG, width), lambda i, p: (p[0] ^ i, 0)), full(gain)],
        [like((rows, width), BF16), like((width, rows), BF16), like((rows, width), BF16), like((1, width))],
        [
            by_rows,
            pl.BlockSpec((width, SEG), lambda i, p: (0, i)),
            by_rows,
            pl.BlockSpec((1, width), lambda i, p: (0, 0)),
        ],
        us=3.4,
    )


def spread_kernel(plane, blocks, order, dtype):
    width = blocks[0].shape[1]
    count = len(blocks)
    spots = [(n, r) for n, x in enumerate(blocks) for r in range(x.shape[0] // SEG)]

    def kernel(p, *refs):
        ins, out = refs[:count], refs[count]
        for i, (n, r) in enumerate(spots):

            @pl.when(pl.program_id(0) == p[0] ^ order[i])
            def _(n=n, r=r):
                out[...] = ins[n][r * SEG : (r + 1) * SEG].astype(dtype)

    return prefetch_call(
        kernel,
        plane.reshape(1),
        (4,),
        tuple(blocks),
        [full(x) for x in blocks],
        like((4 * SEG, width), dtype),
        pl.BlockSpec((SEG, width), lambda i, p: (i, 0)),
        us=3,
    )


def attention_back_kernel(
    flags, back, got, mid, cotangent, gain_ffn, attn, gain_post, wo_t, query, query_raw, gain_query,
    slots, cos_table, sin_table, head,
):
    width, total = wo_t.shape
    heads = total // head
    half = head // 2
    scale = head**-0.5

    def kernel(
        f, back_ref, got_ref, mid_ref, up_ref, gain_ffn_ref, attn_ref, gain_post_ref, w_ref, q_ref,
        raw_ref, gain_query_ref, slots_ref, c_ref, s_ref,
        d_mid, d_attn, d_attn_turned, shares, d_query, query_share, d_self, d_a, d_b, sums,
    ):
        h = pl.program_id(0)

        @pl.when(h == 0)
        def _():
            incoming = back_ref[...] + got_ref[...].astype(F32)
            add, share = norm_back(mid_ref[...], gain_ffn_ref[...], incoming)
            made = up_ref[...].astype(F32) + add
            d_mid[...] = made
            d_a_low, share_post = norm_back(attn_ref[...], gain_post_ref[...], made)
            low = d_a_low.astype(BF16)
            d_attn[...] = low
            d_attn_turned[...] = low.T
            shares[0:1, :] = jnp.sum(share, axis=0, keepdims=True)
            shares[1:2, :] = jnp.sum(share_post, axis=0, keepdims=True)
            sums[...] = jnp.zeros_like(sums)
            query_share[...] = jnp.zeros_like(query_share)

        keys, values = slots_ref[:, :head], slots_ref[:, head:]
        q = q_ref[...]
        d_heads = dot(d_attn[...], w_ref[...]).astype(BF16)
        probs = softmax_of(q, keys, scale, f[4], f[5])
        d_probs = dot(d_heads, values, (1, 1))
        d_scores = probs * (d_probs - jnp.sum(d_probs * probs, axis=-1, keepdims=True))
        d_scores = d_scores.astype(BF16)
        sums[:, :head] += dot(d_scores, q, (0, 0))
        sums[:, head:] += dot(probs.astype(BF16), d_heads, (0, 0))
        turned = rotate(dot(d_scores, keys) * scale, c_ref[...], -s_ref[...])
        made, share = norm_back(raw_ref[...], gain_query_ref[...], turned)
        d_query[...] = made.astype(BF16)
        query_share[...] += jnp.sum(share, axis=0, keepdims=True)

        @pl.when(h == heads - 1)
        def _():
            sums[:, :head] = sums[:, :head] * scale
            d_self[...] = sums[:SEG]
            d_a[...] = sums[SEG : 2 * SEG].astype(BF16)
            d_b[...] = sums[2 * SEG :].astype(BF16)

    def once(shape):
        return pl.BlockSpec(shape, lambda h, f: (0,) * len(shape))

    by_head = pl.BlockSpec((SEG, head), lambda h, f: (0, h))
    table = pl.BlockSpec((SEG, half), lambda h, f: (f[1], 0))
    rows = once((SEG, width))
    return prefetch_call(
        kernel,
        flags,
        (heads,),
        (back, got, mid, cotangent, gain_ffn, attn, gain_post, wo_t, query, query_raw, gain_query,
         slots, cos_table, sin_table),
        [
            rows,
            rows,
            rows,
            pl.BlockSpec((SEG, width), lambda h, f: (f[1], 0)),
            full(gain_ffn),
            rows,
            full(gain_post),
            pl.BlockSpec((width, head), lambda h, f: (0, h)),
            by_head,
            by_head,
            full(gain_query),
            full(slots),
            table,
            table,
        ],
        [
            like((SEG, width)),
            like((SEG, width), BF16),
            like((width, SEG), BF16),
            like((2, width)),
            like((SEG, total), BF16),
            like((1, head)),
            like((SEG, 2 * head)),
            like((SEG, 2 * head), BF16),
            like((SEG, 2 * head), BF16),
        ],
        [
            rows,
            rows,
            once((width, SEG)),
            once((2, width)),
            by_head,
            once((1, head)),
            once((SEG, 2 * head)),
            once((SEG, 2 * head)),
            once((SEG, 2 * head)),
        ],
        [pltpu.VMEM((3 * SEG, 2 * head), F32)],
        us=12,
    )


def tokens_back_kernel(
    plane, terms, key_raw, gain_key, cos_table, sin_table, wkv, d_normed, d_mid, tokens, gain_in
):
    width = d_mid.shape[1]
    head = key_raw.shape[1]
    half = head // 2
    count = len(terms)

    def kernel(p, *refs):
        terms_in, refs = refs[:count], refs[count:]
        (raw_ref, gain_ref, c_ref, s_ref, w_ref, dn_ref, mid_ref, t_ref, gain_in_ref) = refs[:9]
        d_kv, rows_out, share_key, share_in = refs[9:]
        total = terms_in[0][...].astype(F32)
        for term in terms_in[1:]:
            total = total + term[...].astype(F32)
        turned = rotate(total[:, :head], c_ref[...], -s_ref[...])
        made, share = norm_back(raw_ref[...], gain_ref[...], turned)
        share_key[...] = jnp.sum(share, axis=0, keepdims=True)
        low = jnp.concatenate([made, total[:, head:]], axis=1).astype(BF16)
        d_kv[...] = low
        incoming = dn_ref[...] + dot(low, w_ref[...], (1, 1))
        add, share = norm_back(t_ref[...].astype(F32), gain_in_ref[...], incoming)
        share_in[...] = jnp.sum(share, axis=0, keepdims=True)
        rows_out[...] = (mid_ref[...] + add).astype(BF16)

    table = pl.BlockSpec((SEG, half), lambda i, p: (p[0], 0))
    ins = (*terms, key_raw, gain_key, cos_table, sin_table, wkv, d_normed, d_mid, tokens, gain_in)
    specs = [full(x) for x in ins]
    specs[count + 2] = specs[count + 3] = table
    specs[count + 7] = pl.BlockSpec((SEG, width), lambda i, p: (p[0], 0))
    outs = [like((SEG, 2 * head), BF16), like((SEG, width), BF16), like((1, head)), like((1, width))]
    return prefetch_call(
        kernel, plane.reshape(1), (1,), ins, specs, outs, [full(o) for o in outs], us=3
    )


def window_kernel(flags, d_self, d_a, d_b, back_1, back_2, back_3):
    shape = (2,) + d_self.shape

    def kernel(f, own_ref, a_ref, b_ref, b1, b2, b3, sent, kept):
        role, plane = f[0], f[1]
        near = role == 0
        ats = [
            plane,
            jnp.where(near & (f[4] > 0), f[2], -1),
            jnp.where(near & (f[5] > 0), f[3], -1),
            jnp.where(role <= 1, f[6], -1),
            jnp.where(role <= 1, f[7], -1),
            jnp.where(near, f[8], -1),
        ]
        refs = (own_ref, a_ref, b_ref, b1, b2, b3)
        for out, k, other in ((sent, 0, 1), (sent, 1, 3), (kept, 0, 0), (kept, 1, 2)):
            number = plane ^ other
            total = jnp.zeros(out.shape[1:], F32)
            for at, ref in zip(ats, refs):
                total = total + jnp.where(at == number, ref[...].astype(F32), 0.0)
            out[k] = total.astype(BF16)

    return pl.pallas_call(
        kernel,
        out_shape=[like(shape, BF16)] * 2,
        in_specs=[whole(pltpu.SMEM)] + [whole(pltpu.VMEM)] * 6,
        out_specs=[whole(pltpu.VMEM)] * 2,
        compiler_params=params(32),
        cost_estimate=cost(2.4),
    )(flags, d_self, d_a, d_b, back_1, back_2, back_3)


def z_first(sent, kept, kept_far):
    got = across(sent, 1).astype(F32)
    return tie((kept.astype(F32) + got[0]).astype(BF16), (kept_far.astype(F32) + got[1]).astype(BF16))


def z_halve(x):
    here = lax.axis_index("gx")

    def at(n):
        return lax.dynamic_index_in_dim(x, n, 0, keepdims=False)

    return z_first(jnp.stack([at(here ^ 1), at(here ^ 3)]), at(here), at(here ^ 2))


def body(
    tokens,
    parents,
    w_query,
    w_key,
    w_value,
    w_out,
    w_gate,
    w_up,
    w_down,
    g_attn_in,
    g_attn_out,
    g_ffn_in,
    g_ffn_out,
    g_query,
    g_key,
    cotangent,
):
    column = lax.axis_index(PLANE)
    columns = lax.axis_size(PLANE)
    plane = lax.axis_index("gx")
    planes = lax.axis_size("gx")
    width = tokens.shape[1]
    head_width = w_key.shape[1]
    heads = planes * w_query.shape[1] // head_width
    block, small = w_query.shape[0], w_key.shape[0]
    gains_len = 4 * block + 2 * g_query.shape[0]
    pack_width = 2 * head_width
    gain_rows = -(-gains_len // pack_width)
    used = small + gain_rows
    gain_spot = -(-small // 8) * 8
    pack_rows = -(-(block + gain_spot + gain_rows) // 16) * 16

    core = lax.axis_index("gc")
    down_t = w_down.T
    ffn_mine = jnp.concatenate([w_gate, w_up, down_t], axis=0)
    gains = jnp.concatenate([g_attn_in, g_attn_out, g_ffn_in, g_ffn_out, g_query, g_key])
    gains = jnp.pad(gains, (0, gain_rows * pack_width - gains_len)).reshape(gain_rows, pack_width)
    pack = jnp.concatenate(
        [
            jnp.concatenate([w_query, w_out.T], axis=1),
            jnp.concatenate([w_key, w_value], axis=1),
            jnp.zeros((gain_spot - small, pack_width), BF16),
            gains,
            jnp.zeros((pack_rows - block - gain_spot - gain_rows, pack_width), BF16),
        ],
        axis=0,
    )
    flags = flags_kernel(parents, jnp.stack([column, plane]).astype(jnp.int32))
    depth = flags[9:13, None] * SEG + jnp.arange(SEG, dtype=jnp.int32)[None, :]
    half_width = head_width // 2
    rates = 10000.0 ** (-jnp.arange(half_width, dtype=F32) / half_width)
    turned = depth.reshape(-1).astype(F32)[:, None] * rates[None, :]
    cos_table, sin_table = jnp.cos(turned), jnp.sin(turned)
    if square():
        ffn_x, ffn_y = send_near(ffn_mine)
        pack = lax.all_gather(pack, "gx", axis=0)
        pack, other_gate = tie(pack, w_gate)
        their_gate = across(other_gate, 2)
        pack_x, pack_y = send_near(pack)
        ffn_x, ffn_y, pack, pack_x, pack_y, cos_table, sin_table = tie(
            ffn_x, ffn_y, pack, pack_x, pack_y, cos_table, sin_table
        )
        pack_far = send_far(pack_x, pack_y)
        ffn_far = send_far(ffn_x, ffn_y)
        *pack_far, their_gate, other_up, other_down = tie(*pack_far, their_gate, w_up, down_t)
        their_up, their_down = across(other_up, 2), across(other_down, 2)
        pack_all = collect((pack, pack_x, pack_y, *pack_far), planes)
        pack_other = swap(pack_all, "gc")
        wq, wo_t, wkv, gains = unpack(
            [pack_all, pack_other], block, head_width, gain_spot, gain_rows
        )
    else:
        pack = lax.all_gather(pack, "gx", axis=0, tiled=True)
        pack = lax.all_gather(pack, PLANE, axis=0).reshape(columns, planes, pack_rows, pack_width)

        def from_blocks(blocks):
            return blocks.transpose(0, 2, 1, 3).reshape(columns * block, -1)

        wq = from_blocks(pack[:, :, :block, :head_width])
        wo_t = from_blocks(pack[:, :, :block, head_width:])
        wkv = pack[:, :, block : block + small].transpose(1, 0, 2, 3).reshape(width, pack_width)
        gains = pack[:, 0, block + gain_spot : block + gain_spot + gain_rows]

        def ffn_weights(mine):
            stacked = lax.all_gather(mine, PLANE, axis=0).reshape(columns, 3, block, -1)
            return Blocks([stacked[:, i].reshape(width, -1) for i in range(3)], None)

        quarter_mine = ffn_weights(ffn_mine)
        quarter_theirs = ffn_weights(across(ffn_mine, 2))

    gains = gains.reshape(columns, -1)[:, :gains_len].astype(F32)
    gain_in, gain_post, gain_ffn, gain_last = [
        gains[:, i * block : (i + 1) * block].reshape(1, -1) for i in range(4)
    ]
    gain_query, gain_key = [
        gains[:, 4 * block + i * g_query.shape[0] :][:, : g_query.shape[0]].reshape(1, -1)
        for i in range(2)
    ]

    role = column % 4
    trees = range(columns // 4)
    route_1 = [(4 * t + i, 4 * t + i + 1) for t in trees for i in (0, 1)]
    route_2 = [(4 * t + i, 4 * t + i + 2) for t in trees for i in (0, 1)]
    route_3 = [(4 * t + i, 4 * t + i + 1) for t in trees for i in (0, 2)]

    def send(x, route):
        return lax.ppermute(x, PLANE, route)

    def send_back(x, route):
        return lax.ppermute(x, PLANE, [(b, a) for a, b in route])

    pairs, normed_own, key_raw, send_1, send_2, send_3 = key_value_kernel(
        flags, tokens, gain_in, wkv, gain_key, cos_table, sin_table
    )
    if square():
        send_1, send_2, *ffn_far = tie(send_1, send_2, *ffn_far)
    got_1 = send(send_1, route_1)
    got_2 = send(send_2, route_2)
    query, query_raw = query_kernel(
        plane, normed_own, wq, gain_query, cos_table, sin_table, head_width
    )
    if square():
        query, ffn_x, ffn_y, *ffn_far = tie(query, ffn_x, ffn_y, *ffn_far)
        mine_all = collect((ffn_mine, ffn_x, ffn_y, *ffn_far), 3 * block)
        got_1, got_2, mine_all, their_up, their_down = tie(
            got_1, got_2, mine_all, their_up, their_down
        )
        mine_other = swap(mine_all, "gc")
        theirs = jnp.concatenate([their_gate, their_up, their_down], axis=0)
        their_x, their_y = send_near(theirs)
    got_3 = send(jnp.where(role == 2, got_2, send_3), route_3)
    heads_low, slots = attention_kernel(flags, query, pairs, got_1, got_2, got_3)

    if square():
        heads_low, mine_other = tie(heads_low, mine_other)
        heads_got = across(heads_low, 1)
        quarter_mine = Blocks.collected(mine_all, mine_other, block)
    else:
        heads_got = across(heads_low, 1)
    attn, mid, normed_ffn = middle_kernel(
        plane, heads_low, heads_got, wo_t, tokens, gain_post, gain_ffn
    )
    if square():
        normed_ffn, their_x, their_y = tie(normed_ffn, their_x, their_y)
        their_far = send_far(their_x, their_y)
        quarter_theirs = Blocks(
            both_cores(
                [
                    (theirs, 0, 0),
                    (their_x, 0, 2),
                    (their_y, 0, 4),
                    (their_far[0], 0, 6),
                    (their_far[1], their_far[0].shape[0], 6),
                ]
            ),
            block,
        )
    act_m, slope_m, hidden_m, ffn_part = ffn_forward_kernel(quarter_mine, normed_ffn, None)
    act_t, slope_t, hidden_t, ffn_part = ffn_forward_kernel(quarter_theirs, normed_ffn, ffn_part)
    ffn_got = across(ffn_part[SEG:].astype(BF16), 1)
    ffn_own = (ffn_part[:SEG] + ffn_got.astype(F32)).astype(BF16)
    ffn_other = across(ffn_own, 1)
    d_ffn_low, d_ffn_t, output, d_gain_last = ffn_end_kernel(
        plane, ffn_own, ffn_other, mid, cotangent, gain_last
    )

    output_far = [across(output[:SEG], 2)]
    d_gate_t, d_up_t, back = ffn_backward_kernel(quarter_theirs, d_ffn_low, act_t, slope_t, None)
    if square():
        lefts = (normed_ffn.T, d_ffn_t)
        send_theirs = ffn_weight_grads(1 - core, *lefts, d_gate_t, d_up_t, hidden_t, block)
        back, send_theirs, output_far[0] = tie(back, send_theirs, output_far[0])
        recv_theirs = swap(send_theirs, "gc")
    d_gate_m, d_up_m, back = ffn_backward_kernel(quarter_mine, d_ffn_low, act_m, slope_m, back)
    back, d_gate_t = tie(back, d_gate_t)
    back_got = across(back[SEG:].astype(BF16), 1)
    if square():
        keep_theirs = ffn_weight_grads(core, *lefts, d_gate_t, d_up_t, hidden_t, block)
        back_got, recv_theirs, keep_theirs, output = tie(
            back_got, recv_theirs, keep_theirs, output
        )
        theirs_far = Scatter(keep_theirs, recv_theirs).send_far()
    else:
        grads = []
        for d_gate, d_up, hidden in ((d_gate_m, d_up_m, hidden_m), (d_gate_t, d_up_t, hidden_t)):
            blocks = [
                dot(normed_ffn, d_gate, (0, 0)),
                dot(normed_ffn, d_up, (0, 0)),
                dot(d_ffn_low, hidden, (0, 0)),
            ]
            blocks = [m.astype(BF16).reshape(columns, block, -1) for m in blocks]
            grads.append(plane_scatter(jnp.concatenate(blocks, axis=1)))
        ffn_grad = grads[0] + across(grads[1].astype(BF16), 2).astype(F32)

    output_far.append(across(output[SEG : SEG + SEG // 2], 2))

    (
        d_mid, d_attn_low, d_attn_t, d_gains_mid, d_query_low, d_gain_query, d_self, d_a, d_b,
    ) = attention_back_kernel(
        flags, back, back_got, mid, cotangent, gain_ffn, attn, gain_post, wo_t, query, query_raw,
        gain_query, slots, cos_table, sin_table, head_width,
    )
    if square():
        d_a, d_b, output_far[1], output = tie(d_a, d_b, output_far[1], output)
    output_far.append(across(output[SEG + SEG // 2 :], 2))
    back_1 = send_back(d_a, route_1)
    back_3 = send_back(d_b, route_3)
    if square():
        d_a, d_b, back_1, back_3, *theirs_far = tie(d_a, d_b, back_1, back_3, *theirs_far)
    d_b_far = jnp.where(role == 2, d_b.astype(F32) + back_3.astype(F32), 0.0).astype(BF16)
    to_back_2 = jnp.where(role == 3, d_a, d_b_far)
    if square():
        to_back_2, keep_theirs, recv_theirs, d_gate_m, *theirs_far = tie(
            to_back_2, keep_theirs, recv_theirs, d_gate_m, *theirs_far
        )
    back_2 = send_back(to_back_2, route_2)
    if square():
        to_near = Scatter(keep_theirs, recv_theirs).near_blocks(*theirs_far)
        made = (*lefts, d_gate_m, d_up_m, hidden_m)
        send_mine = ffn_weight_grads(1 - core, *made, block)
        back_2, output_far[2], send_mine, *to_near = tie(
            back_2, output_far[2], send_mine, *to_near
        )
        recv_mine = swap(send_mine, "gc")
        half = to_near[0].shape[0] // 32 * 16

        near_first = swap(to_near[0][:half], "ga"), swap(to_near[1][:half], "gb")
    sent, kept = window_kernel(flags, d_self, d_a, d_b, back_1, back_2, back_3)
    kept, passed = z_first(sent, kept[0], kept[1])
    if square():
        keep_mine = ffn_weight_grads(core, *made, block)
        passed, keep_mine, recv_mine, *near = tie(passed, keep_mine, recv_mine, *near_first, *to_near)
        near_first = near[:2]
        near_second = swap(near[2][half:], "ga"), swap(near[3][half:], "gb")
    d_normed_query = dot(d_query_low, wq, (1, 1))
    own_terms = [kept, across(passed, 2)]
    if square():
        own_terms[1], keep_theirs, recv_theirs, *near = tie(
            own_terms[1], keep_theirs, recv_theirs, *near_first, *near_second
        )
        theirs_near = [jnp.concatenate([near[i], near[i + 2]], axis=0) for i in range(2)]
        theirs_sum = Scatter(keep_theirs, recv_theirs).total(*theirs_near).astype(BF16)
        gate_sum = across(theirs_sum[:block], 2)
        mine_far = Scatter(keep_mine, recv_mine).send_far()
        theirs_sum = Scatter(keep_theirs, recv_theirs).total(*theirs_near).astype(BF16)
        gate_sum = across(theirs_sum[:block], 2)
    d_kv_low, token_rows, d_gain_key, d_gain_in = tokens_back_kernel(
        plane, own_terms, key_raw, gain_key, cos_table, sin_table, wkv, d_normed_query, d_mid,
        tokens, gain_in,
    )
    tokens_far = across(token_rows, 2)

    grad_kv = dot(normed_own, d_kv_low, (0, 0)).astype(BF16)
    grad_kv = grad_kv.reshape(planes, columns, small, -1).transpose(1, 0, 2, 3)
    gain_sums = [
        d_gain_in,
        d_gains_mid[1:],
        d_gains_mid[:1],
        d_gain_last,
        d_gain_query,
        d_gain_key,
    ]
    gain_sums = jnp.concatenate([g.reshape(columns, -1) for g in gain_sums], axis=1).astype(BF16)
    gain_sums = jnp.pad(gain_sums, ((0, 0), (0, gain_rows * pack_width - gains_len)))
    gain_sums = jnp.broadcast_to(
        gain_sums.reshape(columns, 1, gain_rows, pack_width),
        (columns, planes, gain_rows, pack_width),
    )
    rest_rows = pack_rows - block
    rest = jnp.concatenate(
        [grad_kv, gain_sums, jnp.zeros((columns, planes, pack_rows - block - used, pack_width), BF16)],
        axis=2,
    ).reshape(columns, planes * rest_rows, pack_width)
    if square():
        attn_lefts = (normed_own.T, d_query_low, d_attn_t, heads_low, rest)
        attn_send = attention_weight_grads(1 - core, *attn_lefts, block, planes)
        attn_keep = attention_weight_grads(core, *attn_lefts, block, planes)
        attn_received = swap(attn_send, "gc")
        gate_sum, other_up, attn_keep, attn_received, keep_mine, recv_mine, *mine_far = tie(
            gate_sum, theirs_sum[block : 2 * block], attn_keep, attn_received, keep_mine, recv_mine,
            *mine_far,
        )
        attn_far = Scatter(attn_keep, attn_received).send_far()
        tokens_far, other_down, attn_keep, attn_received, *attn_far = tie(
            tokens_far, theirs_sum[2 * block :], attn_keep, attn_received, *attn_far
        )
        attn_work = Scatter(attn_keep, attn_received)
        attn_near = attn_work.send_near(*attn_far)
        up_sum = across(other_up, 2)
        tokens_near = across(jnp.concatenate([token_rows, tokens_far], axis=0), 1)
        up_sum, keep_mine, recv_mine, *attn_near = tie(up_sum, keep_mine, recv_mine, *attn_near)
        mine = Scatter(keep_mine, recv_mine)
        mine_near = mine.send_near(*mine_far)
        down_sum = across(other_down, 2)
        grads = attn_work.total(*attn_near)
    else:

        def to_blocks(grad):
            return grad.astype(BF16).reshape(columns, block, planes, -1).transpose(0, 2, 1, 3)

        grads = jnp.concatenate(
            [
                to_blocks(dot(normed_own, d_query_low, (0, 0))),
                to_blocks(dot(d_attn_low, heads_low, (0, 0))),
            ],
            axis=3,
        ).reshape(columns, planes * block, pack_width)
        grads = jnp.concatenate(
            [grads.reshape(columns, planes, block, -1), rest.reshape(columns, planes, rest_rows, -1)],
            axis=2,
        ).reshape(columns, planes * pack_rows, pack_width)
        grads = plane_scatter(grads)
    grads = grads.reshape(planes, pack_rows, pack_width)
    rest = jnp.broadcast_to(
        grads[:1, block + small :], (planes, pack_rows - block - small, pack_width)
    )
    grads = jnp.concatenate([grads[:, : block + small], rest], axis=1).astype(BF16)
    kept, passed = z_halve(grads)
    if square():
        passed, down_sum = tie(passed, down_sum)
    else:
        tokens_near = across(jnp.concatenate([token_rows, tokens_far], axis=0), 1)
    grads = kept.astype(F32) + across(passed, 2).astype(F32)
    if square():
        ffn_grad = mine.total(*mine_near) + jnp.concatenate(
            [gate_sum, up_sum, down_sum], axis=0
        ).astype(F32)
    grad_tokens = spread_kernel(plane, (token_rows, tokens_far, tokens_near), (0, 2, 1, 3), F32)
    output_far[1:] = [jnp.concatenate(output_far[1:], axis=0)]
    output = spread_kernel(plane, (output, *output_far), (0, 1, 2, 3), BF16)
    gain_grads = grads[block + small : block + used].reshape(-1)
    return (
        output,
        grad_tokens,
        gain_grads[:block],
        gain_grads[block : 2 * block],
        gain_grads[2 * block : 3 * block],
        gain_grads[3 * block : 4 * block],
        gain_grads[4 * block : 4 * block + g_query.shape[0]],
        gain_grads[4 * block + g_query.shape[0] : gains_len],
        grads[:block, :head_width],
        grads[block : block + small, :head_width],
        grads[block : block + small, head_width:],
        grads[:block, head_width:].T,
        ffn_grad[:block],
        ffn_grad[block : 2 * block],
        ffn_grad[2 * block :].T,
    )


def solution(mesh):
    side = math.isqrt(mesh.shape["gy"] // 2)
    split = Mesh(mesh.devices.reshape(mesh.shape["gx"], side, side, 2), ("gx",) + PLANE)
    whole = ("gx",) + PLANE
    return jax.shard_map(
        body,
        mesh=split,
        in_specs=(
            P(PLANE, None),
            P(),
            P(PLANE, "gx"),
            P(whole, None),
            P(whole, None),
            P("gx", PLANE),
            P(PLANE, "gx"),
            P(PLANE, "gx"),
            P("gx", PLANE),
            P(PLANE),
            P(PLANE),
            P(PLANE),
            P(PLANE),
            P(PLANE),
            P(PLANE),
            P(PLANE, None),
        ),
        out_specs=(
            P(PLANE, None),
            P(PLANE, None),
            P(PLANE),
            P(PLANE),
            P(PLANE),
            P(PLANE),
            P(PLANE),
            P(PLANE),
            P(PLANE, "gx"),
            P(whole, None),
            P(whole, None),
            P("gx", PLANE),
            P(PLANE, "gx"),
            P(PLANE, "gx"),
            P("gx", PLANE),
        ),
        check_vma=False,
    )
```

```python
import math

import jax
import jax.numpy as jnp
from jax import lax
from jax.experimental import pallas as pl
from jax.experimental.pallas import tpu as pltpu
from jax.sharding import Mesh
from jax.sharding import PartitionSpec as P

SEG = 256
EPSILON = 1e-06
MASKED = -1e30
PLANE = ("gb", "ga", "gc")
SWAP = [(0, 1), (1, 0)]
F32 = jnp.float32
BF16 = jnp.bfloat16


def rms_norm(values, gain):
    return values * lax.rsqrt(jnp.mean(values * values, axis=-1, keepdims=True) + EPSILON) * gain


def norm_back(values, gain, incoming):
    r = lax.rsqrt(jnp.mean(values * values, axis=-1, keepdims=True) + EPSILON)
    scaled = gain * incoming
    inner = jnp.mean(values * scaled, axis=-1, keepdims=True)
    return r * scaled - values * (r * r * r) * inner, incoming * values * r


def rotate(values, cos_table, sin_table):
    half_width = values.shape[-1] // 2
    a, b = values[..., :half_width], values[..., half_width:]
    return jnp.concatenate([a * cos_table - b * sin_table, b * cos_table + a * sin_table], axis=-1)


def dot(a, b, dims=(1, 0)):
    return lax.dot_general(
        a, b, (((dims[0],), (dims[1],)), ((), ())), preferred_element_type=F32
    )


def swap(x, axis):
    return lax.ppermute(x, axis, SWAP)


def across(x, distance):
    return lax.ppermute(x, "gx", [(i, i ^ distance) for i in range(4)])


def tie(*values):
    return lax.optimization_barrier(values)


def cost(microseconds):
    flops = int(microseconds * 1.0 * 1.15e9)
    return pl.CostEstimate(flops=flops, bytes_accessed=0, transcendentals=0)


def whole(array_or_space):
    return pl.BlockSpec(memory_space=array_or_space)


def params(mib):
    return pltpu.CompilerParams(vmem_limit_bytes=mib * 2**20)


def square():
    return lax.axis_size("ga") == 2


def halves(x):
    half = x.shape[0] // 32 * 16 or x.shape[0] // 2
    return x[:half], x[half:]


def send_near(x):
    return swap(x, "ga"), swap(x, "gb")


def send_far(from_x, from_y):
    return swap(halves(from_y)[0], "ga"), swap(halves(from_x)[1], "gb")


def collect(pieces, rows):
    count = len(pieces)
    starts = [0, rows, 2 * rows, 3 * rows, 3 * rows + pieces[3].shape[0]]
    shape = (4 * rows,) + pieces[0].shape[1:]

    def kernel(*refs):
        ins, (out, held, sems) = refs[:count], refs[count:]
        spots = [pl.ds(start, piece.shape[0]) for start, piece in zip(starts, pieces)]
        loads = [
            pltpu.make_async_copy(ref, held.at[spot], sems.at[0, i])
            for i, (ref, spot) in enumerate(zip(ins, spots))
        ]
        stores = [
            pltpu.make_async_copy(held.at[spot], out.at[spot], sems.at[1, i])
            for i, spot in enumerate(spots)
        ]
        for load in loads:
            load.start()
        for load, store in zip(loads, stores):
            load.wait()
            store.start()
        for store in stores:
            store.wait()

    return pl.pallas_call(
        kernel,
        out_shape=jax.ShapeDtypeStruct(shape, pieces[0].dtype),
        in_specs=[whole(pl.ANY)] * count,
        out_specs=whole(pl.ANY),
        scratch_shapes=[pltpu.VMEM(shape, pieces[0].dtype), pltpu.SemaphoreType.DMA((2, count))],
        compiler_params=params(24),
        cost_estimate=cost(4),
    )(*pieces)


def chip_slots():
    here = lax.axis_index(PLANE)
    return jnp.array([0, 2, 4, 6, 1, 3, 5, 7], jnp.int32) ^ here


def unpack(pieces, block, head_width, gain_spot, gain_rows):
    four, rows, width = pieces[0].shape
    planes = four // 4
    rest = rows - block
    small = block // planes
    count = len(pieces)
    jobs = [(i, 4 * chip + h, 4 * i + chip, h) for i in range(2) for chip in range(4) for h in range(planes)]

    def kernel(slot_ref, *refs):
        ins, (wq, wo, wkv, gains, other, sems) = refs[:count], refs[count:]
        copies = []
        for n, (i, j, at_slot, h) in enumerate(jobs):
            slot = slot_ref[at_slot]
            at = pl.ds(pl.multiple_of(slot * block, 16), block)
            to = pl.ds(h * head_width, head_width)
            parts = [
                (ins[i].at[j, pl.ds(0, block), pl.ds(0, head_width)], wq.at[at, to]),
                (ins[i].at[j, pl.ds(0, block), pl.ds(head_width, head_width)], wo.at[at, to]),
                (ins[i].at[j, pl.ds(block, rest), :], other.at[slot, h]),
            ]
            copies += [
                pltpu.make_async_copy(a, b, sems.at[n, m]) for m, (a, b) in enumerate(parts)
            ]
        for copy in copies:
            copy.start()
        for copy in copies:
            copy.wait()
        for c in range(8):
            gains[c] = other[c, 0, gain_spot : gain_spot + gain_rows, :]
        for h in range(planes):
            wkv[h * 8 * small : (h + 1) * 8 * small] = jnp.concatenate(
                [other[c, h, :small, :].astype(F32) for c in range(8)], axis=0
            ).astype(BF16)

    matrix = jax.ShapeDtypeStruct((8 * block, planes * head_width), BF16)
    return pl.pallas_call(
        kernel,
        out_shape=[
            matrix,
            matrix,
            jax.ShapeDtypeStruct((8 * block, width), BF16),
            jax.ShapeDtypeStruct((8, gain_rows, width), BF16),
        ],
        in_specs=[whole(pltpu.SMEM)] + [whole(pl.ANY)] * count,
        out_specs=[whole(pltpu.VMEM)] * 4,
        scratch_shapes=[
            pltpu.VMEM((8, planes, rest, width), BF16),
            pltpu.SemaphoreType.DMA((len(jobs), 3)),
        ],
        compiler_params=params(24),
        cost_estimate=cost(4.3),
    )(chip_slots(), *pieces)


def core_rows(ref, core, block):
    return jnp.concatenate(
        [ref[pl.ds(pl.multiple_of((2 * k + core) * block, 16), block), :] for k in range(4)],
        axis=0,
    )


def ffn_weight_grads(core, normed_t, d_ffn_t, d_gate, d_up, hidden, block):
    units = d_gate.shape[1]

    def kernel(core_ref, normed_ref, d_ffn_ref, gate_ref, up_ref, hidden_ref, out):
        m = pl.program_id(0)

        def run(left, right):
            rows = core_rows(left, core_ref[0], block)
            for n in range(0, units, 256):
                w = min(256, units - n)
                made = dot(rows, right[:, n : n + w]).astype(BF16)
                out[:, :, n : n + w] = made.reshape(4, block, w)

        for number, (left, right) in enumerate(
            ((normed_ref, gate_ref), (normed_ref, up_ref), (d_ffn_ref, hidden_ref))
        ):
            pl.when(m == number)(lambda left=left, right=right: run(left, right))

    def full(x):
        return pl.BlockSpec(x.shape, lambda m, c: (0, 0))

    ins = (normed_t, d_ffn_t, d_gate, d_up, hidden)
    return pl.pallas_call(
        kernel,
        grid_spec=pltpu.PrefetchScalarGridSpec(
            num_scalar_prefetch=1,
            grid=(3,),
            in_specs=[full(x) for x in ins],
            out_specs=pl.BlockSpec((4, block, units), lambda m, c: (0, m, 0)),
        ),
        out_shape=jax.ShapeDtypeStruct((4, 3 * block, units), BF16),
        compiler_params=params(48),
        cost_estimate=cost(6.7),
    )(core.reshape(1), *ins)


def attention_weight_grads(core, normed_t, d_query, d_attn_t, heads_low, other, block, planes):
    head_width = d_query.shape[1] // planes
    more = other.shape[1] // planes
    rows_all = block + more

    def kernel(core_ref, normed_ref, query_ref, d_attn_ref, heads_ref, other_ref, out):
        for half, (left, right) in enumerate(((normed_ref, query_ref), (d_attn_ref, heads_ref))):
            rows = core_rows(left, core_ref[0], block)
            for h in range(planes):
                made = dot(rows, right[:, h * head_width : (h + 1) * head_width]).astype(BF16)
                out[:, h * rows_all : h * rows_all + block, half * head_width : (half + 1) * head_width] = (
                    made.reshape(4, block, head_width)
                )
        for chip in range(4):
            for h in range(planes):
                out[chip, h * rows_all + block : (h + 1) * rows_all] = other_ref[
                    2 * chip + core_ref[0], h * more : (h + 1) * more
                ]

    return pl.pallas_call(
        kernel,
        out_shape=jax.ShapeDtypeStruct((4, planes * rows_all, 2 * head_width), BF16),
        in_specs=[whole(pltpu.SMEM)] + [whole(pltpu.VMEM)] * 5,
        out_specs=whole(pltpu.VMEM),
        compiler_params=params(32),
        cost_estimate=cost(2.5),
    )(core.reshape(1), normed_t, d_query, d_attn_t, heads_low, other)


class Scatter:
    def __init__(self, keep, received):
        y, x = lax.axis_index("gb"), lax.axis_index("ga")
        self.keep, self.received = keep, received
        self.here, self.x, self.y = 2 * y + x, 2 * y + 1 - x, 2 * (1 - y) + x
        self.far = 2 * (1 - y) + 1 - x
        self.half = keep.shape[1] // 32 * 16

    def part(self, chip, second=None):
        made = 0.0
        for values in (self.keep, self.received):
            block = lax.dynamic_index_in_dim(values, chip, 0, keepdims=False)
            if second is not None:
                block = block[self.half :] if second else block[: self.half]
            made = made + block.astype(F32)
        return made

    def far_blocks(self):
        return self.part(self.far, False).astype(BF16), self.part(self.far, True).astype(BF16)

    def first_blocks(self):
        return self.part(self.x, False).astype(BF16), self.part(self.y, True).astype(BF16)

    def second_blocks(self, got_first, got_second):
        to_x = self.part(self.x, True) + got_second.astype(F32)
        to_y = self.part(self.y, False) + got_first.astype(F32)
        return to_x.astype(BF16), to_y.astype(BF16)

    def near_blocks(self, got_first, got_second):
        first, second = self.first_blocks(), self.second_blocks(got_first, got_second)
        return jnp.concatenate([first[0], second[0]]), jnp.concatenate([second[1], first[1]])

    def near_total(self, got_x, got_y):
        return self.part(self.here) + got_x.astype(F32) + got_y.astype(F32)

    def total(self, first, second):
        upper = self.part(self.here, False) + first[0].astype(F32) + second[1].astype(F32)
        lower = self.part(self.here, True) + second[0].astype(F32) + first[1].astype(F32)
        return jnp.concatenate([upper, lower], axis=0)


def send_xy(blocks):
    return swap(blocks[0], "ga"), swap(blocks[1], "gb")


def plane_scatter(g):
    if not square():
        return lax.psum_scatter(g, PLANE, scatter_dimension=0).astype(F32)
    c = lax.axis_index("gc")
    g = g.reshape((4, 2) + g.shape[1:])
    keep = lax.dynamic_index_in_dim(g, c, 1, keepdims=False)
    received = swap(lax.dynamic_index_in_dim(g, 1 - c, 1, keepdims=False), "gc")
    work = Scatter(keep, received)
    second = work.second_blocks(*send_xy(work.far_blocks()))
    return work.total(send_xy(work.first_blocks()), send_xy(second))


GELU_A = 0.7978845608028654
GELU_B = 0.044715


def row_scale(values):
    return lax.rsqrt(jnp.mean(values * values, axis=-1, keepdims=True) + EPSILON)


def full(x):
    return pl.BlockSpec(x.shape, lambda *_: (0,) * len(x.shape))


def like(shape, dtype=F32):
    return jax.ShapeDtypeStruct(shape, dtype)


def prefetch_call(kernel, scalars, grid, ins, in_specs, outs, out_specs, scratch=(), mib=48, us=3):
    return pl.pallas_call(
        kernel,
        grid_spec=pltpu.PrefetchScalarGridSpec(
            num_scalar_prefetch=1,
            grid=grid,
            in_specs=in_specs,
            out_specs=out_specs,
            scratch_shapes=scratch,
        ),
        out_shape=outs,
        compiler_params=params(mib),
        cost_estimate=cost(us),
    )(scalars, *ins)


def flags_kernel(parents, spot):
    segments = parents.shape[0]

    def kernel(parents_ref, spot_ref, out):
        def parent_of(segment):
            found = parents_ref[jnp.maximum(segment, 0)]
            return jnp.where(segment >= 0, found, -1)

        column, plane = spot_ref[0], spot_ref[1]
        first = 4 * column
        own = first + plane

        def later(distance):
            return parent_of(jnp.minimum(own + 4 * distance, segments - 1))

        def local(segment):
            return jnp.clip(segment - first, 0, 3)

        role = lax.rem(column, 4)
        a, a1, a2 = parent_of(own), later(1), later(2)
        b, b1, b2 = parent_of(a), parent_of(a1), parent_of(a2)
        made = [
            role,
            plane,
            local(a),
            local(b),
            (a >= 0).astype(jnp.int32),
            (b >= 0).astype(jnp.int32),
            local(a1),
            local(jnp.where(role == 0, b2, a2)),
            local(b1),
        ]
        for i in range(4):
            segment, level = first + i, jnp.int32(0)
            for _ in range(5):
                segment = parent_of(segment)
                level = level + (segment >= 0).astype(jnp.int32)
            made.append(level)
        for i, value in enumerate(made):
            out[i] = value

    return pl.pallas_call(
        kernel,
        out_shape=like((13,), jnp.int32),
        in_specs=[whole(pltpu.SMEM)] * 2,
        out_specs=whole(pltpu.SMEM),
    )(parents, spot)


def key_value_kernel(flags, tokens, gain_in, wkv, gain_key, cos_table, sin_table):
    rows, width = tokens.shape
    head = wkv.shape[1] // 2
    half = head // 2

    def kernel(f, t_ref, gain_ref, w_ref, key_gain_ref, c_ref, s_ref, pairs, normed, raw, *sends):
        values = t_ref[...].astype(F32)
        low = (values * row_scale(values) * gain_ref[...]).astype(BF16)
        made = dot(low, w_ref[...])
        key = made[:, :head]
        scaled = key * row_scale(key) * key_gain_ref[...]
        pair = jnp.concatenate(
            [rotate(scaled, c_ref[...], s_ref[...]), made[:, head:]], axis=1
        ).astype(BF16)
        pairs[...] = pair
        for n in range(3):

            @pl.when(pl.program_id(0) == f[6 + n])
            def _(n=n):
                sends[n][...] = pair

        @pl.when(pl.program_id(0) == f[1])
        def _():
            normed[...] = low
            raw[...] = key

    def rows_of(x):
        return pl.BlockSpec((SEG, x), lambda i, p: (i, 0))

    return prefetch_call(
        kernel,
        flags,
        (rows // SEG,),
        (tokens, gain_in, wkv, gain_key, cos_table, sin_table),
        [rows_of(width), full(gain_in), full(wkv), full(gain_key), rows_of(half), rows_of(half)],
        [like((rows, 2 * head), BF16), like((SEG, width), BF16), like((SEG, head))]
        + [like((SEG, 2 * head), BF16)] * 3,
        [
            rows_of(2 * head),
            pl.BlockSpec((SEG, width), lambda i, p: (0, 0)),
            pl.BlockSpec((SEG, head), lambda i, p: (0, 0)),
        ]
        + [pl.BlockSpec((SEG, 2 * head), lambda i, p: (0, 0))] * 3,
        us=6,
    )


def query_kernel(plane, normed, wq, gain_query, cos_table, sin_table, head):
    width, total = wq.shape
    half = head // 2

    def kernel(plane_ref, n_ref, w_ref, gain_ref, c_ref, s_ref, query, raw):
        made = dot(n_ref[...], w_ref[...])
        raw[...] = made
        scaled = made * row_scale(made) * gain_ref[...]
        query[...] = rotate(scaled, c_ref[...], s_ref[...]).astype(BF16)

    by_head = pl.BlockSpec((SEG, head), lambda h, p: (0, h))
    table = pl.BlockSpec((SEG, half), lambda h, p: (p[0], 0))
    return prefetch_call(
        kernel,
        plane.reshape(1),
        (total // head,),
        (normed, wq, gain_query, cos_table, sin_table),
        [full(normed), pl.BlockSpec((width, head), lambda h, p: (0, h)), full(gain_query), table, table],
        [like((SEG, total), BF16), like((SEG, total))],
        [by_head, by_head],
        us=2.3,
    )


def visible_pairs(alive_a, alive_b):
    at_query = lax.broadcasted_iota(jnp.int32, (SEG, 3 * SEG), 0)
    spot = lax.broadcasted_iota(jnp.int32, (SEG, 3 * SEG), 1)
    own = (spot < SEG) & (spot <= at_query)
    above = (spot >= SEG) & (spot < 2 * SEG) & (alive_a > 0)
    top = (spot - 2 * SEG > at_query) & (alive_b > 0)
    return own | above | top


def softmax_of(query, keys, scale, alive_a, alive_b):
    scores = dot(query, keys, (1, 1)) * scale
    scores = jnp.where(visible_pairs(alive_a, alive_b), scores, MASKED)
    weights = jnp.exp(scores - jnp.max(scores, axis=-1, keepdims=True))
    return weights / jnp.sum(weights, axis=-1, keepdims=True)


def attention_kernel(flags, query, pairs, got_1, got_2, got_3):
    total = query.shape[1]
    head = pairs.shape[1] // 2

    def kernel(f, q_ref, pairs_ref, g1, g2, g3, heads, slots):
        @pl.when(pl.program_id(0) == 0)
        def _():
            role = f[0]

            def near(n):
                return pairs_ref[pl.ds(pl.multiple_of(n * SEG, SEG), SEG), :]

            slots[:SEG] = near(f[1])

            @pl.when(role == 0)
            def _():
                slots[SEG : 2 * SEG] = near(f[2])
                slots[2 * SEG :] = near(f[3])

            @pl.when(role == 1)
            def _():
                slots[SEG : 2 * SEG] = g1[...]
                slots[2 * SEG :] = g3[...]

            @pl.when(role == 2)
            def _():
                slots[SEG : 2 * SEG] = g1[...]
                slots[2 * SEG :] = g2[...]

            @pl.when(role == 3)
            def _():
                slots[SEG : 2 * SEG] = g2[...]
                slots[2 * SEG :] = g3[...]

        probs = softmax_of(q_ref[...], slots[:, :head], head**-0.5, f[4], f[5])
        heads[...] = dot(probs.astype(BF16), slots[:, head:]).astype(BF16)

    by_head = pl.BlockSpec((SEG, head), lambda h, f: (0, h))
    ins = (query, pairs, got_1, got_2, got_3)
    return prefetch_call(
        kernel,
        flags,
        (total // head,),
        ins,
        [by_head] + [full(x) for x in ins[1:]],
        [like((SEG, total), BF16), like((3 * SEG, 2 * head), BF16)],
        [by_head, pl.BlockSpec((3 * SEG, 2 * head), lambda h, f: (0, 0))],
        us=5.4,
    )


def middle_kernel(plane, heads_own, heads_got, wo_t, tokens, gain_post, gain_ffn):
    width, total = wo_t.shape

    def kernel(p, own, got, w_ref, t_ref, post_ref, gain_ref, attn, mid, normed):
        i = pl.program_id(0)

        def run(heads):
            made = dot(heads[...], w_ref[...], (1, 1))

            @pl.when(i == 0)
            def _():
                attn[...] = made

            middle = t_ref[...].astype(F32) + made * row_scale(made) * post_ref[...]
            mid[...] = middle
            normed[...] = (middle * row_scale(middle) * gain_ref[...]).astype(BF16)

        pl.when(i == 0)(lambda: run(own))
        pl.when(i == 1)(lambda: run(got))

    rows = pl.BlockSpec((SEG, width), lambda i, p: (i, 0))
    return prefetch_call(
        kernel,
        plane.reshape(1),
        (2,),
        (heads_own, heads_got, wo_t, tokens, gain_post, gain_ffn),
        [
            full(heads_own),
            full(heads_got),
            full(wo_t),
            pl.BlockSpec((SEG, width), lambda i, p: (p[0] ^ i, 0)),
            full(gain_post),
            full(gain_ffn),
        ],
        [like((SEG, width)), like((2 * SEG, width)), like((2 * SEG, width), BF16)],
        [pl.BlockSpec((SEG, width), lambda i, p: (0, 0)), rows, rows],
        us=4.5,
    )


def both_cores(pieces):
    return pieces + [(swap(piece, "gc"), row, slot + 1) for piece, row, slot in pieces]


class Blocks:
    def __init__(self, pieces, block):
        self.jobs = []
        if block is None:
            self.pieces = tuple(pieces)
            self.width, self.units = pieces[0].shape
            self.slots = jnp.zeros((1,), jnp.int32)
            self.jobs = [(m, 0, m, 0, self.width, None) for m in range(3)]
            return
        self.pieces = tuple(piece for piece, _, _ in pieces)
        self.units = self.pieces[0].shape[1]
        self.width = 8 * block
        here = lax.axis_index(PLANE)
        self.slots = jnp.array([slot for _, _, slot in pieces], jnp.int32)
        self.slots = (self.slots ^ here) * block
        for i, (piece, start, _) in enumerate(pieces):
            for m in range(3):
                low, high = max(start, m * block), min(start + piece.shape[0], (m + 1) * block)
                if low < high:
                    self.jobs.append((i, low - start, m, low - m * block, high - low, i))

    @classmethod
    def collected(cls, own, other, block):
        made = cls([(own, 0, 0), (other, 0, 1)], block)
        here = lax.axis_index(PLANE)
        made.slots = chip_slots() * block
        made.jobs = [
            (i, (3 * chip + m) * block, m, 0, block, 4 * i + chip)
            for i in range(2)
            for chip in range(4)
            for m in range(3)
        ]
        return made

    def scratch(self):
        return [
            pltpu.VMEM((3, self.width, self.units), BF16),
            pltpu.SemaphoreType.DMA((len(self.jobs),)),
        ]

    def copies(self, slots, refs, held, sems, matrix):
        made = []
        for n, (i, source, m, to, rows, slot) in enumerate(self.jobs):
            if m == matrix:
                base = 0 if slot is None else pl.multiple_of(slots[slot], 16)
                made.append(
                    pltpu.make_async_copy(
                        refs[i].at[pl.ds(source, rows)],
                        held.at[m, pl.ds(base + to, rows)],
                        sems.at[n],
                    )
                )
        return made


def ffn_forward_kernel(blocks, normed, part):
    rows, width = normed.shape
    units = blocks.units
    count = len(blocks.pieces)
    first = part is None

    def kernel(slots, n_ref, *refs):
        if not first:
            part_ref, refs = refs[0], refs[1:]
        pieces, (act, slope, hidden, out, held, sems) = refs[:count], refs[count:]
        start = pl.program_id(0) == 0

        def wait(m):
            @pl.when(start)
            def _():
                for copy in blocks.copies(slots, pieces, held, sems, m):
                    copy.wait()

        @pl.when(start)
        def _():
            for m in range(3):
                for copy in blocks.copies(slots, pieces, held, sems, m):
                    copy.start()

        left = n_ref[...]
        wait(0)
        gate = dot(left, held[0])
        wait(1)
        up = dot(left, held[1])
        square_gate = gate * gate
        turn = jnp.tanh(GELU_A * (gate + GELU_B * gate * square_gate))
        spread = 0.5 * (1.0 + turn)
        gelu = gate * spread
        bend = spread + 0.5 * gate * (1.0 - turn * turn) * (
            GELU_A * (1.0 + 3.0 * GELU_B * square_gate)
        )
        act[...] = gelu.astype(BF16)
        slope[...] = (up * bend).astype(BF16)
        low = (gelu * up).astype(BF16)
        hidden[...] = low
        wait(2)
        made = dot(low, held[2], (1, 1))
        out[...] = made if first else part_ref[...] + made

    by_rows = pl.BlockSpec((SEG, width), lambda i, s: (i, 0))
    by_units = pl.BlockSpec((SEG, units), lambda i, s: (i, 0))
    return prefetch_call(
        kernel,
        blocks.slots,
        (rows // SEG,),
        (normed,) + (() if first else (part,)) + blocks.pieces,
        [by_rows] + ([] if first else [by_rows]) + [whole(pl.ANY)] * count,
        [like((rows, units), BF16)] * 3 + [like((rows, width))],
        [by_units] * 3 + [by_rows],
        blocks.scratch(),
        mib=58,
        us=16,
    )


def ffn_backward_kernel(blocks, d_ffn, act, slope, back):
    rows, width = d_ffn.shape
    units = blocks.units
    count = len(blocks.pieces)
    first = back is None

    def kernel(slots, d_ref, act_ref, slope_ref, *refs):
        if not first:
            back_ref, refs = refs[0], refs[1:]
        pieces, (d_gate, d_up, out, held, sems) = refs[:count], refs[count:]
        start = pl.program_id(0) == 0

        def wait(m):
            @pl.when(start)
            def _():
                for copy in blocks.copies(slots, pieces, held, sems, m):
                    copy.wait()

        @pl.when(start)
        def _():
            for m in (2, 0, 1):
                for copy in blocks.copies(slots, pieces, held, sems, m):
                    copy.start()

        wait(2)
        d_hidden = dot(d_ref[...], held[2])
        to_gate = (d_hidden * slope_ref[...].astype(F32)).astype(BF16)
        to_up = (d_hidden * act_ref[...].astype(F32)).astype(BF16)
        d_gate[...] = to_gate
        d_up[...] = to_up
        wait(0)
        wait(1)
        made = dot(to_gate, held[0], (1, 1)) + dot(to_up, held[1], (1, 1))
        out[...] = made if first else back_ref[...] + made

    by_rows = pl.BlockSpec((SEG, width), lambda i, s: (i, 0))
    by_units = pl.BlockSpec((SEG, units), lambda i, s: (i, 0))
    return prefetch_call(
        kernel,
        blocks.slots,
        (rows // SEG,),
        (d_ffn, act, slope) + (() if first else (back,)) + blocks.pieces,
        [by_rows, by_units, by_units] + ([] if first else [by_rows]) + [whole(pl.ANY)] * count,
        [like((rows, units), BF16)] * 2 + [like((rows, width))],
        [by_units] * 2 + [by_rows],
        blocks.scratch(),
        mib=58,
        us=16,
    )


def ffn_end_kernel(plane, ffn_own, ffn_other, mid, cotangent, gain):
    rows, width = mid.shape

    def kernel(p, own_ref, other_ref, mid_ref, up_ref, gain_ref, d_out, d_turned, out, share):
        i = pl.program_id(0)
        g = gain_ref[...]

        def run(ref, own):
            ffn = ref[...].astype(F32)
            r = row_scale(ffn)
            incoming = up_ref[...].astype(F32)
            out[...] = (mid_ref[...] + ffn * r * g).astype(BF16)
            if own:
                share[...] = jnp.sum(incoming * ffn * r, axis=0, keepdims=True)
            scaled = g * incoming
            inner = jnp.mean(ffn * scaled, axis=-1, keepdims=True)
            made = (r * scaled - ffn * (r * r * r) * inner).astype(BF16)
            d_out[...] = made
            d_turned[...] = made.T

        pl.when(i == 0)(lambda: run(own_ref, True))
        pl.when(i == 1)(lambda: run(other_ref, False))

    once = pl.BlockSpec((SEG, width), lambda i, p: (0, 0))
    by_rows = pl.BlockSpec((SEG, width), lambda i, p: (i, 0))
    return prefetch_call(
        kernel,
        plane.reshape(1),
        (2,),
        (ffn_own, ffn_other, mid, cotangent, gain),
        [once, once, by_rows, pl.BlockSpec((SEG, width), lambda i, p: (p[0] ^ i, 0)), full(gain)],
        [like((rows, width), BF16), like((width, rows), BF16), like((rows, width), BF16), like((1, width))],
        [
            by_rows,
            pl.BlockSpec((width, SEG), lambda i, p: (0, i)),
            by_rows,
            pl.BlockSpec((1, width), lambda i, p: (0, 0)),
        ],
        us=3.4,
    )


def spread_kernel(plane, blocks, order, dtype):
    width = blocks[0].shape[1]
    count = len(blocks)
    spots = [(n, r) for n, x in enumerate(blocks) for r in range(x.shape[0] // SEG)]

    def kernel(p, *refs):
        ins, out = refs[:count], refs[count]
        for i, (n, r) in enumerate(spots):

            @pl.when(pl.program_id(0) == p[0] ^ order[i])
            def _(n=n, r=r):
                out[...] = ins[n][r * SEG : (r + 1) * SEG].astype(dtype)

    return prefetch_call(
        kernel,
        plane.reshape(1),
        (4,),
        tuple(blocks),
        [full(x) for x in blocks],
        like((4 * SEG, width), dtype),
        pl.BlockSpec((SEG, width), lambda i, p: (i, 0)),
        us=3,
    )


def attention_back_kernel(
    flags, back, got, mid, cotangent, gain_ffn, attn, gain_post, wo_t, query, query_raw, gain_query,
    slots, cos_table, sin_table, head,
):
    width, total = wo_t.shape
    heads = total // head
    half = head // 2
    scale = head**-0.5

    def kernel(
        f, back_ref, got_ref, mid_ref, up_ref, gain_ffn_ref, attn_ref, gain_post_ref, w_ref, q_ref,
        raw_ref, gain_query_ref, slots_ref, c_ref, s_ref,
        d_mid, d_attn, d_attn_turned, shares, d_query, query_share, d_self, d_a, d_b, sums,
    ):
        h = pl.program_id(0)

        @pl.when(h == 0)
        def _():
            incoming = back_ref[...] + got_ref[...].astype(F32)
            add, share = norm_back(mid_ref[...], gain_ffn_ref[...], incoming)
            made = up_ref[...].astype(F32) + add
            d_mid[...] = made
            d_a_low, share_post = norm_back(attn_ref[...], gain_post_ref[...], made)
            low = d_a_low.astype(BF16)
            d_attn[...] = low
            d_attn_turned[...] = low.T
            shares[0:1, :] = jnp.sum(share, axis=0, keepdims=True)
            shares[1:2, :] = jnp.sum(share_post, axis=0, keepdims=True)
            sums[...] = jnp.zeros_like(sums)
            query_share[...] = jnp.zeros_like(query_share)

        keys, values = slots_ref[:, :head], slots_ref[:, head:]
        q = q_ref[...]
        d_heads = dot(d_attn[...], w_ref[...]).astype(BF16)
        probs = softmax_of(q, keys, scale, f[4], f[5])
        d_probs = dot(d_heads, values, (1, 1))
        d_scores = probs * (d_probs - jnp.sum(d_probs * probs, axis=-1, keepdims=True))
        d_scores = d_scores.astype(BF16)
        sums[:, :head] += dot(d_scores, q, (0, 0))
        sums[:, head:] += dot(probs.astype(BF16), d_heads, (0, 0))
        turned = rotate(dot(d_scores, keys) * scale, c_ref[...], -s_ref[...])
        made, share = norm_back(raw_ref[...], gain_query_ref[...], turned)
        d_query[...] = made.astype(BF16)
        query_share[...] += jnp.sum(share, axis=0, keepdims=True)

        @pl.when(h == heads - 1)
        def _():
            sums[:, :head] = sums[:, :head] * scale
            d_self[...] = sums[:SEG]
            d_a[...] = sums[SEG : 2 * SEG].astype(BF16)
            d_b[...] = sums[2 * SEG :].astype(BF16)

    def once(shape):
        return pl.BlockSpec(shape, lambda h, f: (0,) * len(shape))

    by_head = pl.BlockSpec((SEG, head), lambda h, f: (0, h))
    table = pl.BlockSpec((SEG, half), lambda h, f: (f[1], 0))
    rows = once((SEG, width))
    return prefetch_call(
        kernel,
        flags,
        (heads,),
        (back, got, mid, cotangent, gain_ffn, attn, gain_post, wo_t, query, query_raw, gain_query,
         slots, cos_table, sin_table),
        [
            rows,
            rows,
            rows,
            pl.BlockSpec((SEG, width), lambda h, f: (f[1], 0)),
            full(gain_ffn),
            rows,
            full(gain_post),
            pl.BlockSpec((width, head), lambda h, f: (0, h)),
            by_head,
            by_head,
            full(gain_query),
            full(slots),
            table,
            table,
        ],
        [
            like((SEG, width)),
            like((SEG, width), BF16),
            like((width, SEG), BF16),
            like((2, width)),
            like((SEG, total), BF16),
            like((1, head)),
            like((SEG, 2 * head)),
            like((SEG, 2 * head), BF16),
            like((SEG, 2 * head), BF16),
        ],
        [
            rows,
            rows,
            once((width, SEG)),
            once((2, width)),
            by_head,
            once((1, head)),
            once((SEG, 2 * head)),
            once((SEG, 2 * head)),
            once((SEG, 2 * head)),
        ],
        [pltpu.VMEM((3 * SEG, 2 * head), F32)],
        us=12,
    )


def tokens_back_kernel(
    plane, terms, key_raw, gain_key, cos_table, sin_table, wkv, d_normed, d_mid, tokens, gain_in
):
    width = d_mid.shape[1]
    head = key_raw.shape[1]
    half = head // 2
    count = len(terms)

    def kernel(p, *refs):
        terms_in, refs = refs[:count], refs[count:]
        (raw_ref, gain_ref, c_ref, s_ref, w_ref, dn_ref, mid_ref, t_ref, gain_in_ref) = refs[:9]
        d_kv, rows_out, share_key, share_in = refs[9:]
        total = terms_in[0][...].astype(F32)
        for term in terms_in[1:]:
            total = total + term[...].astype(F32)
        turned = rotate(total[:, :head], c_ref[...], -s_ref[...])
        made, share = norm_back(raw_ref[...], gain_ref[...], turned)
        share_key[...] = jnp.sum(share, axis=0, keepdims=True)
        low = jnp.concatenate([made, total[:, head:]], axis=1).astype(BF16)
        d_kv[...] = low
        incoming = dn_ref[...] + dot(low, w_ref[...], (1, 1))
        add, share = norm_back(t_ref[...].astype(F32), gain_in_ref[...], incoming)
        share_in[...] = jnp.sum(share, axis=0, keepdims=True)
        rows_out[...] = (mid_ref[...] + add).astype(BF16)

    table = pl.BlockSpec((SEG, half), lambda i, p: (p[0], 0))
    ins = (*terms, key_raw, gain_key, cos_table, sin_table, wkv, d_normed, d_mid, tokens, gain_in)
    specs = [full(x) for x in ins]
    specs[count + 2] = specs[count + 3] = table
    specs[count + 7] = pl.BlockSpec((SEG, width), lambda i, p: (p[0], 0))
    outs = [like((SEG, 2 * head), BF16), like((SEG, width), BF16), like((1, head)), like((1, width))]
    return prefetch_call(
        kernel, plane.reshape(1), (1,), ins, specs, outs, [full(o) for o in outs], us=3
    )


def window_kernel(flags, d_self, d_a, d_b, back_1, back_2, back_3):
    shape = (2,) + d_self.shape

    def kernel(f, own_ref, a_ref, b_ref, b1, b2, b3, sent, kept):
        role, plane = f[0], f[1]
        near = role == 0
        ats = [
            plane,
            jnp.where(near & (f[4] > 0), f[2], -1),
            jnp.where(near & (f[5] > 0), f[3], -1),
            jnp.where(role <= 1, f[6], -1),
            jnp.where(role <= 1, f[7], -1),
            jnp.where(near, f[8], -1),
        ]
        refs = (own_ref, a_ref, b_ref, b1, b2, b3)
        for out, k, other in ((sent, 0, 1), (sent, 1, 3), (kept, 0, 0), (kept, 1, 2)):
            number = plane ^ other
            total = jnp.zeros(out.shape[1:], F32)
            for at, ref in zip(ats, refs):
                total = total + jnp.where(at == number, ref[...].astype(F32), 0.0)
            out[k] = total.astype(BF16)

    return pl.pallas_call(
        kernel,
        out_shape=[like(shape, BF16)] * 2,
        in_specs=[whole(pltpu.SMEM)] + [whole(pltpu.VMEM)] * 6,
        out_specs=[whole(pltpu.VMEM)] * 2,
        compiler_params=params(32),
        cost_estimate=cost(2.4),
    )(flags, d_self, d_a, d_b, back_1, back_2, back_3)


def z_first(sent, kept, kept_far):
    got = across(sent, 1).astype(F32)
    return tie((kept.astype(F32) + got[0]).astype(BF16), (kept_far.astype(F32) + got[1]).astype(BF16))


def z_halve(x):
    here = lax.axis_index("gx")

    def at(n):
        return lax.dynamic_index_in_dim(x, n, 0, keepdims=False)

    return z_first(jnp.stack([at(here ^ 1), at(here ^ 3)]), at(here), at(here ^ 2))


def body(
    tokens,
    parents,
    w_query,
    w_key,
    w_value,
    w_out,
    w_gate,
    w_up,
    w_down,
    g_attn_in,
    g_attn_out,
    g_ffn_in,
    g_ffn_out,
    g_query,
    g_key,
    cotangent,
):
    column = lax.axis_index(PLANE)
    columns = lax.axis_size(PLANE)
    plane = lax.axis_index("gx")
    planes = lax.axis_size("gx")
    width = tokens.shape[1]
    head_width = w_key.shape[1]
    heads = planes * w_query.shape[1] // head_width
    block, small = w_query.shape[0], w_key.shape[0]
    gains_len = 4 * block + 2 * g_query.shape[0]
    pack_width = 2 * head_width
    gain_rows = -(-gains_len // pack_width)
    used = small + gain_rows
    gain_spot = -(-small // 8) * 8
    pack_rows = -(-(block + gain_spot + gain_rows) // 16) * 16

    core = lax.axis_index("gc")
    down_t = w_down.T
    ffn_mine = jnp.concatenate([w_gate, w_up, down_t], axis=0)
    gains = jnp.concatenate([g_attn_in, g_attn_out, g_ffn_in, g_ffn_out, g_query, g_key])
    gains = jnp.pad(gains, (0, gain_rows * pack_width - gains_len)).reshape(gain_rows, pack_width)
    pack = jnp.concatenate(
        [
            jnp.concatenate([w_query, w_out.T], axis=1),
            jnp.concatenate([w_key, w_value], axis=1),
            jnp.zeros((gain_spot - small, pack_width), BF16),
            gains,
            jnp.zeros((pack_rows - block - gain_spot - gain_rows, pack_width), BF16),
        ],
        axis=0,
    )
    flags = flags_kernel(parents, jnp.stack([column, plane]).astype(jnp.int32))
    depth = flags[9:13, None] * SEG + jnp.arange(SEG, dtype=jnp.int32)[None, :]
    half_width = head_width // 2
    rates = 10000.0 ** (-jnp.arange(half_width, dtype=F32) / half_width)
    turned = depth.reshape(-1).astype(F32)[:, None] * rates[None, :]
    cos_table, sin_table = jnp.cos(turned), jnp.sin(turned)
    if square():
        ffn_x, ffn_y = send_near(ffn_mine)
        pack = lax.all_gather(pack, "gx", axis=0)
        pack, other_gu = tie(pack, ffn_mine[: 2 * block])
        their_gu = across(other_gu, 2)
        pack_x, pack_y = send_near(pack)
        ffn_x, ffn_y, pack, pack_x, pack_y, cos_table, sin_table = tie(
            ffn_x, ffn_y, pack, pack_x, pack_y, cos_table, sin_table
        )
        pack_far = send_far(pack_x, pack_y)
        ffn_far = send_far(ffn_x, ffn_y)
        *pack_far, their_gu, other_down = tie(*pack_far, their_gu, down_t)
        their_down = across(other_down, 2)
        pack_all = collect((pack, pack_x, pack_y, *pack_far), planes)
        pack_other = swap(pack_all, "gc")
        wq, wo_t, wkv, gains = unpack(
            [pack_all, pack_other], block, head_width, gain_spot, gain_rows
        )
    else:
        pack = lax.all_gather(pack, "gx", axis=0, tiled=True)
        pack = lax.all_gather(pack, PLANE, axis=0).reshape(columns, planes, pack_rows, pack_width)

        def from_blocks(blocks):
            return blocks.transpose(0, 2, 1, 3).reshape(columns * block, -1)

        wq = from_blocks(pack[:, :, :block, :head_width])
        wo_t = from_blocks(pack[:, :, :block, head_width:])
        wkv = pack[:, :, block : block + small].transpose(1, 0, 2, 3).reshape(width, pack_width)
        gains = pack[:, 0, block + gain_spot : block + gain_spot + gain_rows]

        def ffn_weights(mine):
            stacked = lax.all_gather(mine, PLANE, axis=0).reshape(columns, 3, block, -1)
            return Blocks([stacked[:, i].reshape(width, -1) for i in range(3)], None)

        quarter_mine = ffn_weights(ffn_mine)
        quarter_theirs = ffn_weights(across(ffn_mine, 2))

    gains = gains.reshape(columns, -1)[:, :gains_len].astype(F32)
    gain_in, gain_post, gain_ffn, gain_last = [
        gains[:, i * block : (i + 1) * block].reshape(1, -1) for i in range(4)
    ]
    gain_query, gain_key = [
        gains[:, 4 * block + i * g_query.shape[0] :][:, : g_query.shape[0]].reshape(1, -1)
        for i in range(2)
    ]

    role = column % 4
    trees = range(columns // 4)
    route_1 = [(4 * t + i, 4 * t + i + 1) for t in trees for i in (0, 1)]
    route_2 = [(4 * t + i, 4 * t + i + 2) for t in trees for i in (0, 1)]
    route_3 = [(4 * t + i, 4 * t + i + 1) for t in trees for i in (0, 2)]

    def send(x, route):
        return lax.ppermute(x, PLANE, route)

    def send_back(x, route):
        return lax.ppermute(x, PLANE, [(b, a) for a, b in route])

    pairs, normed_own, key_raw, send_1, send_2, send_3 = key_value_kernel(
        flags, tokens, gain_in, wkv, gain_key, cos_table, sin_table
    )
    if square():
        send_1, send_2 = tie(send_1, send_2)
    got_1 = send(send_1, route_1)
    got_2 = send(send_2, route_2)
    query, query_raw = query_kernel(
        plane, normed_own, wq, gain_query, cos_table, sin_table, head_width
    )
    if square():
        query, ffn_x, ffn_y, their_down, *ffn_far = tie(query, ffn_x, ffn_y, their_down, *ffn_far)
        theirs = jnp.concatenate([their_gu, their_down], axis=0)
        mine_all = collect((ffn_mine, ffn_x, ffn_y, *ffn_far), 3 * block)
        got_1, got_2, mine_all, theirs = tie(got_1, got_2, mine_all, theirs)
        mine_other = swap(mine_all, "gc")
        their_x, their_y = send_near(theirs)
    got_3 = send(jnp.where(role == 2, got_2, send_3), route_3)
    heads_low, slots = attention_kernel(flags, query, pairs, got_1, got_2, got_3)

    if square():
        heads_low, mine_other = tie(heads_low, mine_other)
        heads_got = across(heads_low, 1)
        quarter_mine = Blocks.collected(mine_all, mine_other, block)
    else:
        heads_got = across(heads_low, 1)
    attn, mid, normed_ffn = middle_kernel(
        plane, heads_low, heads_got, wo_t, tokens, gain_post, gain_ffn
    )
    if square():
        normed_ffn, their_x, their_y = tie(normed_ffn, their_x, their_y)
        their_far = send_far(their_x, their_y)
        near_pieces = both_cores([(theirs, 0, 0), (their_x, 0, 2), (their_y, 0, 4)])
    act_m, slope_m, hidden_m, ffn_part = ffn_forward_kernel(quarter_mine, normed_ffn, None)
    if square():
        ffn_part, *their_far = tie(ffn_part, *their_far)
        far_pieces = both_cores([(their_far[0], 0, 6), (their_far[1], their_far[0].shape[0], 6)])
        quarter_theirs = Blocks(near_pieces + far_pieces, block)
    act_t, slope_t, hidden_t, ffn_part = ffn_forward_kernel(quarter_theirs, normed_ffn, ffn_part)
    ffn_got = across(ffn_part[SEG:].astype(BF16), 1)
    ffn_own = (ffn_part[:SEG] + ffn_got.astype(F32)).astype(BF16)
    ffn_other = across(ffn_own, 1)
    d_ffn_low, d_ffn_t, output, d_gain_last = ffn_end_kernel(
        plane, ffn_own, ffn_other, mid, cotangent, gain_last
    )

    output_far = [across(output[:SEG], 2)]
    d_gate_t, d_up_t, back = ffn_backward_kernel(quarter_theirs, d_ffn_low, act_t, slope_t, None)
    if square():
        lefts = (normed_ffn.T, d_ffn_t)
        send_theirs = ffn_weight_grads(1 - core, *lefts, d_gate_t, d_up_t, hidden_t, block)
        keep_theirs = ffn_weight_grads(core, *lefts, d_gate_t, d_up_t, hidden_t, block)
        back, send_theirs, keep_theirs, output_far[0] = tie(
            back, send_theirs, keep_theirs, output_far[0]
        )
        recv_theirs = swap(send_theirs, "gc")
    d_gate_m, d_up_m, back = ffn_backward_kernel(quarter_mine, d_ffn_low, act_m, slope_m, back)
    if square():
        back, recv_theirs = tie(back, recv_theirs)
        theirs = Scatter(keep_theirs, recv_theirs)
    back_got = across(back[SEG:].astype(BF16), 1)
    if square():
        theirs_far = send_xy(theirs.far_blocks())
        theirs_first = send_xy(theirs.first_blocks())
        back_got, output = tie(back_got, output)
    else:
        grads = []
        for d_gate, d_up, hidden in ((d_gate_m, d_up_m, hidden_m), (d_gate_t, d_up_t, hidden_t)):
            blocks = [
                dot(normed_ffn, d_gate, (0, 0)),
                dot(normed_ffn, d_up, (0, 0)),
                dot(d_ffn_low, hidden, (0, 0)),
            ]
            blocks = [m.astype(BF16).reshape(columns, block, -1) for m in blocks]
            grads.append(plane_scatter(jnp.concatenate(blocks, axis=1)))
        ffn_grad = grads[0] + across(grads[1].astype(BF16), 2).astype(F32)

    output_far.append(across(output[SEG : SEG + SEG // 2], 2))

    (
        d_mid, d_attn_low, d_attn_t, d_gains_mid, d_query_low, d_gain_query, d_self, d_a, d_b,
    ) = attention_back_kernel(
        flags, back, back_got, mid, cotangent, gain_ffn, attn, gain_post, wo_t, query, query_raw,
        gain_query, slots, cos_table, sin_table, head_width,
    )
    if square():
        d_a, d_b, output_far[1], output, d_gate_m = tie(
            d_a, d_b, output_far[1], output, d_gate_m
        )
    output_far.append(across(output[SEG + SEG // 2 :], 2))
    back_1 = send_back(d_a, route_1)
    back_3 = send_back(d_b, route_3)
    if square():
        theirs_second = theirs.second_blocks(*theirs_far)
        made = (*lefts, d_gate_m, d_up_m, hidden_m)
        send_mine = ffn_weight_grads(1 - core, *made, block)
        d_a, d_b, back_1, back_3, send_mine, d_gate_m, *flat = tie(
            d_a, d_b, back_1, back_3, send_mine, d_gate_m, *theirs_first, *theirs_second
        )
        theirs_first, theirs_second = flat[:2], flat[2:]
    d_b_far = jnp.where(role == 2, d_b.astype(F32) + back_3.astype(F32), 0.0).astype(BF16)
    to_back_2 = jnp.where(role == 3, d_a, d_b_far)
    back_2 = send_back(to_back_2, route_2)
    if square():
        theirs_second = send_xy(theirs_second)
        keep_mine = ffn_weight_grads(core, *lefts, d_gate_m, d_up_m, hidden_m, block)
        back_2, output_far[2], keep_mine, send_mine = tie(
            back_2, output_far[2], keep_mine, send_mine
        )
        recv_mine = swap(send_mine, "gc")
    sent, kept = window_kernel(flags, d_self, d_a, d_b, back_1, back_2, back_3)
    kept, passed = z_first(sent, kept[0], kept[1])
    if square():
        passed, d_query_low, keep_mine, recv_mine = tie(
            passed, d_query_low, keep_mine, recv_mine
        )
    d_normed_query = dot(d_query_low, wq, (1, 1))
    own_terms = [kept, across(passed, 2)]
    if square():
        mine = Scatter(keep_mine, recv_mine)
        mine_far = send_xy(mine.far_blocks())
        theirs_sum = theirs.total(theirs_first, theirs_second).astype(BF16)
        own_terms[1], theirs_sum, d_normed_query, d_gains_mid, d_gain_last, d_gain_query = tie(
            own_terms[1], theirs_sum, d_normed_query, d_gains_mid, d_gain_last, d_gain_query
        )
    d_kv_low, token_rows, d_gain_key, d_gain_in = tokens_back_kernel(
        plane, own_terms, key_raw, gain_key, cos_table, sin_table, wkv, d_normed_query, d_mid,
        tokens, gain_in,
    )
    tokens_far = across(token_rows, 2)

    grad_kv = dot(normed_own, d_kv_low, (0, 0)).astype(BF16)
    grad_kv = grad_kv.reshape(planes, columns, small, -1).transpose(1, 0, 2, 3)
    gain_sums = [
        d_gain_in,
        d_gains_mid[1:],
        d_gains_mid[:1],
        d_gain_last,
        d_gain_query,
        d_gain_key,
    ]
    gain_sums = jnp.concatenate([g.reshape(columns, -1) for g in gain_sums], axis=1).astype(BF16)
    gain_sums = jnp.pad(gain_sums, ((0, 0), (0, gain_rows * pack_width - gains_len)))
    gain_sums = jnp.broadcast_to(
        gain_sums.reshape(columns, 1, gain_rows, pack_width),
        (columns, planes, gain_rows, pack_width),
    )
    rest_rows = pack_rows - block
    rest = jnp.concatenate(
        [grad_kv, gain_sums, jnp.zeros((columns, planes, pack_rows - block - used, pack_width), BF16)],
        axis=2,
    ).reshape(columns, planes * rest_rows, pack_width)
    if square():
        attn_lefts = (normed_own.T, d_query_low, d_attn_t, heads_low, rest)
        attn_send = attention_weight_grads(1 - core, *attn_lefts, block, planes)
        attn_keep = attention_weight_grads(core, *attn_lefts, block, planes)
        attn_received = swap(attn_send, "gc")
        attn_keep, attn_received, *mine_far = tie(attn_keep, attn_received, *mine_far)
        attn_work = Scatter(attn_keep, attn_received)
        attn_far = send_xy(attn_work.far_blocks())
        tokens_far, theirs_sum, *attn_far = tie(tokens_far, theirs_sum, *attn_far)
        attn_near = send_xy(attn_work.near_blocks(*attn_far))
        tokens_near = across(jnp.concatenate([token_rows, tokens_far], axis=0), 1)
        gate_sum = across(theirs_sum[:block], 2)
        mine_second = mine.second_blocks(*mine_far)
        gate_sum, tokens_near, other_up, *flat = tie(
            gate_sum, tokens_near, theirs_sum[block : 2 * block], *attn_near, *mine_second
        )
        up_sum = across(other_up, 2)
        mine_first = send_xy(mine.first_blocks())
        mine_second = flat[2:]
        grads = attn_work.near_total(*flat[:2])
    else:

        def to_blocks(grad):
            return grad.astype(BF16).reshape(columns, block, planes, -1).transpose(0, 2, 1, 3)

        grads = jnp.concatenate(
            [
                to_blocks(dot(normed_own, d_query_low, (0, 0))),
                to_blocks(dot(d_attn_low, heads_low, (0, 0))),
            ],
            axis=3,
        ).reshape(columns, planes * block, pack_width)
        grads = jnp.concatenate(
            [grads.reshape(columns, planes, block, -1), rest.reshape(columns, planes, rest_rows, -1)],
            axis=2,
        ).reshape(columns, planes * pack_rows, pack_width)
        grads = plane_scatter(grads)
    grads = grads.reshape(planes, pack_rows, pack_width)
    rest = jnp.broadcast_to(
        grads[:1, block + small :], (planes, pack_rows - block - small, pack_width)
    )
    grads = jnp.concatenate([grads[:, : block + small], rest], axis=1).astype(BF16)
    kept, passed = z_halve(grads)
    if square():
        passed, up_sum, other_down, *mine_second = tie(
            passed, up_sum, theirs_sum[2 * block :], *mine_second
        )
        mine_second = send_xy(mine_second)
        down_sum = across(other_down, 2)
    else:
        tokens_near = across(jnp.concatenate([token_rows, tokens_far], axis=0), 1)
    grads = kept.astype(F32) + across(passed, 2).astype(F32)
    if square():
        ffn_grad = mine.total(mine_first, mine_second) + jnp.concatenate(
            [gate_sum, up_sum, down_sum], axis=0
        ).astype(F32)
    grad_tokens = spread_kernel(plane, (token_rows, tokens_far, tokens_near), (0, 2, 1, 3), F32)
    output_far[1:] = [jnp.concatenate(output_far[1:], axis=0)]
    output = spread_kernel(plane, (output, *output_far), (0, 1, 2, 3), BF16)
    gain_grads = grads[block + small : block + used].reshape(-1)
    return (
        output,
        grad_tokens,
        gain_grads[:block],
        gain_grads[block : 2 * block],
        gain_grads[2 * block : 3 * block],
        gain_grads[3 * block : 4 * block],
        gain_grads[4 * block : 4 * block + g_query.shape[0]],
        gain_grads[4 * block + g_query.shape[0] : gains_len],
        grads[:block, :head_width],
        grads[block : block + small, :head_width],
        grads[block : block + small, head_width:],
        grads[:block, head_width:].T,
        ffn_grad[:block],
        ffn_grad[block : 2 * block],
        ffn_grad[2 * block :].T,
    )


def solution(mesh):
    side = math.isqrt(mesh.shape["gy"] // 2)
    split = Mesh(mesh.devices.reshape(mesh.shape["gx"], side, side, 2), ("gx",) + PLANE)
    whole = ("gx",) + PLANE
    return jax.shard_map(
        body,
        mesh=split,
        in_specs=(
            P(PLANE, None),
            P(),
            P(PLANE, "gx"),
            P(whole, None),
            P(whole, None),
            P("gx", PLANE),
            P(PLANE, "gx"),
            P(PLANE, "gx"),
            P("gx", PLANE),
            P(PLANE),
            P(PLANE),
            P(PLANE),
            P(PLANE),
            P(PLANE),
            P(PLANE),
            P(PLANE, None),
        ),
        out_specs=(
            P(PLANE, None),
            P(PLANE, None),
            P(PLANE),
            P(PLANE),
            P(PLANE),
            P(PLANE),
            P(PLANE),
            P(PLANE),
            P(PLANE, "gx"),
            P(whole, None),
            P(whole, None),
            P("gx", PLANE),
            P(PLANE, "gx"),
            P(PLANE, "gx"),
            P("gx", PLANE),
        ),
        check_vma=False,
    )
```

```python
import math

import jax
import jax.numpy as jnp
from jax import lax
from jax.experimental import pallas as pl
from jax.experimental.pallas import tpu as pltpu
from jax.sharding import Mesh
from jax.sharding import PartitionSpec as P

SEG = 256
EPSILON = 1e-06
MASKED = -1e30
PLANE = ("gb", "ga", "gc")
SWAP = [(0, 1), (1, 0)]
F32 = jnp.float32
BF16 = jnp.bfloat16


def rms_norm(values, gain):
    return values * lax.rsqrt(jnp.mean(values * values, axis=-1, keepdims=True) + EPSILON) * gain


def norm_back(values, gain, incoming):
    r = lax.rsqrt(jnp.mean(values * values, axis=-1, keepdims=True) + EPSILON)
    scaled = gain * incoming
    inner = jnp.mean(values * scaled, axis=-1, keepdims=True)
    return r * scaled - values * (r * r * r) * inner, incoming * values * r


def rotate(values, cos_table, sin_table):
    half_width = values.shape[-1] // 2
    a, b = values[..., :half_width], values[..., half_width:]
    return jnp.concatenate([a * cos_table - b * sin_table, b * cos_table + a * sin_table], axis=-1)


def dot(a, b, dims=(1, 0)):
    return lax.dot_general(
        a, b, (((dims[0],), (dims[1],)), ((), ())), preferred_element_type=F32
    )


def swap(x, axis):
    return lax.ppermute(x, axis, SWAP)


def across(x, distance):
    return lax.ppermute(x, "gx", [(i, i ^ distance) for i in range(4)])


def tie(*values):
    return lax.optimization_barrier(values)


def cost(microseconds):
    flops = int(microseconds * 1.0 * 1.15e9)
    return pl.CostEstimate(flops=flops, bytes_accessed=0, transcendentals=0)


def whole(array_or_space):
    return pl.BlockSpec(memory_space=array_or_space)


def params(mib):
    return pltpu.CompilerParams(vmem_limit_bytes=mib * 2**20)


def square():
    return lax.axis_size("ga") == 2


def halves(x):
    half = x.shape[0] // 32 * 16 or x.shape[0] // 2
    return x[:half], x[half:]


def send_near(x):
    return swap(x, "ga"), swap(x, "gb")


def send_far(from_x, from_y):
    return swap(halves(from_y)[0], "ga"), swap(halves(from_x)[1], "gb")


def collect(pieces, rows):
    count = len(pieces)
    starts = [0, rows, 2 * rows, 3 * rows, 3 * rows + pieces[3].shape[0]]
    shape = (4 * rows,) + pieces[0].shape[1:]

    def kernel(*refs):
        ins, (out, held, sems) = refs[:count], refs[count:]
        spots = [pl.ds(start, piece.shape[0]) for start, piece in zip(starts, pieces)]
        loads = [
            pltpu.make_async_copy(ref, held.at[spot], sems.at[0, i])
            for i, (ref, spot) in enumerate(zip(ins, spots))
        ]
        stores = [
            pltpu.make_async_copy(held.at[spot], out.at[spot], sems.at[1, i])
            for i, spot in enumerate(spots)
        ]
        for load in loads:
            load.start()
        for load, store in zip(loads, stores):
            load.wait()
            store.start()
        for store in stores:
            store.wait()

    return pl.pallas_call(
        kernel,
        out_shape=jax.ShapeDtypeStruct(shape, pieces[0].dtype),
        in_specs=[whole(pl.ANY)] * count,
        out_specs=whole(pl.ANY),
        scratch_shapes=[pltpu.VMEM(shape, pieces[0].dtype), pltpu.SemaphoreType.DMA((2, count))],
        compiler_params=params(24),
        cost_estimate=cost(4),
    )(*pieces)


def chip_slots():
    here = lax.axis_index(PLANE)
    return jnp.array([0, 2, 4, 6, 1, 3, 5, 7], jnp.int32) ^ here


def unpack(pieces, block, head_width, gain_spot, gain_rows):
    four, rows, width = pieces[0].shape
    planes = four // 4
    rest = rows - block
    small = block // planes
    count = len(pieces)
    jobs = [(i, 4 * chip + h, 4 * i + chip, h) for i in range(2) for chip in range(4) for h in range(planes)]

    def kernel(slot_ref, *refs):
        ins, (wq, wo, wkv, gains, other, sems) = refs[:count], refs[count:]
        copies = []
        for n, (i, j, at_slot, h) in enumerate(jobs):
            slot = slot_ref[at_slot]
            at = pl.ds(pl.multiple_of(slot * block, 16), block)
            to = pl.ds(h * head_width, head_width)
            parts = [
                (ins[i].at[j, pl.ds(0, block), pl.ds(0, head_width)], wq.at[at, to]),
                (ins[i].at[j, pl.ds(0, block), pl.ds(head_width, head_width)], wo.at[at, to]),
                (ins[i].at[j, pl.ds(block, rest), :], other.at[slot, h]),
            ]
            copies += [
                pltpu.make_async_copy(a, b, sems.at[n, m]) for m, (a, b) in enumerate(parts)
            ]
        for copy in copies:
            copy.start()
        for copy in copies:
            copy.wait()
        for c in range(8):
            gains[c] = other[c, 0, gain_spot : gain_spot + gain_rows, :]
        for h in range(planes):
            wkv[h * 8 * small : (h + 1) * 8 * small] = jnp.concatenate(
                [other[c, h, :small, :].astype(F32) for c in range(8)], axis=0
            ).astype(BF16)

    matrix = jax.ShapeDtypeStruct((8 * block, planes * head_width), BF16)
    return pl.pallas_call(
        kernel,
        out_shape=[
            matrix,
            matrix,
            jax.ShapeDtypeStruct((8 * block, width), BF16),
            jax.ShapeDtypeStruct((8, gain_rows, width), BF16),
        ],
        in_specs=[whole(pltpu.SMEM)] + [whole(pl.ANY)] * count,
        out_specs=[whole(pltpu.VMEM)] * 4,
        scratch_shapes=[
            pltpu.VMEM((8, planes, rest, width), BF16),
            pltpu.SemaphoreType.DMA((len(jobs), 3)),
        ],
        compiler_params=params(24),
        cost_estimate=cost(4.3),
    )(chip_slots(), *pieces)


def core_rows(ref, core, block):
    return jnp.concatenate(
        [ref[pl.ds(pl.multiple_of((2 * k + core) * block, 16), block), :] for k in range(4)],
        axis=0,
    )


def ffn_weight_grads(core, normed_t, d_ffn_t, d_gate, d_up, hidden, block):
    units = d_gate.shape[1]

    def kernel(core_ref, normed_ref, d_ffn_ref, gate_ref, up_ref, hidden_ref, out):
        m = pl.program_id(0)

        def run(left, right):
            rows = core_rows(left, core_ref[0], block)
            for n in range(0, units, 256):
                w = min(256, units - n)
                made = dot(rows, right[:, n : n + w]).astype(BF16)
                out[:, :, n : n + w] = made.reshape(4, block, w)

        for number, (left, right) in enumerate(
            ((normed_ref, gate_ref), (normed_ref, up_ref), (d_ffn_ref, hidden_ref))
        ):
            pl.when(m == number)(lambda left=left, right=right: run(left, right))

    def full(x):
        return pl.BlockSpec(x.shape, lambda m, c: (0, 0))

    ins = (normed_t, d_ffn_t, d_gate, d_up, hidden)
    return pl.pallas_call(
        kernel,
        grid_spec=pltpu.PrefetchScalarGridSpec(
            num_scalar_prefetch=1,
            grid=(3,),
            in_specs=[full(x) for x in ins],
            out_specs=pl.BlockSpec((4, block, units), lambda m, c: (0, m, 0)),
        ),
        out_shape=jax.ShapeDtypeStruct((4, 3 * block, units), BF16),
        compiler_params=params(48),
        cost_estimate=cost(6.7),
    )(core.reshape(1), *ins)


def attention_weight_grads(core, normed_t, d_query, d_attn_t, heads_low, other, block, planes):
    head_width = d_query.shape[1] // planes
    more = other.shape[1] // planes
    rows_all = block + more

    def kernel(core_ref, normed_ref, query_ref, d_attn_ref, heads_ref, other_ref, out):
        for half, (left, right) in enumerate(((normed_ref, query_ref), (d_attn_ref, heads_ref))):
            rows = core_rows(left, core_ref[0], block)
            for h in range(planes):
                made = dot(rows, right[:, h * head_width : (h + 1) * head_width]).astype(BF16)
                out[:, h * rows_all : h * rows_all + block, half * head_width : (half + 1) * head_width] = (
                    made.reshape(4, block, head_width)
                )
        for chip in range(4):
            for h in range(planes):
                out[chip, h * rows_all + block : (h + 1) * rows_all] = other_ref[
                    2 * chip + core_ref[0], h * more : (h + 1) * more
                ]

    return pl.pallas_call(
        kernel,
        out_shape=jax.ShapeDtypeStruct((4, planes * rows_all, 2 * head_width), BF16),
        in_specs=[whole(pltpu.SMEM)] + [whole(pltpu.VMEM)] * 5,
        out_specs=whole(pltpu.VMEM),
        compiler_params=params(32),
        cost_estimate=cost(2.5),
    )(core.reshape(1), normed_t, d_query, d_attn_t, heads_low, other)


class Scatter:
    def __init__(self, keep, received):
        y, x = lax.axis_index("gb"), lax.axis_index("ga")
        self.keep, self.received = keep, received
        self.here, self.x, self.y = 2 * y + x, 2 * y + 1 - x, 2 * (1 - y) + x
        self.far = 2 * (1 - y) + 1 - x
        self.half = keep.shape[1] // 32 * 16

    def part(self, chip, second=None):
        made = 0.0
        for values in (self.keep, self.received):
            block = lax.dynamic_index_in_dim(values, chip, 0, keepdims=False)
            if second is not None:
                block = block[self.half :] if second else block[: self.half]
            made = made + block.astype(F32)
        return made

    def far_blocks(self):
        return self.part(self.far, False).astype(BF16), self.part(self.far, True).astype(BF16)

    def first_blocks(self):
        return self.part(self.x, False).astype(BF16), self.part(self.y, True).astype(BF16)

    def second_blocks(self, got_first, got_second):
        to_x = self.part(self.x, True) + got_second.astype(F32)
        to_y = self.part(self.y, False) + got_first.astype(F32)
        return to_x.astype(BF16), to_y.astype(BF16)

    def near_blocks(self, got_first, got_second):
        first, second = self.first_blocks(), self.second_blocks(got_first, got_second)
        return jnp.concatenate([first[0], second[0]]), jnp.concatenate([second[1], first[1]])

    def near_total(self, got_x, got_y):
        return self.part(self.here) + got_x.astype(F32) + got_y.astype(F32)

    def total(self, first, second):
        upper = self.part(self.here, False) + first[0].astype(F32) + second[1].astype(F32)
        lower = self.part(self.here, True) + second[0].astype(F32) + first[1].astype(F32)
        return jnp.concatenate([upper, lower], axis=0)


def send_xy(blocks):
    return swap(blocks[0], "ga"), swap(blocks[1], "gb")


def plane_scatter(g):
    if not square():
        return lax.psum_scatter(g, PLANE, scatter_dimension=0).astype(F32)
    c = lax.axis_index("gc")
    g = g.reshape((4, 2) + g.shape[1:])
    keep = lax.dynamic_index_in_dim(g, c, 1, keepdims=False)
    received = swap(lax.dynamic_index_in_dim(g, 1 - c, 1, keepdims=False), "gc")
    work = Scatter(keep, received)
    second = work.second_blocks(*send_xy(work.far_blocks()))
    return work.total(send_xy(work.first_blocks()), send_xy(second))


GELU_A = 0.7978845608028654
GELU_B = 0.044715


def row_scale(values):
    return lax.rsqrt(jnp.mean(values * values, axis=-1, keepdims=True) + EPSILON)


def full(x):
    return pl.BlockSpec(x.shape, lambda *_: (0,) * len(x.shape))


def like(shape, dtype=F32):
    return jax.ShapeDtypeStruct(shape, dtype)


def prefetch_call(kernel, scalars, grid, ins, in_specs, outs, out_specs, scratch=(), mib=48, us=3):
    return pl.pallas_call(
        kernel,
        grid_spec=pltpu.PrefetchScalarGridSpec(
            num_scalar_prefetch=1,
            grid=grid,
            in_specs=in_specs,
            out_specs=out_specs,
            scratch_shapes=scratch,
        ),
        out_shape=outs,
        compiler_params=params(mib),
        cost_estimate=cost(us),
    )(scalars, *ins)


def flags_kernel(parents, spot):
    segments = parents.shape[0]

    def kernel(parents_ref, spot_ref, out):
        def parent_of(segment):
            found = parents_ref[jnp.maximum(segment, 0)]
            return jnp.where(segment >= 0, found, -1)

        column, plane = spot_ref[0], spot_ref[1]
        first = 4 * column
        own = first + plane

        def later(distance):
            return parent_of(jnp.minimum(own + 4 * distance, segments - 1))

        def local(segment):
            return jnp.clip(segment - first, 0, 3)

        role = lax.rem(column, 4)
        a, a1, a2 = parent_of(own), later(1), later(2)
        b, b1, b2 = parent_of(a), parent_of(a1), parent_of(a2)
        made = [
            role,
            plane,
            local(a),
            local(b),
            (a >= 0).astype(jnp.int32),
            (b >= 0).astype(jnp.int32),
            local(a1),
            local(jnp.where(role == 0, b2, a2)),
            local(b1),
        ]
        for i in range(4):
            segment, level = first + i, jnp.int32(0)
            for _ in range(5):
                segment = parent_of(segment)
                level = level + (segment >= 0).astype(jnp.int32)
            made.append(level)
        for i, value in enumerate(made):
            out[i] = value

    return pl.pallas_call(
        kernel,
        out_shape=like((13,), jnp.int32),
        in_specs=[whole(pltpu.SMEM)] * 2,
        out_specs=whole(pltpu.SMEM),
    )(parents, spot)


def key_value_kernel(flags, tokens, gain_in, wkv, gain_key, cos_table, sin_table):
    rows, width = tokens.shape
    head = wkv.shape[1] // 2
    half = head // 2

    def kernel(f, t_ref, gain_ref, w_ref, key_gain_ref, c_ref, s_ref, pairs, normed, raw, *sends):
        values = t_ref[...].astype(F32)
        low = (values * row_scale(values) * gain_ref[...]).astype(BF16)
        made = dot(low, w_ref[...])
        key = made[:, :head]
        scaled = key * row_scale(key) * key_gain_ref[...]
        pair = jnp.concatenate(
            [rotate(scaled, c_ref[...], s_ref[...]), made[:, head:]], axis=1
        ).astype(BF16)
        pairs[...] = pair
        for n in range(3):

            @pl.when(pl.program_id(0) == f[6 + n])
            def _(n=n):
                sends[n][...] = pair

        @pl.when(pl.program_id(0) == f[1])
        def _():
            normed[...] = low
            raw[...] = key

    def rows_of(x):
        return pl.BlockSpec((SEG, x), lambda i, p: (i, 0))

    return prefetch_call(
        kernel,
        flags,
        (rows // SEG,),
        (tokens, gain_in, wkv, gain_key, cos_table, sin_table),
        [rows_of(width), full(gain_in), full(wkv), full(gain_key), rows_of(half), rows_of(half)],
        [like((rows, 2 * head), BF16), like((SEG, width), BF16), like((SEG, head))]
        + [like((SEG, 2 * head), BF16)] * 3,
        [
            rows_of(2 * head),
            pl.BlockSpec((SEG, width), lambda i, p: (0, 0)),
            pl.BlockSpec((SEG, head), lambda i, p: (0, 0)),
        ]
        + [pl.BlockSpec((SEG, 2 * head), lambda i, p: (0, 0))] * 3,
        us=6,
    )


def query_kernel(plane, normed, wq, gain_query, cos_table, sin_table, head):
    width, total = wq.shape
    half = head // 2

    def kernel(plane_ref, n_ref, w_ref, gain_ref, c_ref, s_ref, query, raw):
        made = dot(n_ref[...], w_ref[...])
        raw[...] = made
        scaled = made * row_scale(made) * gain_ref[...]
        query[...] = rotate(scaled, c_ref[...], s_ref[...]).astype(BF16)

    by_head = pl.BlockSpec((SEG, head), lambda h, p: (0, h))
    table = pl.BlockSpec((SEG, half), lambda h, p: (p[0], 0))
    return prefetch_call(
        kernel,
        plane.reshape(1),
        (total // head,),
        (normed, wq, gain_query, cos_table, sin_table),
        [full(normed), pl.BlockSpec((width, head), lambda h, p: (0, h)), full(gain_query), table, table],
        [like((SEG, total), BF16), like((SEG, total))],
        [by_head, by_head],
        us=2.3,
    )


def visible_pairs(alive_a, alive_b):
    at_query = lax.broadcasted_iota(jnp.int32, (SEG, 3 * SEG), 0)
    spot = lax.broadcasted_iota(jnp.int32, (SEG, 3 * SEG), 1)
    own = (spot < SEG) & (spot <= at_query)
    above = (spot >= SEG) & (spot < 2 * SEG) & (alive_a > 0)
    top = (spot - 2 * SEG > at_query) & (alive_b > 0)
    return own | above | top


def softmax_of(query, keys, scale, alive_a, alive_b):
    scores = dot(query, keys, (1, 1)) * scale
    scores = jnp.where(visible_pairs(alive_a, alive_b), scores, MASKED)
    weights = jnp.exp(scores - jnp.max(scores, axis=-1, keepdims=True))
    return weights / jnp.sum(weights, axis=-1, keepdims=True)


def attention_kernel(flags, query, pairs, got_1, got_2, got_3):
    total = query.shape[1]
    head = pairs.shape[1] // 2

    def kernel(f, q_ref, pairs_ref, g1, g2, g3, heads, slots):
        @pl.when(pl.program_id(0) == 0)
        def _():
            role = f[0]

            def near(n):
                return pairs_ref[pl.ds(pl.multiple_of(n * SEG, SEG), SEG), :]

            slots[:SEG] = near(f[1])

            @pl.when(role == 0)
            def _():
                slots[SEG : 2 * SEG] = near(f[2])
                slots[2 * SEG :] = near(f[3])

            @pl.when(role == 1)
            def _():
                slots[SEG : 2 * SEG] = g1[...]
                slots[2 * SEG :] = g3[...]

            @pl.when(role == 2)
            def _():
                slots[SEG : 2 * SEG] = g1[...]
                slots[2 * SEG :] = g2[...]

            @pl.when(role == 3)
            def _():
                slots[SEG : 2 * SEG] = g2[...]
                slots[2 * SEG :] = g3[...]

        probs = softmax_of(q_ref[...], slots[:, :head], head**-0.5, f[4], f[5])
        heads[...] = dot(probs.astype(BF16), slots[:, head:]).astype(BF16)

    by_head = pl.BlockSpec((SEG, head), lambda h, f: (0, h))
    ins = (query, pairs, got_1, got_2, got_3)
    return prefetch_call(
        kernel,
        flags,
        (total // head,),
        ins,
        [by_head] + [full(x) for x in ins[1:]],
        [like((SEG, total), BF16), like((3 * SEG, 2 * head), BF16)],
        [by_head, pl.BlockSpec((3 * SEG, 2 * head), lambda h, f: (0, 0))],
        us=5.4,
    )


def middle_kernel(plane, heads_own, heads_got, wo_t, tokens, gain_post, gain_ffn):
    width, total = wo_t.shape

    def kernel(p, own, got, w_ref, t_ref, post_ref, gain_ref, attn, mid, normed):
        i = pl.program_id(0)

        def run(heads):
            made = dot(heads[...], w_ref[...], (1, 1))

            @pl.when(i == 0)
            def _():
                attn[...] = made

            middle = t_ref[...].astype(F32) + made * row_scale(made) * post_ref[...]
            mid[...] = middle
            normed[...] = (middle * row_scale(middle) * gain_ref[...]).astype(BF16)

        pl.when(i == 0)(lambda: run(own))
        pl.when(i == 1)(lambda: run(got))

    rows = pl.BlockSpec((SEG, width), lambda i, p: (i, 0))
    return prefetch_call(
        kernel,
        plane.reshape(1),
        (2,),
        (heads_own, heads_got, wo_t, tokens, gain_post, gain_ffn),
        [
            full(heads_own),
            full(heads_got),
            full(wo_t),
            pl.BlockSpec((SEG, width), lambda i, p: (p[0] ^ i, 0)),
            full(gain_post),
            full(gain_ffn),
        ],
        [like((SEG, width)), like((2 * SEG, width)), like((2 * SEG, width), BF16)],
        [pl.BlockSpec((SEG, width), lambda i, p: (0, 0)), rows, rows],
        us=4.5,
    )


def both_cores(pieces):
    return pieces + [(swap(piece, "gc"), row, slot + 1) for piece, row, slot in pieces]


class Blocks:
    def __init__(self, pieces, block):
        self.jobs = []
        if block is None:
            self.pieces = tuple(pieces)
            self.width, self.units = pieces[0].shape
            self.slots = jnp.zeros((1,), jnp.int32)
            self.jobs = [(m, 0, m, 0, self.width, None) for m in range(3)]
            return
        self.pieces = tuple(piece for piece, _, _ in pieces)
        self.units = self.pieces[0].shape[1]
        self.width = 8 * block
        here = lax.axis_index(PLANE)
        self.slots = jnp.array([slot for _, _, slot in pieces], jnp.int32)
        self.slots = (self.slots ^ here) * block
        for i, (piece, start, _) in enumerate(pieces):
            for m in range(3):
                low, high = max(start, m * block), min(start + piece.shape[0], (m + 1) * block)
                if low < high:
                    self.jobs.append((i, low - start, m, low - m * block, high - low, i))

    @classmethod
    def collected(cls, own, other, block):
        made = cls([(own, 0, 0), (other, 0, 1)], block)
        here = lax.axis_index(PLANE)
        made.slots = chip_slots() * block
        made.jobs = [
            (i, (3 * chip + m) * block, m, 0, block, 4 * i + chip)
            for i in range(2)
            for chip in range(4)
            for m in range(3)
        ]
        return made

    def scratch(self):
        return [
            pltpu.VMEM((3, self.width, self.units), BF16),
            pltpu.SemaphoreType.DMA((len(self.jobs),)),
        ]

    def copies(self, slots, refs, held, sems, matrix):
        made = []
        for n, (i, source, m, to, rows, slot) in enumerate(self.jobs):
            if m == matrix:
                base = 0 if slot is None else pl.multiple_of(slots[slot], 16)
                made.append(
                    pltpu.make_async_copy(
                        refs[i].at[pl.ds(source, rows)],
                        held.at[m, pl.ds(base + to, rows)],
                        sems.at[n],
                    )
                )
        return made


def ffn_forward_kernel(blocks, normed, part):
    rows, width = normed.shape
    units = blocks.units
    count = len(blocks.pieces)
    first = part is None

    def kernel(slots, n_ref, *refs):
        if not first:
            part_ref, refs = refs[0], refs[1:]
        pieces, (act, slope, hidden, out, held, sems) = refs[:count], refs[count:]
        start = pl.program_id(0) == 0

        def wait(m):
            @pl.when(start)
            def _():
                for copy in blocks.copies(slots, pieces, held, sems, m):
                    copy.wait()

        @pl.when(start)
        def _():
            for m in range(3):
                for copy in blocks.copies(slots, pieces, held, sems, m):
                    copy.start()

        left = n_ref[...]
        wait(0)
        gate = dot(left, held[0])
        wait(1)
        up = dot(left, held[1])
        square_gate = gate * gate
        turn = jnp.tanh(GELU_A * (gate + GELU_B * gate * square_gate))
        spread = 0.5 * (1.0 + turn)
        gelu = gate * spread
        bend = spread + 0.5 * gate * (1.0 - turn * turn) * (
            GELU_A * (1.0 + 3.0 * GELU_B * square_gate)
        )
        act[...] = gelu.astype(BF16)
        slope[...] = (up * bend).astype(BF16)
        low = (gelu * up).astype(BF16)
        hidden[...] = low
        wait(2)
        made = dot(low, held[2], (1, 1))
        out[...] = made if first else part_ref[...] + made

    by_rows = pl.BlockSpec((SEG, width), lambda i, s: (i, 0))
    by_units = pl.BlockSpec((SEG, units), lambda i, s: (i, 0))
    return prefetch_call(
        kernel,
        blocks.slots,
        (rows // SEG,),
        (normed,) + (() if first else (part,)) + blocks.pieces,
        [by_rows] + ([] if first else [by_rows]) + [whole(pl.ANY)] * count,
        [like((rows, units), BF16)] * 3 + [like((rows, width))],
        [by_units] * 3 + [by_rows],
        blocks.scratch(),
        mib=58,
        us=16,
    )


def ffn_backward_kernel(blocks, d_ffn, act, slope, back):
    rows, width = d_ffn.shape
    units = blocks.units
    count = len(blocks.pieces)
    first = back is None

    def kernel(slots, d_ref, act_ref, slope_ref, *refs):
        if not first:
            back_ref, refs = refs[0], refs[1:]
        pieces, (d_gate, d_up, out, held, sems) = refs[:count], refs[count:]
        start = pl.program_id(0) == 0

        def wait(m):
            @pl.when(start)
            def _():
                for copy in blocks.copies(slots, pieces, held, sems, m):
                    copy.wait()

        @pl.when(start)
        def _():
            for m in (2, 0, 1):
                for copy in blocks.copies(slots, pieces, held, sems, m):
                    copy.start()

        wait(2)
        d_hidden = dot(d_ref[...], held[2])
        to_gate = (d_hidden * slope_ref[...].astype(F32)).astype(BF16)
        to_up = (d_hidden * act_ref[...].astype(F32)).astype(BF16)
        d_gate[...] = to_gate
        d_up[...] = to_up
        wait(0)
        wait(1)
        made = dot(to_gate, held[0], (1, 1)) + dot(to_up, held[1], (1, 1))
        out[...] = made if first else back_ref[...] + made

    by_rows = pl.BlockSpec((SEG, width), lambda i, s: (i, 0))
    by_units = pl.BlockSpec((SEG, units), lambda i, s: (i, 0))
    return prefetch_call(
        kernel,
        blocks.slots,
        (rows // SEG,),
        (d_ffn, act, slope) + (() if first else (back,)) + blocks.pieces,
        [by_rows, by_units, by_units] + ([] if first else [by_rows]) + [whole(pl.ANY)] * count,
        [like((rows, units), BF16)] * 2 + [like((rows, width))],
        [by_units] * 2 + [by_rows],
        blocks.scratch(),
        mib=58,
        us=16,
    )


def ffn_end_kernel(plane, ffn_own, ffn_other, mid, cotangent, gain):
    rows, width = mid.shape

    def kernel(p, own_ref, other_ref, mid_ref, up_ref, gain_ref, d_out, d_turned, out, share):
        i = pl.program_id(0)
        g = gain_ref[...]

        def run(ref, own):
            ffn = ref[...].astype(F32)
            r = row_scale(ffn)
            incoming = up_ref[...].astype(F32)
            out[...] = (mid_ref[...] + ffn * r * g).astype(BF16)
            if own:
                share[...] = jnp.sum(incoming * ffn * r, axis=0, keepdims=True)
            scaled = g * incoming
            inner = jnp.mean(ffn * scaled, axis=-1, keepdims=True)
            made = (r * scaled - ffn * (r * r * r) * inner).astype(BF16)
            d_out[...] = made
            d_turned[...] = made.T

        pl.when(i == 0)(lambda: run(own_ref, True))
        pl.when(i == 1)(lambda: run(other_ref, False))

    once = pl.BlockSpec((SEG, width), lambda i, p: (0, 0))
    by_rows = pl.BlockSpec((SEG, width), lambda i, p: (i, 0))
    return prefetch_call(
        kernel,
        plane.reshape(1),
        (2,),
        (ffn_own, ffn_other, mid, cotangent, gain),
        [once, once, by_rows, pl.BlockSpec((SEG, width), lambda i, p: (p[0] ^ i, 0)), full(gain)],
        [like((rows, width), BF16), like((width, rows), BF16), like((rows, width), BF16), like((1, width))],
        [
            by_rows,
            pl.BlockSpec((width, SEG), lambda i, p: (0, i)),
            by_rows,
            pl.BlockSpec((1, width), lambda i, p: (0, 0)),
        ],
        us=3.4,
    )


def spread_kernel(plane, blocks, order, dtype):
    width = blocks[0].shape[1]
    count = len(blocks)
    spots = [(n, r) for n, x in enumerate(blocks) for r in range(x.shape[0] // SEG)]

    def kernel(p, *refs):
        ins, out = refs[:count], refs[count]
        for i, (n, r) in enumerate(spots):

            @pl.when(pl.program_id(0) == p[0] ^ order[i])
            def _(n=n, r=r):
                out[...] = ins[n][r * SEG : (r + 1) * SEG].astype(dtype)

    return prefetch_call(
        kernel,
        plane.reshape(1),
        (4,),
        tuple(blocks),
        [full(x) for x in blocks],
        like((4 * SEG, width), dtype),
        pl.BlockSpec((SEG, width), lambda i, p: (i, 0)),
        us=3,
    )


def attention_back_kernel(
    flags, back, got, mid, cotangent, gain_ffn, attn, gain_post, wo_t, query, query_raw, gain_query,
    slots, cos_table, sin_table, head,
):
    width, total = wo_t.shape
    heads = total // head
    half = head // 2
    scale = head**-0.5

    def kernel(
        f, back_ref, got_ref, mid_ref, up_ref, gain_ffn_ref, attn_ref, gain_post_ref, w_ref, q_ref,
        raw_ref, gain_query_ref, slots_ref, c_ref, s_ref,
        d_mid, d_attn, d_attn_turned, shares, d_query, query_share, d_self, d_a, d_b, sums,
    ):
        h = pl.program_id(0)

        @pl.when(h == 0)
        def _():
            incoming = back_ref[...] + got_ref[...].astype(F32)
            add, share = norm_back(mid_ref[...], gain_ffn_ref[...], incoming)
            made = up_ref[...].astype(F32) + add
            d_mid[...] = made
            d_a_low, share_post = norm_back(attn_ref[...], gain_post_ref[...], made)
            low = d_a_low.astype(BF16)
            d_attn[...] = low
            d_attn_turned[...] = low.T
            shares[0:1, :] = jnp.sum(share, axis=0, keepdims=True)
            shares[1:2, :] = jnp.sum(share_post, axis=0, keepdims=True)
            sums[...] = jnp.zeros_like(sums)
            query_share[...] = jnp.zeros_like(query_share)

        keys, values = slots_ref[:, :head], slots_ref[:, head:]
        q = q_ref[...]
        d_heads = dot(d_attn[...], w_ref[...]).astype(BF16)
        probs = softmax_of(q, keys, scale, f[4], f[5])
        d_probs = dot(d_heads, values, (1, 1))
        d_scores = probs * (d_probs - jnp.sum(d_probs * probs, axis=-1, keepdims=True))
        d_scores = d_scores.astype(BF16)
        sums[:, :head] += dot(d_scores, q, (0, 0))
        sums[:, head:] += dot(probs.astype(BF16), d_heads, (0, 0))
        turned = rotate(dot(d_scores, keys) * scale, c_ref[...], -s_ref[...])
        made, share = norm_back(raw_ref[...], gain_query_ref[...], turned)
        d_query[...] = made.astype(BF16)
        query_share[...] += jnp.sum(share, axis=0, keepdims=True)

        @pl.when(h == heads - 1)
        def _():
            sums[:, :head] = sums[:, :head] * scale
            d_self[...] = sums[:SEG]
            d_a[...] = sums[SEG : 2 * SEG].astype(BF16)
            d_b[...] = sums[2 * SEG :].astype(BF16)

    def once(shape):
        return pl.BlockSpec(shape, lambda h, f: (0,) * len(shape))

    by_head = pl.BlockSpec((SEG, head), lambda h, f: (0, h))
    table = pl.BlockSpec((SEG, half), lambda h, f: (f[1], 0))
    rows = once((SEG, width))
    return prefetch_call(
        kernel,
        flags,
        (heads,),
        (back, got, mid, cotangent, gain_ffn, attn, gain_post, wo_t, query, query_raw, gain_query,
         slots, cos_table, sin_table),
        [
            rows,
            rows,
            rows,
            pl.BlockSpec((SEG, width), lambda h, f: (f[1], 0)),
            full(gain_ffn),
            rows,
            full(gain_post),
            pl.BlockSpec((width, head), lambda h, f: (0, h)),
            by_head,
            by_head,
            full(gain_query),
            full(slots),
            table,
            table,
        ],
        [
            like((SEG, width)),
            like((SEG, width), BF16),
            like((width, SEG), BF16),
            like((2, width)),
            like((SEG, total), BF16),
            like((1, head)),
            like((SEG, 2 * head)),
            like((SEG, 2 * head), BF16),
            like((SEG, 2 * head), BF16),
        ],
        [
            rows,
            rows,
            once((width, SEG)),
            once((2, width)),
            by_head,
            once((1, head)),
            once((SEG, 2 * head)),
            once((SEG, 2 * head)),
            once((SEG, 2 * head)),
        ],
        [pltpu.VMEM((3 * SEG, 2 * head), F32)],
        us=12,
    )


def tokens_back_kernel(
    plane, terms, key_raw, gain_key, cos_table, sin_table, wkv, d_normed, d_mid, tokens, gain_in
):
    width = d_mid.shape[1]
    head = key_raw.shape[1]
    half = head // 2
    count = len(terms)

    def kernel(p, *refs):
        terms_in, refs = refs[:count], refs[count:]
        (raw_ref, gain_ref, c_ref, s_ref, w_ref, dn_ref, mid_ref, t_ref, gain_in_ref) = refs[:9]
        d_kv, rows_out, share_key, share_in = refs[9:]
        total = terms_in[0][...].astype(F32)
        for term in terms_in[1:]:
            total = total + term[...].astype(F32)
        turned = rotate(total[:, :head], c_ref[...], -s_ref[...])
        made, share = norm_back(raw_ref[...], gain_ref[...], turned)
        share_key[...] = jnp.sum(share, axis=0, keepdims=True)
        low = jnp.concatenate([made, total[:, head:]], axis=1).astype(BF16)
        d_kv[...] = low
        incoming = dn_ref[...] + dot(low, w_ref[...], (1, 1))
        add, share = norm_back(t_ref[...].astype(F32), gain_in_ref[...], incoming)
        share_in[...] = jnp.sum(share, axis=0, keepdims=True)
        rows_out[...] = (mid_ref[...] + add).astype(BF16)

    table = pl.BlockSpec((SEG, half), lambda i, p: (p[0], 0))
    ins = (*terms, key_raw, gain_key, cos_table, sin_table, wkv, d_normed, d_mid, tokens, gain_in)
    specs = [full(x) for x in ins]
    specs[count + 2] = specs[count + 3] = table
    specs[count + 7] = pl.BlockSpec((SEG, width), lambda i, p: (p[0], 0))
    outs = [like((SEG, 2 * head), BF16), like((SEG, width), BF16), like((1, head)), like((1, width))]
    return prefetch_call(
        kernel, plane.reshape(1), (1,), ins, specs, outs, [full(o) for o in outs], us=3
    )


def window_kernel(flags, d_self, d_a, d_b, back_1, back_2, back_3):
    shape = (2,) + d_self.shape

    def kernel(f, own_ref, a_ref, b_ref, b1, b2, b3, sent, kept):
        role, plane = f[0], f[1]
        near = role == 0
        ats = [
            plane,
            jnp.where(near & (f[4] > 0), f[2], -1),
            jnp.where(near & (f[5] > 0), f[3], -1),
            jnp.where(role <= 1, f[6], -1),
            jnp.where(role <= 1, f[7], -1),
            jnp.where(near, f[8], -1),
        ]
        refs = (own_ref, a_ref, b_ref, b1, b2, b3)
        for out, k, other in ((sent, 0, 1), (sent, 1, 3), (kept, 0, 0), (kept, 1, 2)):
            number = plane ^ other
            total = jnp.zeros(out.shape[1:], F32)
            for at, ref in zip(ats, refs):
                total = total + jnp.where(at == number, ref[...].astype(F32), 0.0)
            out[k] = total.astype(BF16)

    return pl.pallas_call(
        kernel,
        out_shape=[like(shape, BF16)] * 2,
        in_specs=[whole(pltpu.SMEM)] + [whole(pltpu.VMEM)] * 6,
        out_specs=[whole(pltpu.VMEM)] * 2,
        compiler_params=params(58),
        cost_estimate=cost(2.4),
    )(flags, d_self, d_a, d_b, back_1, back_2, back_3)


def z_first(sent, kept, kept_far):
    got = across(sent, 1).astype(F32)
    return tie((kept.astype(F32) + got[0]).astype(BF16), (kept_far.astype(F32) + got[1]).astype(BF16))


def z_halve(x):
    here = lax.axis_index("gx")

    def at(n):
        return lax.dynamic_index_in_dim(x, n, 0, keepdims=False)

    return z_first(jnp.stack([at(here ^ 1), at(here ^ 3)]), at(here), at(here ^ 2))


def body(
    tokens,
    parents,
    w_query,
    w_key,
    w_value,
    w_out,
    w_gate,
    w_up,
    w_down,
    g_attn_in,
    g_attn_out,
    g_ffn_in,
    g_ffn_out,
    g_query,
    g_key,
    cotangent,
):
    column = lax.axis_index(PLANE)
    columns = lax.axis_size(PLANE)
    plane = lax.axis_index("gx")
    planes = lax.axis_size("gx")
    width = tokens.shape[1]
    head_width = w_key.shape[1]
    heads = planes * w_query.shape[1] // head_width
    block, small = w_query.shape[0], w_key.shape[0]
    gains_len = 4 * block + 2 * g_query.shape[0]
    pack_width = 2 * head_width
    gain_rows = -(-gains_len // pack_width)
    used = small + gain_rows
    gain_spot = -(-small // 8) * 8
    pack_rows = -(-(block + gain_spot + gain_rows) // 16) * 16

    core = lax.axis_index("gc")
    down_t = w_down.T
    ffn_mine = jnp.concatenate([w_gate, w_up, down_t], axis=0)
    gains = jnp.concatenate([g_attn_in, g_attn_out, g_ffn_in, g_ffn_out, g_query, g_key])
    gains = jnp.pad(gains, (0, gain_rows * pack_width - gains_len)).reshape(gain_rows, pack_width)
    pack = jnp.concatenate(
        [
            jnp.concatenate([w_query, w_out.T], axis=1),
            jnp.concatenate([w_key, w_value], axis=1),
            jnp.zeros((gain_spot - small, pack_width), BF16),
            gains,
            jnp.zeros((pack_rows - block - gain_spot - gain_rows, pack_width), BF16),
        ],
        axis=0,
    )
    flags = flags_kernel(parents, jnp.stack([column, plane]).astype(jnp.int32))
    depth = flags[9:13, None] * SEG + jnp.arange(SEG, dtype=jnp.int32)[None, :]
    half_width = head_width // 2
    rates = 10000.0 ** (-jnp.arange(half_width, dtype=F32) / half_width)
    turned = depth.reshape(-1).astype(F32)[:, None] * rates[None, :]
    cos_table, sin_table = jnp.cos(turned), jnp.sin(turned)
    if square():
        ffn_x, ffn_y = send_near(ffn_mine)
        pack = lax.all_gather(pack, "gx", axis=0)
        pack, other_gu = tie(pack, ffn_mine[: 2 * block])
        their_gu = across(other_gu, 2)
        pack_x, pack_y = send_near(pack)
        ffn_x, ffn_y, pack, pack_x, pack_y, cos_table, sin_table = tie(
            ffn_x, ffn_y, pack, pack_x, pack_y, cos_table, sin_table
        )
        pack_far = send_far(pack_x, pack_y)
        ffn_far = send_far(ffn_x, ffn_y)
        *pack_far, their_gu, other_down = tie(*pack_far, their_gu, down_t)
        their_down = across(other_down, 2)
        pack_all = collect((pack, pack_x, pack_y, *pack_far), planes)
        pack_other = swap(pack_all, "gc")
        wq, wo_t, wkv, gains = unpack(
            [pack_all, pack_other], block, head_width, gain_spot, gain_rows
        )
    else:
        pack = lax.all_gather(pack, "gx", axis=0, tiled=True)
        pack = lax.all_gather(pack, PLANE, axis=0).reshape(columns, planes, pack_rows, pack_width)

        def from_blocks(blocks):
            return blocks.transpose(0, 2, 1, 3).reshape(columns * block, -1)

        wq = from_blocks(pack[:, :, :block, :head_width])
        wo_t = from_blocks(pack[:, :, :block, head_width:])
        wkv = pack[:, :, block : block + small].transpose(1, 0, 2, 3).reshape(width, pack_width)
        gains = pack[:, 0, block + gain_spot : block + gain_spot + gain_rows]

        def ffn_weights(mine):
            stacked = lax.all_gather(mine, PLANE, axis=0).reshape(columns, 3, block, -1)
            return Blocks([stacked[:, i].reshape(width, -1) for i in range(3)], None)

        quarter_mine = ffn_weights(ffn_mine)
        quarter_theirs = ffn_weights(across(ffn_mine, 2))

    gains = gains.reshape(columns, -1)[:, :gains_len].astype(F32)
    gain_in, gain_post, gain_ffn, gain_last = [
        gains[:, i * block : (i + 1) * block].reshape(1, -1) for i in range(4)
    ]
    gain_query, gain_key = [
        gains[:, 4 * block + i * g_query.shape[0] :][:, : g_query.shape[0]].reshape(1, -1)
        for i in range(2)
    ]

    role = column % 4
    trees = range(columns // 4)
    route_1 = [(4 * t + i, 4 * t + i + 1) for t in trees for i in (0, 1)]
    route_2 = [(4 * t + i, 4 * t + i + 2) for t in trees for i in (0, 1)]
    route_3 = [(4 * t + i, 4 * t + i + 1) for t in trees for i in (0, 2)]

    def send(x, route):
        return lax.ppermute(x, PLANE, route)

    def send_back(x, route):
        return lax.ppermute(x, PLANE, [(b, a) for a, b in route])

    pairs, normed_own, key_raw, send_1, send_2, send_3 = key_value_kernel(
        flags, tokens, gain_in, wkv, gain_key, cos_table, sin_table
    )
    if square():
        send_1, send_2 = tie(send_1, send_2)
    got_1 = send(send_1, route_1)
    got_2 = send(send_2, route_2)
    query, query_raw = query_kernel(
        plane, normed_own, wq, gain_query, cos_table, sin_table, head_width
    )
    if square():
        query, ffn_x, ffn_y, their_down, *ffn_far = tie(query, ffn_x, ffn_y, their_down, *ffn_far)
        theirs = jnp.concatenate([their_gu, their_down], axis=0)
        mine_all = collect((ffn_mine, ffn_x, ffn_y, *ffn_far), 3 * block)
        got_1, got_2, mine_all, theirs = tie(got_1, got_2, mine_all, theirs)
        mine_other = swap(mine_all, "gc")
        their_x, their_y = send_near(theirs)
    got_3 = send(jnp.where(role == 2, got_2, send_3), route_3)
    heads_low, slots = attention_kernel(flags, query, pairs, got_1, got_2, got_3)

    if square():
        heads_low, mine_other = tie(heads_low, mine_other)
        heads_got = across(heads_low, 1)
        quarter_mine = Blocks.collected(mine_all, mine_other, block)
    else:
        heads_got = across(heads_low, 1)
    attn, mid, normed_ffn = middle_kernel(
        plane, heads_low, heads_got, wo_t, tokens, gain_post, gain_ffn
    )
    if square():
        normed_ffn, their_x, their_y = tie(normed_ffn, their_x, their_y)
        their_far = send_far(their_x, their_y)
        near_pieces = both_cores([(theirs, 0, 0), (their_x, 0, 2), (their_y, 0, 4)])
    act_m, slope_m, hidden_m, ffn_part = ffn_forward_kernel(quarter_mine, normed_ffn, None)
    if square():
        ffn_part, *their_far = tie(ffn_part, *their_far)
        far_pieces = both_cores([(their_far[0], 0, 6), (their_far[1], their_far[0].shape[0], 6)])
        quarter_theirs = Blocks(near_pieces + far_pieces, block)
    act_t, slope_t, hidden_t, ffn_part = ffn_forward_kernel(quarter_theirs, normed_ffn, ffn_part)
    ffn_got = across(ffn_part[SEG:].astype(BF16), 1)
    ffn_own = (ffn_part[:SEG] + ffn_got.astype(F32)).astype(BF16)
    ffn_other = across(ffn_own, 1)
    d_ffn_low, d_ffn_t, output, d_gain_last = ffn_end_kernel(
        plane, ffn_own, ffn_other, mid, cotangent, gain_last
    )

    output_far = [across(output[:SEG], 2)]
    d_gate_t, d_up_t, back = ffn_backward_kernel(quarter_theirs, d_ffn_low, act_t, slope_t, None)
    if square():
        lefts = (normed_ffn.T, d_ffn_t)
        send_theirs = ffn_weight_grads(1 - core, *lefts, d_gate_t, d_up_t, hidden_t, block)
        keep_theirs = ffn_weight_grads(core, *lefts, d_gate_t, d_up_t, hidden_t, block)
        back, send_theirs, keep_theirs, output_far[0] = tie(
            back, send_theirs, keep_theirs, output_far[0]
        )
        recv_theirs = swap(send_theirs, "gc")
    d_gate_m, d_up_m, back = ffn_backward_kernel(quarter_mine, d_ffn_low, act_m, slope_m, back)
    if square():
        back, recv_theirs = tie(back, recv_theirs)
        theirs = Scatter(keep_theirs, recv_theirs)
    back_got = across(back[SEG:].astype(BF16), 1)
    if square():
        theirs_far = send_xy(theirs.far_blocks())
        theirs_first = send_xy(theirs.first_blocks())
        back_got, output = tie(back_got, output)
    else:
        grads = []
        for d_gate, d_up, hidden in ((d_gate_m, d_up_m, hidden_m), (d_gate_t, d_up_t, hidden_t)):
            blocks = [
                dot(normed_ffn, d_gate, (0, 0)),
                dot(normed_ffn, d_up, (0, 0)),
                dot(d_ffn_low, hidden, (0, 0)),
            ]
            blocks = [m.astype(BF16).reshape(columns, block, -1) for m in blocks]
            grads.append(plane_scatter(jnp.concatenate(blocks, axis=1)))
        ffn_grad = grads[0] + across(grads[1].astype(BF16), 2).astype(F32)

    output_far.append(across(output[SEG : SEG + SEG // 2], 2))

    (
        d_mid, d_attn_low, d_attn_t, d_gains_mid, d_query_low, d_gain_query, d_self, d_a, d_b,
    ) = attention_back_kernel(
        flags, back, back_got, mid, cotangent, gain_ffn, attn, gain_post, wo_t, query, query_raw,
        gain_query, slots, cos_table, sin_table, head_width,
    )
    if square():
        d_a, d_b, output_far[1], output, d_gate_m = tie(
            d_a, d_b, output_far[1], output, d_gate_m
        )
    output_far.append(across(output[SEG + SEG // 2 :], 2))
    back_1 = send_back(d_a, route_1)
    back_3 = send_back(d_b, route_3)
    if square():
        theirs_second = theirs.second_blocks(*theirs_far)
        made = (*lefts, d_gate_m, d_up_m, hidden_m)
        send_mine = ffn_weight_grads(1 - core, *made, block)
        d_a, d_b, back_1, back_3, send_mine, d_gate_m, *flat = tie(
            d_a, d_b, back_1, back_3, send_mine, d_gate_m, *theirs_first, *theirs_second
        )
        theirs_first, theirs_second = flat[:2], flat[2:]
    d_b_far = jnp.where(role == 2, d_b.astype(F32) + back_3.astype(F32), 0.0).astype(BF16)
    to_back_2 = jnp.where(role == 3, d_a, d_b_far)
    back_2 = send_back(to_back_2, route_2)
    if square():
        theirs_second = send_xy(theirs_second)
        keep_mine = ffn_weight_grads(core, *lefts, d_gate_m, d_up_m, hidden_m, block)
        back_2, output_far[2], keep_mine, send_mine = tie(
            back_2, output_far[2], keep_mine, send_mine
        )
        recv_mine = swap(send_mine, "gc")
    sent, kept = window_kernel(flags, d_self, d_a, d_b, back_1, back_2, back_3)
    kept, passed = z_first(sent, kept[0], kept[1])
    if square():
        passed, d_query_low, keep_mine, recv_mine = tie(
            passed, d_query_low, keep_mine, recv_mine
        )
    d_normed_query = dot(d_query_low, wq, (1, 1))
    own_terms = [kept, across(passed, 2)]
    if square():
        mine = Scatter(keep_mine, recv_mine)
        mine_far = mine.far_blocks()
        theirs_sum = theirs.total(theirs_first, theirs_second).astype(BF16)
        own_terms[1], theirs_sum, d_normed_query, d_gains_mid, d_gain_last, d_gain_query, *mine_far = tie(
            own_terms[1], theirs_sum, d_normed_query, d_gains_mid, d_gain_last, d_gain_query, *mine_far
        )
        mine_far = send_xy(mine_far)
    d_kv_low, token_rows, d_gain_key, d_gain_in = tokens_back_kernel(
        plane, own_terms, key_raw, gain_key, cos_table, sin_table, wkv, d_normed_query, d_mid,
        tokens, gain_in,
    )
    tokens_far = across(token_rows, 2)

    grad_kv = dot(normed_own, d_kv_low, (0, 0)).astype(BF16)
    grad_kv = grad_kv.reshape(planes, columns, small, -1).transpose(1, 0, 2, 3)
    gain_sums = [
        d_gain_in,
        d_gains_mid[1:],
        d_gains_mid[:1],
        d_gain_last,
        d_gain_query,
        d_gain_key,
    ]
    gain_sums = jnp.concatenate([g.reshape(columns, -1) for g in gain_sums], axis=1).astype(BF16)
    gain_sums = jnp.pad(gain_sums, ((0, 0), (0, gain_rows * pack_width - gains_len)))
    gain_sums = jnp.broadcast_to(
        gain_sums.reshape(columns, 1, gain_rows, pack_width),
        (columns, planes, gain_rows, pack_width),
    )
    rest_rows = pack_rows - block
    rest = jnp.concatenate(
        [grad_kv, gain_sums, jnp.zeros((columns, planes, pack_rows - block - used, pack_width), BF16)],
        axis=2,
    ).reshape(columns, planes * rest_rows, pack_width)
    if square():
        attn_lefts = (normed_own.T, d_query_low, d_attn_t, heads_low, rest)
        attn_send = attention_weight_grads(1 - core, *attn_lefts, block, planes)
        attn_keep = attention_weight_grads(core, *attn_lefts, block, planes)
        attn_received = swap(attn_send, "gc")
        attn_keep, attn_received = tie(attn_keep, attn_received)
        attn_work = Scatter(attn_keep, attn_received)
        attn_far = send_xy(attn_work.far_blocks())
        tokens_far, theirs_sum, *flat = tie(tokens_far, theirs_sum, *attn_far, *mine_far)
        attn_far, mine_far = flat[:2], flat[2:]
        attn_near = send_xy(attn_work.near_blocks(*attn_far))
        tokens_near = across(jnp.concatenate([token_rows, tokens_far], axis=0), 1)
        gate_sum = across(theirs_sum[:block], 2)
        mine_second = mine.second_blocks(*mine_far)
        gate_sum, tokens_near, other_up, *flat = tie(
            gate_sum, tokens_near, theirs_sum[block : 2 * block], *attn_near, *mine_second
        )
        up_sum = across(other_up, 2)
        mine_first = send_xy(mine.first_blocks())
        mine_second = flat[2:]
        grads = attn_work.near_total(*flat[:2])
    else:

        def to_blocks(grad):
            return grad.astype(BF16).reshape(columns, block, planes, -1).transpose(0, 2, 1, 3)

        grads = jnp.concatenate(
            [
                to_blocks(dot(normed_own, d_query_low, (0, 0))),
                to_blocks(dot(d_attn_low, heads_low, (0, 0))),
            ],
            axis=3,
        ).reshape(columns, planes * block, pack_width)
        grads = jnp.concatenate(
            [grads.reshape(columns, planes, block, -1), rest.reshape(columns, planes, rest_rows, -1)],
            axis=2,
        ).reshape(columns, planes * pack_rows, pack_width)
        grads = plane_scatter(grads)
    grads = grads.reshape(planes, pack_rows, pack_width)
    rest = jnp.broadcast_to(
        grads[:1, block + small :], (planes, pack_rows - block - small, pack_width)
    )
    grads = jnp.concatenate([grads[:, : block + small], rest], axis=1).astype(BF16)
    kept, passed = z_halve(grads)
    if square():
        passed, up_sum, other_down, *mine_second = tie(
            passed, up_sum, theirs_sum[2 * block :], *mine_second
        )
        mine_second = send_xy(mine_second)
        down_sum = across(other_down, 2)
    else:
        tokens_near = across(jnp.concatenate([token_rows, tokens_far], axis=0), 1)
    grads = kept.astype(F32) + across(passed, 2).astype(F32)
    if square():
        ffn_grad = mine.total(mine_first, mine_second) + jnp.concatenate(
            [gate_sum, up_sum, down_sum], axis=0
        ).astype(F32)
    grad_tokens = spread_kernel(plane, (token_rows, tokens_far, tokens_near), (0, 2, 1, 3), F32)
    output_far[1:] = [jnp.concatenate(output_far[1:], axis=0)]
    output = spread_kernel(plane, (output, *output_far), (0, 1, 2, 3), BF16)
    gain_grads = grads[block + small : block + used].reshape(-1)
    return (
        output,
        grad_tokens,
        gain_grads[:block],
        gain_grads[block : 2 * block],
        gain_grads[2 * block : 3 * block],
        gain_grads[3 * block : 4 * block],
        gain_grads[4 * block : 4 * block + g_query.shape[0]],
        gain_grads[4 * block + g_query.shape[0] : gains_len],
        grads[:block, :head_width],
        grads[block : block + small, :head_width],
        grads[block : block + small, head_width:],
        grads[:block, head_width:].T,
        ffn_grad[:block],
        ffn_grad[block : 2 * block],
        ffn_grad[2 * block :].T,
    )


def solution(mesh):
    side = math.isqrt(mesh.shape["gy"] // 2)
    split = Mesh(mesh.devices.reshape(mesh.shape["gx"], side, side, 2), ("gx",) + PLANE)
    whole = ("gx",) + PLANE
    return jax.shard_map(
        body,
        mesh=split,
        in_specs=(
            P(PLANE, None),
            P(),
            P(PLANE, "gx"),
            P(whole, None),
            P(whole, None),
            P("gx", PLANE),
            P(PLANE, "gx"),
            P(PLANE, "gx"),
            P("gx", PLANE),
            P(PLANE),
            P(PLANE),
            P(PLANE),
            P(PLANE),
            P(PLANE),
            P(PLANE),
            P(PLANE, None),
        ),
        out_specs=(
            P(PLANE, None),
            P(PLANE, None),
            P(PLANE),
            P(PLANE),
            P(PLANE),
            P(PLANE),
            P(PLANE),
            P(PLANE),
            P(PLANE, "gx"),
            P(whole, None),
            P(whole, None),
            P("gx", PLANE),
            P(PLANE, "gx"),
            P(PLANE, "gx"),
            P("gx", PLANE),
        ),
        check_vma=False,
    )
```

```python
import math

import jax
import jax.numpy as jnp
from jax import lax
from jax.experimental import pallas as pl
from jax.experimental.pallas import tpu as pltpu
from jax.sharding import Mesh
from jax.sharding import PartitionSpec as P

SEG = 256
EPSILON = 1e-06
MASKED = -1e30
PLANE = ("gb", "ga", "gc")
SWAP = [(0, 1), (1, 0)]
F32 = jnp.float32
BF16 = jnp.bfloat16


def rms_norm(values, gain):
    return values * lax.rsqrt(jnp.mean(values * values, axis=-1, keepdims=True) + EPSILON) * gain


def norm_back(values, gain, incoming):
    r = lax.rsqrt(jnp.mean(values * values, axis=-1, keepdims=True) + EPSILON)
    scaled = gain * incoming
    inner = jnp.mean(values * scaled, axis=-1, keepdims=True)
    return r * scaled - values * (r * r * r) * inner, incoming * values * r


def rotate(values, cos_table, sin_table):
    half_width = values.shape[-1] // 2
    a, b = values[..., :half_width], values[..., half_width:]
    return jnp.concatenate([a * cos_table - b * sin_table, b * cos_table + a * sin_table], axis=-1)


def dot(a, b, dims=(1, 0)):
    return lax.dot_general(
        a, b, (((dims[0],), (dims[1],)), ((), ())), preferred_element_type=F32
    )


def swap(x, axis):
    return lax.ppermute(x, axis, SWAP)


def across(x, distance):
    return lax.ppermute(x, "gx", [(i, i ^ distance) for i in range(4)])


def tie(*values):
    return lax.optimization_barrier(values)


def cost(microseconds):
    flops = int(microseconds * 1.0 * 1.15e9)
    return pl.CostEstimate(flops=flops, bytes_accessed=0, transcendentals=0)


def whole(array_or_space):
    return pl.BlockSpec(memory_space=array_or_space)


def params(mib):
    return pltpu.CompilerParams(vmem_limit_bytes=mib * 2**20)


def square():
    return lax.axis_size("ga") == 2


def halves(x):
    half = x.shape[0] // 32 * 16 or x.shape[0] // 2
    return x[:half], x[half:]


def send_near(x):
    return swap(x, "ga"), swap(x, "gb")


def send_far(from_x, from_y):
    return swap(halves(from_y)[0], "ga"), swap(halves(from_x)[1], "gb")


def collect(pieces, rows):
    count = len(pieces)
    starts = [0, rows, 2 * rows, 3 * rows, 3 * rows + pieces[3].shape[0]]
    shape = (4 * rows,) + pieces[0].shape[1:]

    def kernel(*refs):
        ins, (out, held, sems) = refs[:count], refs[count:]
        spots = [pl.ds(start, piece.shape[0]) for start, piece in zip(starts, pieces)]
        loads = [
            pltpu.make_async_copy(ref, held.at[spot], sems.at[0, i])
            for i, (ref, spot) in enumerate(zip(ins, spots))
        ]
        stores = [
            pltpu.make_async_copy(held.at[spot], out.at[spot], sems.at[1, i])
            for i, spot in enumerate(spots)
        ]
        for load in loads:
            load.start()
        for load, store in zip(loads, stores):
            load.wait()
            store.start()
        for store in stores:
            store.wait()

    return pl.pallas_call(
        kernel,
        out_shape=jax.ShapeDtypeStruct(shape, pieces[0].dtype),
        in_specs=[whole(pl.ANY)] * count,
        out_specs=whole(pl.ANY),
        scratch_shapes=[pltpu.VMEM(shape, pieces[0].dtype), pltpu.SemaphoreType.DMA((2, count))],
        compiler_params=params(24),
        cost_estimate=cost(4),
    )(*pieces)


def chip_slots():
    here = lax.axis_index(PLANE)
    return jnp.array([0, 2, 4, 6, 1, 3, 5, 7], jnp.int32) ^ here


def unpack(pieces, block, head_width, gain_spot, gain_rows):
    four, rows, width = pieces[0].shape
    planes = four // 4
    rest = rows - block
    small = block // planes
    count = len(pieces)
    jobs = [(i, 4 * chip + h, 4 * i + chip, h) for i in range(2) for chip in range(4) for h in range(planes)]

    def kernel(slot_ref, *refs):
        ins, (wq, wo, wkv, gains, other, sems) = refs[:count], refs[count:]
        copies = []
        for n, (i, j, at_slot, h) in enumerate(jobs):
            slot = slot_ref[at_slot]
            at = pl.ds(pl.multiple_of(slot * block, 16), block)
            to = pl.ds(h * head_width, head_width)
            parts = [
                (ins[i].at[j, pl.ds(0, block), pl.ds(0, head_width)], wq.at[at, to]),
                (ins[i].at[j, pl.ds(0, block), pl.ds(head_width, head_width)], wo.at[at, to]),
                (ins[i].at[j, pl.ds(block, rest), :], other.at[slot, h]),
            ]
            copies += [
                pltpu.make_async_copy(a, b, sems.at[n, m]) for m, (a, b) in enumerate(parts)
            ]
        for copy in copies:
            copy.start()
        for copy in copies:
            copy.wait()
        for c in range(8):
            gains[c] = other[c, 0, gain_spot : gain_spot + gain_rows, :]
        for h in range(planes):
            wkv[h * 8 * small : (h + 1) * 8 * small] = jnp.concatenate(
                [other[c, h, :small, :].astype(F32) for c in range(8)], axis=0
            ).astype(BF16)

    matrix = jax.ShapeDtypeStruct((8 * block, planes * head_width), BF16)
    return pl.pallas_call(
        kernel,
        out_shape=[
            matrix,
            matrix,
            jax.ShapeDtypeStruct((8 * block, width), BF16),
            jax.ShapeDtypeStruct((8, gain_rows, width), BF16),
        ],
        in_specs=[whole(pltpu.SMEM)] + [whole(pl.ANY)] * count,
        out_specs=[whole(pltpu.VMEM)] * 4,
        scratch_shapes=[
            pltpu.VMEM((8, planes, rest, width), BF16),
            pltpu.SemaphoreType.DMA((len(jobs), 3)),
        ],
        compiler_params=params(24),
        cost_estimate=cost(4.3),
    )(chip_slots(), *pieces)


def core_rows(ref, core, block):
    return jnp.concatenate(
        [ref[pl.ds(pl.multiple_of((2 * k + core) * block, 16), block), :] for k in range(4)],
        axis=0,
    )


def ffn_weight_grads(core, normed_t, d_ffn_t, d_gate, d_up, hidden, block):
    units = d_gate.shape[1]

    def kernel(core_ref, normed_ref, d_ffn_ref, gate_ref, up_ref, hidden_ref, out):
        m = pl.program_id(0)

        def run(left, right):
            rows = core_rows(left, core_ref[0], block)
            for n in range(0, units, 256):
                w = min(256, units - n)
                made = dot(rows, right[:, n : n + w]).astype(BF16)
                out[:, :, n : n + w] = made.reshape(4, block, w)

        for number, (left, right) in enumerate(
            ((normed_ref, gate_ref), (normed_ref, up_ref), (d_ffn_ref, hidden_ref))
        ):
            pl.when(m == number)(lambda left=left, right=right: run(left, right))

    def full(x):
        return pl.BlockSpec(x.shape, lambda m, c: (0, 0))

    ins = (normed_t, d_ffn_t, d_gate, d_up, hidden)
    return pl.pallas_call(
        kernel,
        grid_spec=pltpu.PrefetchScalarGridSpec(
            num_scalar_prefetch=1,
            grid=(3,),
            in_specs=[full(x) for x in ins],
            out_specs=pl.BlockSpec((4, block, units), lambda m, c: (0, m, 0)),
        ),
        out_shape=jax.ShapeDtypeStruct((4, 3 * block, units), BF16),
        compiler_params=params(48),
        cost_estimate=cost(6.7),
    )(core.reshape(1), *ins)


def attention_weight_grads(core, normed_t, d_query, d_attn_t, heads_low, other, block, planes):
    head_width = d_query.shape[1] // planes
    more = other.shape[1] // planes
    rows_all = block + more

    def kernel(core_ref, normed_ref, query_ref, d_attn_ref, heads_ref, other_ref, out):
        for half, (left, right) in enumerate(((normed_ref, query_ref), (d_attn_ref, heads_ref))):
            rows = core_rows(left, core_ref[0], block)
            for h in range(planes):
                made = dot(rows, right[:, h * head_width : (h + 1) * head_width]).astype(BF16)
                out[:, h * rows_all : h * rows_all + block, half * head_width : (half + 1) * head_width] = (
                    made.reshape(4, block, head_width)
                )
        for chip in range(4):
            for h in range(planes):
                out[chip, h * rows_all + block : (h + 1) * rows_all] = other_ref[
                    2 * chip + core_ref[0], h * more : (h + 1) * more
                ]

    return pl.pallas_call(
        kernel,
        out_shape=jax.ShapeDtypeStruct((4, planes * rows_all, 2 * head_width), BF16),
        in_specs=[whole(pltpu.SMEM)] + [whole(pltpu.VMEM)] * 5,
        out_specs=whole(pltpu.VMEM),
        compiler_params=params(32),
        cost_estimate=cost(2.5),
    )(core.reshape(1), normed_t, d_query, d_attn_t, heads_low, other)


class Scatter:
    def __init__(self, keep, received):
        y, x = lax.axis_index("gb"), lax.axis_index("ga")
        self.keep, self.received = keep, received
        self.here, self.x, self.y = 2 * y + x, 2 * y + 1 - x, 2 * (1 - y) + x
        self.far = 2 * (1 - y) + 1 - x
        self.half = keep.shape[1] // 32 * 16

    def part(self, chip, second=None):
        made = 0.0
        for values in (self.keep, self.received):
            block = lax.dynamic_index_in_dim(values, chip, 0, keepdims=False)
            if second is not None:
                block = block[self.half :] if second else block[: self.half]
            made = made + block.astype(F32)
        return made

    def far_blocks(self):
        return self.part(self.far, False).astype(BF16), self.part(self.far, True).astype(BF16)

    def first_blocks(self):
        return self.part(self.x, False).astype(BF16), self.part(self.y, True).astype(BF16)

    def second_blocks(self, got_first, got_second):
        to_x = self.part(self.x, True) + got_second.astype(F32)
        to_y = self.part(self.y, False) + got_first.astype(F32)
        return to_x.astype(BF16), to_y.astype(BF16)

    def near_blocks(self, got_first, got_second):
        first, second = self.first_blocks(), self.second_blocks(got_first, got_second)
        return jnp.concatenate([first[0], second[0]]), jnp.concatenate([second[1], first[1]])

    def near_total(self, got_x, got_y):
        return self.part(self.here) + got_x.astype(F32) + got_y.astype(F32)

    def total(self, first, second):
        upper = self.part(self.here, False) + first[0].astype(F32) + second[1].astype(F32)
        lower = self.part(self.here, True) + second[0].astype(F32) + first[1].astype(F32)
        return jnp.concatenate([upper, lower], axis=0)


def send_xy(blocks):
    return swap(blocks[0], "ga"), swap(blocks[1], "gb")


def plane_scatter(g):
    if not square():
        return lax.psum_scatter(g, PLANE, scatter_dimension=0).astype(F32)
    c = lax.axis_index("gc")
    g = g.reshape((4, 2) + g.shape[1:])
    keep = lax.dynamic_index_in_dim(g, c, 1, keepdims=False)
    received = swap(lax.dynamic_index_in_dim(g, 1 - c, 1, keepdims=False), "gc")
    work = Scatter(keep, received)
    second = work.second_blocks(*send_xy(work.far_blocks()))
    return work.total(send_xy(work.first_blocks()), send_xy(second))


GELU_A = 0.7978845608028654
GELU_B = 0.044715


def row_scale(values):
    return lax.rsqrt(jnp.mean(values * values, axis=-1, keepdims=True) + EPSILON)


def full(x):
    return pl.BlockSpec(x.shape, lambda *_: (0,) * len(x.shape))


def like(shape, dtype=F32):
    return jax.ShapeDtypeStruct(shape, dtype)


def prefetch_call(kernel, scalars, grid, ins, in_specs, outs, out_specs, scratch=(), mib=48, us=3):
    return pl.pallas_call(
        kernel,
        grid_spec=pltpu.PrefetchScalarGridSpec(
            num_scalar_prefetch=1,
            grid=grid,
            in_specs=in_specs,
            out_specs=out_specs,
            scratch_shapes=scratch,
        ),
        out_shape=outs,
        compiler_params=params(mib),
        cost_estimate=cost(us),
    )(scalars, *ins)


def flags_kernel(parents, spot):
    segments = parents.shape[0]

    def kernel(parents_ref, spot_ref, out):
        def parent_of(segment):
            found = parents_ref[jnp.maximum(segment, 0)]
            return jnp.where(segment >= 0, found, -1)

        column, plane = spot_ref[0], spot_ref[1]
        first = 4 * column
        own = first + plane

        def later(distance):
            return parent_of(jnp.minimum(own + 4 * distance, segments - 1))

        def local(segment):
            return jnp.clip(segment - first, 0, 3)

        role = lax.rem(column, 4)
        a, a1, a2 = parent_of(own), later(1), later(2)
        b, b1, b2 = parent_of(a), parent_of(a1), parent_of(a2)
        made = [
            role,
            plane,
            local(a),
            local(b),
            (a >= 0).astype(jnp.int32),
            (b >= 0).astype(jnp.int32),
            local(a1),
            local(jnp.where(role == 0, b2, a2)),
            local(b1),
        ]
        for i in range(4):
            segment, level = first + i, jnp.int32(0)
            for _ in range(5):
                segment = parent_of(segment)
                level = level + (segment >= 0).astype(jnp.int32)
            made.append(level)
        for i, value in enumerate(made):
            out[i] = value

    return pl.pallas_call(
        kernel,
        out_shape=like((13,), jnp.int32),
        in_specs=[whole(pltpu.SMEM)] * 2,
        out_specs=whole(pltpu.SMEM),
    )(parents, spot)


def key_value_kernel(flags, tokens, gain_in, wkv, gain_key, cos_table, sin_table):
    rows, width = tokens.shape
    head = wkv.shape[1] // 2
    half = head // 2

    def kernel(f, t_ref, gain_ref, w_ref, key_gain_ref, c_ref, s_ref, pairs, normed, raw, *sends):
        values = t_ref[...].astype(F32)
        low = (values * row_scale(values) * gain_ref[...]).astype(BF16)
        made = dot(low, w_ref[...])
        key = made[:, :head]
        scaled = key * row_scale(key) * key_gain_ref[...]
        pair = jnp.concatenate(
            [rotate(scaled, c_ref[...], s_ref[...]), made[:, head:]], axis=1
        ).astype(BF16)
        pairs[...] = pair
        for n in range(3):

            @pl.when(pl.program_id(0) == f[6 + n])
            def _(n=n):
                sends[n][...] = pair

        @pl.when(pl.program_id(0) == f[1])
        def _():
            normed[...] = low
            raw[...] = key

    def rows_of(x):
        return pl.BlockSpec((SEG, x), lambda i, p: (i, 0))

    return prefetch_call(
        kernel,
        flags,
        (rows // SEG,),
        (tokens, gain_in, wkv, gain_key, cos_table, sin_table),
        [rows_of(width), full(gain_in), full(wkv), full(gain_key), rows_of(half), rows_of(half)],
        [like((rows, 2 * head), BF16), like((SEG, width), BF16), like((SEG, head))]
        + [like((SEG, 2 * head), BF16)] * 3,
        [
            rows_of(2 * head),
            pl.BlockSpec((SEG, width), lambda i, p: (0, 0)),
            pl.BlockSpec((SEG, head), lambda i, p: (0, 0)),
        ]
        + [pl.BlockSpec((SEG, 2 * head), lambda i, p: (0, 0))] * 3,
        us=6,
    )


def query_kernel(plane, normed, wq, gain_query, cos_table, sin_table, head):
    width, total = wq.shape
    half = head // 2

    def kernel(plane_ref, n_ref, w_ref, gain_ref, c_ref, s_ref, query, raw):
        made = dot(n_ref[...], w_ref[...])
        raw[...] = made
        scaled = made * row_scale(made) * gain_ref[...]
        query[...] = rotate(scaled, c_ref[...], s_ref[...]).astype(BF16)

    by_head = pl.BlockSpec((SEG, head), lambda h, p: (0, h))
    table = pl.BlockSpec((SEG, half), lambda h, p: (p[0], 0))
    return prefetch_call(
        kernel,
        plane.reshape(1),
        (total // head,),
        (normed, wq, gain_query, cos_table, sin_table),
        [full(normed), pl.BlockSpec((width, head), lambda h, p: (0, h)), full(gain_query), table, table],
        [like((SEG, total), BF16), like((SEG, total))],
        [by_head, by_head],
        us=2.3,
    )


def visible_pairs(alive_a, alive_b):
    at_query = lax.broadcasted_iota(jnp.int32, (SEG, 3 * SEG), 0)
    spot = lax.broadcasted_iota(jnp.int32, (SEG, 3 * SEG), 1)
    own = (spot < SEG) & (spot <= at_query)
    above = (spot >= SEG) & (spot < 2 * SEG) & (alive_a > 0)
    top = (spot - 2 * SEG > at_query) & (alive_b > 0)
    return own | above | top


def softmax_of(query, keys, scale, alive_a, alive_b):
    scores = dot(query, keys, (1, 1)) * scale
    scores = jnp.where(visible_pairs(alive_a, alive_b), scores, MASKED)
    weights = jnp.exp(scores - jnp.max(scores, axis=-1, keepdims=True))
    return weights / jnp.sum(weights, axis=-1, keepdims=True)


def attention_kernel(flags, query, pairs, got_1, got_2, got_3):
    total = query.shape[1]
    head = pairs.shape[1] // 2

    def kernel(f, q_ref, pairs_ref, g1, g2, g3, heads, slots):
        @pl.when(pl.program_id(0) == 0)
        def _():
            role = f[0]

            def near(n):
                return pairs_ref[pl.ds(pl.multiple_of(n * SEG, SEG), SEG), :]

            slots[:SEG] = near(f[1])

            @pl.when(role == 0)
            def _():
                slots[SEG : 2 * SEG] = near(f[2])
                slots[2 * SEG :] = near(f[3])

            @pl.when(role == 1)
            def _():
                slots[SEG : 2 * SEG] = g1[...]
                slots[2 * SEG :] = g3[...]

            @pl.when(role == 2)
            def _():
                slots[SEG : 2 * SEG] = g1[...]
                slots[2 * SEG :] = g2[...]

            @pl.when(role == 3)
            def _():
                slots[SEG : 2 * SEG] = g2[...]
                slots[2 * SEG :] = g3[...]

        probs = softmax_of(q_ref[...], slots[:, :head], head**-0.5, f[4], f[5])
        heads[...] = dot(probs.astype(BF16), slots[:, head:]).astype(BF16)

    by_head = pl.BlockSpec((SEG, head), lambda h, f: (0, h))
    ins = (query, pairs, got_1, got_2, got_3)
    return prefetch_call(
        kernel,
        flags,
        (total // head,),
        ins,
        [by_head] + [full(x) for x in ins[1:]],
        [like((SEG, total), BF16), like((3 * SEG, 2 * head), BF16)],
        [by_head, pl.BlockSpec((3 * SEG, 2 * head), lambda h, f: (0, 0))],
        us=5.4,
    )


def middle_kernel(plane, heads_own, heads_got, wo_t, tokens, gain_post, gain_ffn):
    width, total = wo_t.shape

    def kernel(p, own, got, w_ref, t_ref, post_ref, gain_ref, attn, mid, normed):
        i = pl.program_id(0)

        def run(heads):
            made = dot(heads[...], w_ref[...], (1, 1))

            @pl.when(i == 0)
            def _():
                attn[...] = made

            middle = t_ref[...].astype(F32) + made * row_scale(made) * post_ref[...]
            mid[...] = middle
            normed[...] = (middle * row_scale(middle) * gain_ref[...]).astype(BF16)

        pl.when(i == 0)(lambda: run(own))
        pl.when(i == 1)(lambda: run(got))

    rows = pl.BlockSpec((SEG, width), lambda i, p: (i, 0))
    return prefetch_call(
        kernel,
        plane.reshape(1),
        (2,),
        (heads_own, heads_got, wo_t, tokens, gain_post, gain_ffn),
        [
            full(heads_own),
            full(heads_got),
            full(wo_t),
            pl.BlockSpec((SEG, width), lambda i, p: (p[0] ^ i, 0)),
            full(gain_post),
            full(gain_ffn),
        ],
        [like((SEG, width)), like((2 * SEG, width)), like((2 * SEG, width), BF16)],
        [pl.BlockSpec((SEG, width), lambda i, p: (0, 0)), rows, rows],
        us=4.5,
    )


def both_cores(pieces):
    return pieces + [(swap(piece, "gc"), row, slot + 1) for piece, row, slot in pieces]


class Blocks:
    def __init__(self, pieces, block):
        self.jobs = []
        if block is None:
            self.pieces = tuple(pieces)
            self.width, self.units = pieces[0].shape
            self.slots = jnp.zeros((1,), jnp.int32)
            self.jobs = [(m, 0, m, 0, self.width, None) for m in range(3)]
            return
        self.pieces = tuple(piece for piece, _, _ in pieces)
        self.units = self.pieces[0].shape[1]
        self.width = 8 * block
        here = lax.axis_index(PLANE)
        self.slots = jnp.array([slot for _, _, slot in pieces], jnp.int32)
        self.slots = (self.slots ^ here) * block
        for i, (piece, start, _) in enumerate(pieces):
            for m in range(3):
                low, high = max(start, m * block), min(start + piece.shape[0], (m + 1) * block)
                if low < high:
                    self.jobs.append((i, low - start, m, low - m * block, high - low, i))

    @classmethod
    def collected(cls, own, other, block):
        made = cls([(own, 0, 0), (other, 0, 1)], block)
        here = lax.axis_index(PLANE)
        made.slots = chip_slots() * block
        made.jobs = [
            (i, (3 * chip + m) * block, m, 0, block, 4 * i + chip)
            for i in range(2)
            for chip in range(4)
            for m in range(3)
        ]
        return made

    def scratch(self):
        return [
            pltpu.VMEM((3, self.width, self.units), BF16),
            pltpu.SemaphoreType.DMA((len(self.jobs),)),
        ]

    def copies(self, slots, refs, held, sems, matrix):
        made = []
        for n, (i, source, m, to, rows, slot) in enumerate(self.jobs):
            if m == matrix:
                base = 0 if slot is None else pl.multiple_of(slots[slot], 16)
                made.append(
                    pltpu.make_async_copy(
                        refs[i].at[pl.ds(source, rows)],
                        held.at[m, pl.ds(base + to, rows)],
                        sems.at[n],
                    )
                )
        return made


def ffn_forward_kernel(blocks, normed, part):
    rows, width = normed.shape
    units = blocks.units
    count = len(blocks.pieces)
    first = part is None

    def kernel(slots, n_ref, *refs):
        if not first:
            part_ref, refs = refs[0], refs[1:]
        pieces, (act, slope, hidden, out, held, sems) = refs[:count], refs[count:]
        start = pl.program_id(0) == 0

        def wait(m):
            @pl.when(start)
            def _():
                for copy in blocks.copies(slots, pieces, held, sems, m):
                    copy.wait()

        @pl.when(start)
        def _():
            for m in range(3):
                for copy in blocks.copies(slots, pieces, held, sems, m):
                    copy.start()

        left = n_ref[...]
        wait(0)
        gate = dot(left, held[0])
        wait(1)
        up = dot(left, held[1])
        square_gate = gate * gate
        turn = jnp.tanh(GELU_A * (gate + GELU_B * gate * square_gate))
        spread = 0.5 * (1.0 + turn)
        gelu = gate * spread
        bend = spread + 0.5 * gate * (1.0 - turn * turn) * (
            GELU_A * (1.0 + 3.0 * GELU_B * square_gate)
        )
        act[...] = gelu.astype(BF16)
        slope[...] = (up * bend).astype(BF16)
        low = (gelu * up).astype(BF16)
        hidden[...] = low
        wait(2)
        made = dot(low, held[2], (1, 1))
        out[...] = made if first else part_ref[...] + made

    by_rows = pl.BlockSpec((SEG, width), lambda i, s: (i, 0))
    by_units = pl.BlockSpec((SEG, units), lambda i, s: (i, 0))
    return prefetch_call(
        kernel,
        blocks.slots,
        (rows // SEG,),
        (normed,) + (() if first else (part,)) + blocks.pieces,
        [by_rows] + ([] if first else [by_rows]) + [whole(pl.ANY)] * count,
        [like((rows, units), BF16)] * 3 + [like((rows, width))],
        [by_units] * 3 + [by_rows],
        blocks.scratch(),
        mib=58,
        us=16,
    )


def ffn_backward_kernel(blocks, d_ffn, act, slope, back):
    rows, width = d_ffn.shape
    units = blocks.units
    count = len(blocks.pieces)
    first = back is None

    def kernel(slots, d_ref, act_ref, slope_ref, *refs):
        if not first:
            back_ref, refs = refs[0], refs[1:]
        pieces, (d_gate, d_up, out, held, sems) = refs[:count], refs[count:]
        start = pl.program_id(0) == 0

        def wait(m):
            @pl.when(start)
            def _():
                for copy in blocks.copies(slots, pieces, held, sems, m):
                    copy.wait()

        @pl.when(start)
        def _():
            for m in (2, 0, 1):
                for copy in blocks.copies(slots, pieces, held, sems, m):
                    copy.start()

        wait(2)
        d_hidden = dot(d_ref[...], held[2])
        to_gate = (d_hidden * slope_ref[...].astype(F32)).astype(BF16)
        to_up = (d_hidden * act_ref[...].astype(F32)).astype(BF16)
        d_gate[...] = to_gate
        d_up[...] = to_up
        wait(0)
        wait(1)
        made = dot(to_gate, held[0], (1, 1)) + dot(to_up, held[1], (1, 1))
        out[...] = made if first else back_ref[...] + made

    by_rows = pl.BlockSpec((SEG, width), lambda i, s: (i, 0))
    by_units = pl.BlockSpec((SEG, units), lambda i, s: (i, 0))
    return prefetch_call(
        kernel,
        blocks.slots,
        (rows // SEG,),
        (d_ffn, act, slope) + (() if first else (back,)) + blocks.pieces,
        [by_rows, by_units, by_units] + ([] if first else [by_rows]) + [whole(pl.ANY)] * count,
        [like((rows, units), BF16)] * 2 + [like((rows, width))],
        [by_units] * 2 + [by_rows],
        blocks.scratch(),
        mib=58,
        us=16,
    )


def ffn_end_kernel(plane, ffn_own, ffn_other, mid, cotangent, gain):
    rows, width = mid.shape

    def kernel(p, own_ref, other_ref, mid_ref, up_ref, gain_ref, d_out, d_turned, out, share):
        i = pl.program_id(0)
        g = gain_ref[...]

        def run(ref, own):
            ffn = ref[...].astype(F32)
            r = row_scale(ffn)
            incoming = up_ref[...].astype(F32)
            out[...] = (mid_ref[...] + ffn * r * g).astype(BF16)
            if own:
                share[...] = jnp.sum(incoming * ffn * r, axis=0, keepdims=True)
            scaled = g * incoming
            inner = jnp.mean(ffn * scaled, axis=-1, keepdims=True)
            made = (r * scaled - ffn * (r * r * r) * inner).astype(BF16)
            d_out[...] = made
            d_turned[...] = made.T

        pl.when(i == 0)(lambda: run(own_ref, True))
        pl.when(i == 1)(lambda: run(other_ref, False))

    once = pl.BlockSpec((SEG, width), lambda i, p: (0, 0))
    by_rows = pl.BlockSpec((SEG, width), lambda i, p: (i, 0))
    return prefetch_call(
        kernel,
        plane.reshape(1),
        (2,),
        (ffn_own, ffn_other, mid, cotangent, gain),
        [once, once, by_rows, pl.BlockSpec((SEG, width), lambda i, p: (p[0] ^ i, 0)), full(gain)],
        [like((rows, width), BF16), like((width, rows), BF16), like((rows, width), BF16), like((1, width))],
        [
            by_rows,
            pl.BlockSpec((width, SEG), lambda i, p: (0, i)),
            by_rows,
            pl.BlockSpec((1, width), lambda i, p: (0, 0)),
        ],
        us=3.4,
    )


def spread_kernel(plane, blocks, order, dtype):
    width = blocks[0].shape[1]
    count = len(blocks)
    spots = [(n, r) for n, x in enumerate(blocks) for r in range(x.shape[0] // SEG)]

    def kernel(p, *refs):
        ins, out = refs[:count], refs[count]
        for i, (n, r) in enumerate(spots):

            @pl.when(pl.program_id(0) == p[0] ^ order[i])
            def _(n=n, r=r):
                out[...] = ins[n][r * SEG : (r + 1) * SEG].astype(dtype)

    return prefetch_call(
        kernel,
        plane.reshape(1),
        (4,),
        tuple(blocks),
        [full(x) for x in blocks],
        like((4 * SEG, width), dtype),
        pl.BlockSpec((SEG, width), lambda i, p: (i, 0)),
        us=3,
    )


def attention_back_kernel(
    flags, back, got, mid, cotangent, gain_ffn, attn, gain_post, wo_t, query, query_raw, gain_query,
    slots, cos_table, sin_table, head,
):
    width, total = wo_t.shape
    heads = total // head
    half = head // 2
    scale = head**-0.5

    def kernel(
        f, back_ref, got_ref, mid_ref, up_ref, gain_ffn_ref, attn_ref, gain_post_ref, w_ref, q_ref,
        raw_ref, gain_query_ref, slots_ref, c_ref, s_ref,
        d_mid, d_attn, d_attn_turned, shares, d_query, query_share, d_self, d_a, d_b, sums,
    ):
        h = pl.program_id(0)

        @pl.when(h == 0)
        def _():
            incoming = back_ref[...] + got_ref[...].astype(F32)
            add, share = norm_back(mid_ref[...], gain_ffn_ref[...], incoming)
            made = up_ref[...].astype(F32) + add
            d_mid[...] = made
            d_a_low, share_post = norm_back(attn_ref[...], gain_post_ref[...], made)
            low = d_a_low.astype(BF16)
            d_attn[...] = low
            d_attn_turned[...] = low.T
            shares[0:1, :] = jnp.sum(share, axis=0, keepdims=True)
            shares[1:2, :] = jnp.sum(share_post, axis=0, keepdims=True)
            sums[...] = jnp.zeros_like(sums)
            query_share[...] = jnp.zeros_like(query_share)

        keys, values = slots_ref[:, :head], slots_ref[:, head:]
        q = q_ref[...]
        d_heads = dot(d_attn[...], w_ref[...]).astype(BF16)
        probs = softmax_of(q, keys, scale, f[4], f[5])
        d_probs = dot(d_heads, values, (1, 1))
        d_scores = probs * (d_probs - jnp.sum(d_probs * probs, axis=-1, keepdims=True))
        d_scores = d_scores.astype(BF16)
        sums[:, :head] += dot(d_scores, q, (0, 0))
        sums[:, head:] += dot(probs.astype(BF16), d_heads, (0, 0))
        turned = rotate(dot(d_scores, keys) * scale, c_ref[...], -s_ref[...])
        made, share = norm_back(raw_ref[...], gain_query_ref[...], turned)
        d_query[...] = made.astype(BF16)
        query_share[...] += jnp.sum(share, axis=0, keepdims=True)

        @pl.when(h == heads - 1)
        def _():
            sums[:, :head] = sums[:, :head] * scale
            d_self[...] = sums[:SEG]
            d_a[...] = sums[SEG : 2 * SEG].astype(BF16)
            d_b[...] = sums[2 * SEG :].astype(BF16)

    def once(shape):
        return pl.BlockSpec(shape, lambda h, f: (0,) * len(shape))

    by_head = pl.BlockSpec((SEG, head), lambda h, f: (0, h))
    table = pl.BlockSpec((SEG, half), lambda h, f: (f[1], 0))
    rows = once((SEG, width))
    return prefetch_call(
        kernel,
        flags,
        (heads,),
        (back, got, mid, cotangent, gain_ffn, attn, gain_post, wo_t, query, query_raw, gain_query,
         slots, cos_table, sin_table),
        [
            rows,
            rows,
            rows,
            pl.BlockSpec((SEG, width), lambda h, f: (f[1], 0)),
            full(gain_ffn),
            rows,
            full(gain_post),
            pl.BlockSpec((width, head), lambda h, f: (0, h)),
            by_head,
            by_head,
            full(gain_query),
            full(slots),
            table,
            table,
        ],
        [
            like((SEG, width)),
            like((SEG, width), BF16),
            like((width, SEG), BF16),
            like((2, width)),
            like((SEG, total), BF16),
            like((1, head)),
            like((SEG, 2 * head)),
            like((SEG, 2 * head), BF16),
            like((SEG, 2 * head), BF16),
        ],
        [
            rows,
            rows,
            once((width, SEG)),
            once((2, width)),
            by_head,
            once((1, head)),
            once((SEG, 2 * head)),
            once((SEG, 2 * head)),
            once((SEG, 2 * head)),
        ],
        [pltpu.VMEM((3 * SEG, 2 * head), F32)],
        us=12,
    )


def tokens_back_kernel(
    plane, terms, key_raw, gain_key, cos_table, sin_table, wkv, d_normed, d_mid, tokens, gain_in
):
    width = d_mid.shape[1]
    head = key_raw.shape[1]
    half = head // 2
    count = len(terms)

    def kernel(p, *refs):
        terms_in, refs = refs[:count], refs[count:]
        (raw_ref, gain_ref, c_ref, s_ref, w_ref, dn_ref, mid_ref, t_ref, gain_in_ref) = refs[:9]
        d_kv, rows_out, share_key, share_in = refs[9:]
        total = terms_in[0][...].astype(F32)
        for term in terms_in[1:]:
            total = total + term[...].astype(F32)
        turned = rotate(total[:, :head], c_ref[...], -s_ref[...])
        made, share = norm_back(raw_ref[...], gain_ref[...], turned)
        share_key[...] = jnp.sum(share, axis=0, keepdims=True)
        low = jnp.concatenate([made, total[:, head:]], axis=1).astype(BF16)
        d_kv[...] = low
        incoming = dn_ref[...] + dot(low, w_ref[...], (1, 1))
        add, share = norm_back(t_ref[...].astype(F32), gain_in_ref[...], incoming)
        share_in[...] = jnp.sum(share, axis=0, keepdims=True)
        rows_out[...] = (mid_ref[...] + add).astype(BF16)

    table = pl.BlockSpec((SEG, half), lambda i, p: (p[0], 0))
    ins = (*terms, key_raw, gain_key, cos_table, sin_table, wkv, d_normed, d_mid, tokens, gain_in)
    specs = [full(x) for x in ins]
    specs[count + 2] = specs[count + 3] = table
    specs[count + 7] = pl.BlockSpec((SEG, width), lambda i, p: (p[0], 0))
    outs = [like((SEG, 2 * head), BF16), like((SEG, width), BF16), like((1, head)), like((1, width))]
    return prefetch_call(
        kernel, plane.reshape(1), (1,), ins, specs, outs, [full(o) for o in outs], us=3
    )


def window_kernel(flags, d_self, d_a, d_b, back_1, back_2, back_3):
    shape = (2,) + d_self.shape

    def kernel(f, own_ref, a_ref, b_ref, b1, b2, b3, sent, kept):
        role, plane = f[0], f[1]
        near = role == 0
        ats = [
            plane,
            jnp.where(near & (f[4] > 0), f[2], -1),
            jnp.where(near & (f[5] > 0), f[3], -1),
            jnp.where(role <= 1, f[6], -1),
            jnp.where(role <= 1, f[7], -1),
            jnp.where(near, f[8], -1),
        ]
        refs = (own_ref, a_ref, b_ref, b1, b2, b3)
        for out, k, other in ((sent, 0, 1), (sent, 1, 3), (kept, 0, 0), (kept, 1, 2)):
            number = plane ^ other
            total = jnp.zeros(out.shape[1:], F32)
            for at, ref in zip(ats, refs):
                total = total + jnp.where(at == number, ref[...].astype(F32), 0.0)
            out[k] = total.astype(BF16)

    return pl.pallas_call(
        kernel,
        out_shape=[like(shape, BF16)] * 2,
        in_specs=[whole(pltpu.SMEM)] + [whole(pltpu.VMEM)] * 6,
        out_specs=[whole(pltpu.VMEM)] * 2,
        compiler_params=params(58),
        cost_estimate=cost(2.4),
    )(flags, d_self, d_a, d_b, back_1, back_2, back_3)


def z_first(sent, kept, kept_far):
    got = across(sent, 1).astype(F32)
    return tie((kept.astype(F32) + got[0]).astype(BF16), (kept_far.astype(F32) + got[1]).astype(BF16))


def z_halve(x):
    here = lax.axis_index("gx")

    def at(n):
        return lax.dynamic_index_in_dim(x, n, 0, keepdims=False)

    return z_first(jnp.stack([at(here ^ 1), at(here ^ 3)]), at(here), at(here ^ 2))


def body(
    tokens,
    parents,
    w_query,
    w_key,
    w_value,
    w_out,
    w_gate,
    w_up,
    w_down,
    g_attn_in,
    g_attn_out,
    g_ffn_in,
    g_ffn_out,
    g_query,
    g_key,
    cotangent,
):
    column = lax.axis_index(PLANE)
    columns = lax.axis_size(PLANE)
    plane = lax.axis_index("gx")
    planes = lax.axis_size("gx")
    width = tokens.shape[1]
    head_width = w_key.shape[1]
    heads = planes * w_query.shape[1] // head_width
    block, small = w_query.shape[0], w_key.shape[0]
    gains_len = 4 * block + 2 * g_query.shape[0]
    pack_width = 2 * head_width
    gain_rows = -(-gains_len // pack_width)
    used = small + gain_rows
    gain_spot = -(-small // 8) * 8
    pack_rows = -(-(block + gain_spot + gain_rows) // 16) * 16

    core = lax.axis_index("gc")
    down_t = w_down.T
    ffn_mine = jnp.concatenate([w_gate, w_up, down_t], axis=0)
    gains = jnp.concatenate([g_attn_in, g_attn_out, g_ffn_in, g_ffn_out, g_query, g_key])
    gains = jnp.pad(gains, (0, gain_rows * pack_width - gains_len)).reshape(gain_rows, pack_width)
    pack = jnp.concatenate(
        [
            jnp.concatenate([w_query, w_out.T], axis=1),
            jnp.concatenate([w_key, w_value], axis=1),
            jnp.zeros((gain_spot - small, pack_width), BF16),
            gains,
            jnp.zeros((pack_rows - block - gain_spot - gain_rows, pack_width), BF16),
        ],
        axis=0,
    )
    flags = flags_kernel(parents, jnp.stack([column, plane]).astype(jnp.int32))
    depth = flags[9:13, None] * SEG + jnp.arange(SEG, dtype=jnp.int32)[None, :]
    half_width = head_width // 2
    rates = 10000.0 ** (-jnp.arange(half_width, dtype=F32) / half_width)
    turned = depth.reshape(-1).astype(F32)[:, None] * rates[None, :]
    cos_table, sin_table = jnp.cos(turned), jnp.sin(turned)
    if square():
        ffn_x, ffn_y = send_near(ffn_mine)
        pack = lax.all_gather(pack, "gx", axis=0)
        pack, other_gu = tie(pack, ffn_mine[: 2 * block])
        their_gu = across(other_gu, 2)
        pack_x, pack_y = send_near(pack)
        ffn_x, ffn_y, pack, pack_x, pack_y, cos_table, sin_table = tie(
            ffn_x, ffn_y, pack, pack_x, pack_y, cos_table, sin_table
        )
        pack_far = send_far(pack_x, pack_y)
        ffn_far = send_far(ffn_x, ffn_y)
        pack_all = collect((pack, pack_x, pack_y, *pack_far), planes)
        pack_all, their_gu, other_down = tie(pack_all, their_gu, down_t)
        their_down = across(other_down, 2)
        pack_other = swap(pack_all, "gc")
        wq, wo_t, wkv, gains = unpack(
            [pack_all, pack_other], block, head_width, gain_spot, gain_rows
        )
    else:
        pack = lax.all_gather(pack, "gx", axis=0, tiled=True)
        pack = lax.all_gather(pack, PLANE, axis=0).reshape(columns, planes, pack_rows, pack_width)

        def from_blocks(blocks):
            return blocks.transpose(0, 2, 1, 3).reshape(columns * block, -1)

        wq = from_blocks(pack[:, :, :block, :head_width])
        wo_t = from_blocks(pack[:, :, :block, head_width:])
        wkv = pack[:, :, block : block + small].transpose(1, 0, 2, 3).reshape(width, pack_width)
        gains = pack[:, 0, block + gain_spot : block + gain_spot + gain_rows]

        def ffn_weights(mine):
            stacked = lax.all_gather(mine, PLANE, axis=0).reshape(columns, 3, block, -1)
            return Blocks([stacked[:, i].reshape(width, -1) for i in range(3)], None)

        quarter_mine = ffn_weights(ffn_mine)
        quarter_theirs = ffn_weights(across(ffn_mine, 2))

    gains = gains.reshape(columns, -1)[:, :gains_len].astype(F32)
    gain_in, gain_post, gain_ffn, gain_last = [
        gains[:, i * block : (i + 1) * block].reshape(1, -1) for i in range(4)
    ]
    gain_query, gain_key = [
        gains[:, 4 * block + i * g_query.shape[0] :][:, : g_query.shape[0]].reshape(1, -1)
        for i in range(2)
    ]

    role = column % 4
    trees = range(columns // 4)
    route_1 = [(4 * t + i, 4 * t + i + 1) for t in trees for i in (0, 1)]
    route_2 = [(4 * t + i, 4 * t + i + 2) for t in trees for i in (0, 1)]
    route_3 = [(4 * t + i, 4 * t + i + 1) for t in trees for i in (0, 2)]

    def send(x, route):
        return lax.ppermute(x, PLANE, route)

    def send_back(x, route):
        return lax.ppermute(x, PLANE, [(b, a) for a, b in route])

    pairs, normed_own, key_raw, send_1, send_2, send_3 = key_value_kernel(
        flags, tokens, gain_in, wkv, gain_key, cos_table, sin_table
    )
    if square():
        send_1, send_2 = tie(send_1, send_2)
    got_1 = send(send_1, route_1)
    got_2 = send(send_2, route_2)
    query, query_raw = query_kernel(
        plane, normed_own, wq, gain_query, cos_table, sin_table, head_width
    )
    if square():
        query, ffn_x, ffn_y, their_down, *ffn_far = tie(query, ffn_x, ffn_y, their_down, *ffn_far)
        theirs = jnp.concatenate([their_gu, their_down], axis=0)
        mine_all = collect((ffn_mine, ffn_x, ffn_y, *ffn_far), 3 * block)
        got_1, got_2, mine_all, theirs = tie(got_1, got_2, mine_all, theirs)
        mine_other = swap(mine_all, "gc")
        their_x, their_y = send_near(theirs)
    got_3 = send(jnp.where(role == 2, got_2, send_3), route_3)
    heads_low, slots = attention_kernel(flags, query, pairs, got_1, got_2, got_3)

    if square():
        heads_low, mine_other = tie(heads_low, mine_other)
        heads_got = across(heads_low, 1)
        quarter_mine = Blocks.collected(mine_all, mine_other, block)
    else:
        heads_got = across(heads_low, 1)
    attn, mid, normed_ffn = middle_kernel(
        plane, heads_low, heads_got, wo_t, tokens, gain_post, gain_ffn
    )
    if square():
        normed_ffn, their_x, their_y = tie(normed_ffn, their_x, their_y)
        their_far = send_far(their_x, their_y)
        near_pieces = both_cores([(theirs, 0, 0), (their_x, 0, 2), (their_y, 0, 4)])
    act_m, slope_m, hidden_m, ffn_part = ffn_forward_kernel(quarter_mine, normed_ffn, None)
    if square():
        ffn_part, *their_far = tie(ffn_part, *their_far)
        far_pieces = both_cores([(their_far[0], 0, 6), (their_far[1], their_far[0].shape[0], 6)])
        quarter_theirs = Blocks(near_pieces + far_pieces, block)
    act_t, slope_t, hidden_t, ffn_part = ffn_forward_kernel(quarter_theirs, normed_ffn, ffn_part)
    ffn_got = across(ffn_part[SEG:].astype(BF16), 1)
    ffn_own = (ffn_part[:SEG] + ffn_got.astype(F32)).astype(BF16)
    ffn_other = across(ffn_own, 1)
    d_ffn_low, d_ffn_t, output, d_gain_last = ffn_end_kernel(
        plane, ffn_own, ffn_other, mid, cotangent, gain_last
    )

    output_far = [across(output[:SEG], 2)]
    d_gate_t, d_up_t, back = ffn_backward_kernel(quarter_theirs, d_ffn_low, act_t, slope_t, None)
    if square():
        lefts = (normed_ffn.T, d_ffn_t)
        send_theirs = ffn_weight_grads(1 - core, *lefts, d_gate_t, d_up_t, hidden_t, block)
        keep_theirs = ffn_weight_grads(core, *lefts, d_gate_t, d_up_t, hidden_t, block)
        back, send_theirs, keep_theirs, output_far[0] = tie(
            back, send_theirs, keep_theirs, output_far[0]
        )
        recv_theirs = swap(send_theirs, "gc")
    d_gate_m, d_up_m, back = ffn_backward_kernel(quarter_mine, d_ffn_low, act_m, slope_m, back)
    if square():
        back, recv_theirs = tie(back, recv_theirs)
        theirs = Scatter(keep_theirs, recv_theirs)
    back_got = across(back[SEG:].astype(BF16), 1)
    if square():
        theirs_far = send_xy(theirs.far_blocks())
        theirs_first = send_xy(theirs.first_blocks())
        back_got, output = tie(back_got, output)
    else:
        grads = []
        for d_gate, d_up, hidden in ((d_gate_m, d_up_m, hidden_m), (d_gate_t, d_up_t, hidden_t)):
            blocks = [
                dot(normed_ffn, d_gate, (0, 0)),
                dot(normed_ffn, d_up, (0, 0)),
                dot(d_ffn_low, hidden, (0, 0)),
            ]
            blocks = [m.astype(BF16).reshape(columns, block, -1) for m in blocks]
            grads.append(plane_scatter(jnp.concatenate(blocks, axis=1)))
        ffn_grad = grads[0] + across(grads[1].astype(BF16), 2).astype(F32)

    output_far.append(across(output[SEG : SEG + SEG // 2], 2))

    (
        d_mid, d_attn_low, d_attn_t, d_gains_mid, d_query_low, d_gain_query, d_self, d_a, d_b,
    ) = attention_back_kernel(
        flags, back, back_got, mid, cotangent, gain_ffn, attn, gain_post, wo_t, query, query_raw,
        gain_query, slots, cos_table, sin_table, head_width,
    )
    if square():
        d_a, d_b, output_far[1], output, d_gate_m = tie(
            d_a, d_b, output_far[1], output, d_gate_m
        )
    output_far.append(across(output[SEG + SEG // 2 :], 2))
    back_1 = send_back(d_a, route_1)
    back_3 = send_back(d_b, route_3)
    if square():
        theirs_second = theirs.second_blocks(*theirs_far)
        made = (*lefts, d_gate_m, d_up_m, hidden_m)
        send_mine = ffn_weight_grads(1 - core, *made, block)
        d_a, d_b, back_1, back_3, send_mine, d_gate_m, *flat = tie(
            d_a, d_b, back_1, back_3, send_mine, d_gate_m, *theirs_first, *theirs_second
        )
        theirs_first, theirs_second = flat[:2], flat[2:]
    d_b_far = jnp.where(role == 2, d_b.astype(F32) + back_3.astype(F32), 0.0).astype(BF16)
    to_back_2 = jnp.where(role == 3, d_a, d_b_far)
    back_2 = send_back(to_back_2, route_2)
    if square():
        theirs_second = send_xy(theirs_second)
        keep_mine = ffn_weight_grads(core, *lefts, d_gate_m, d_up_m, hidden_m, block)
        back_2, output_far[2], keep_mine, send_mine = tie(
            back_2, output_far[2], keep_mine, send_mine
        )
        recv_mine = swap(send_mine, "gc")
    sent, kept = window_kernel(flags, d_self, d_a, d_b, back_1, back_2, back_3)
    kept, passed = z_first(sent, kept[0], kept[1])
    if square():
        passed, d_query_low, keep_mine, recv_mine = tie(
            passed, d_query_low, keep_mine, recv_mine
        )
    d_normed_query = dot(d_query_low, wq, (1, 1))
    own_terms = [kept, across(passed, 2)]
    if square():
        mine = Scatter(keep_mine, recv_mine)
        mine_far = mine.far_blocks()
        theirs_sum = theirs.total(theirs_first, theirs_second).astype(BF16)
        own_terms[1], theirs_sum, d_normed_query, d_gains_mid, d_gain_last, d_gain_query, *mine_far = tie(
            own_terms[1], theirs_sum, d_normed_query, d_gains_mid, d_gain_last, d_gain_query, *mine_far
        )
        mine_far = send_xy(mine_far)
    d_kv_low, token_rows, d_gain_key, d_gain_in = tokens_back_kernel(
        plane, own_terms, key_raw, gain_key, cos_table, sin_table, wkv, d_normed_query, d_mid,
        tokens, gain_in,
    )
    tokens_far = across(token_rows, 2)

    grad_kv = dot(normed_own, d_kv_low, (0, 0)).astype(BF16)
    grad_kv = grad_kv.reshape(planes, columns, small, -1).transpose(1, 0, 2, 3)
    gain_sums = [
        d_gain_in,
        d_gains_mid[1:],
        d_gains_mid[:1],
        d_gain_last,
        d_gain_query,
        d_gain_key,
    ]
    gain_sums = jnp.concatenate([g.reshape(columns, -1) for g in gain_sums], axis=1).astype(BF16)
    gain_sums = jnp.pad(gain_sums, ((0, 0), (0, gain_rows * pack_width - gains_len)))
    gain_sums = jnp.broadcast_to(
        gain_sums.reshape(columns, 1, gain_rows, pack_width),
        (columns, planes, gain_rows, pack_width),
    )
    rest_rows = pack_rows - block
    rest = jnp.concatenate(
        [grad_kv, gain_sums, jnp.zeros((columns, planes, pack_rows - block - used, pack_width), BF16)],
        axis=2,
    ).reshape(columns, planes * rest_rows, pack_width)
    if square():
        attn_lefts = (normed_own.T, d_query_low, d_attn_t, heads_low, rest)
        attn_send = attention_weight_grads(1 - core, *attn_lefts, block, planes)
        attn_keep = attention_weight_grads(core, *attn_lefts, block, planes)
        attn_received = swap(attn_send, "gc")
        attn_keep, attn_received = tie(attn_keep, attn_received)
        attn_work = Scatter(attn_keep, attn_received)
        attn_far = send_xy(attn_work.far_blocks())
        tokens_far, theirs_sum, *flat = tie(tokens_far, theirs_sum, *attn_far, *mine_far)
        attn_far, mine_far = flat[:2], flat[2:]
        attn_near = send_xy(attn_work.near_blocks(*attn_far))
        tokens_near = across(jnp.concatenate([token_rows, tokens_far], axis=0), 1)
        gate_sum = across(theirs_sum[:block], 2)
        mine_second = mine.second_blocks(*mine_far)
        gate_sum, tokens_near, other_up, *flat = tie(
            gate_sum, tokens_near, theirs_sum[block : 2 * block], *attn_near, *mine_second
        )
        up_sum = across(other_up, 2)
        mine_first = send_xy(mine.first_blocks())
        mine_second = flat[2:]
        grads = attn_work.near_total(*flat[:2])
    else:

        def to_blocks(grad):
            return grad.astype(BF16).reshape(columns, block, planes, -1).transpose(0, 2, 1, 3)

        grads = jnp.concatenate(
            [
                to_blocks(dot(normed_own, d_query_low, (0, 0))),
                to_blocks(dot(d_attn_low, heads_low, (0, 0))),
            ],
            axis=3,
        ).reshape(columns, planes * block, pack_width)
        grads = jnp.concatenate(
            [grads.reshape(columns, planes, block, -1), rest.reshape(columns, planes, rest_rows, -1)],
            axis=2,
        ).reshape(columns, planes * pack_rows, pack_width)
        grads = plane_scatter(grads)
    grads = grads.reshape(planes, pack_rows, pack_width)
    rest = jnp.broadcast_to(
        grads[:1, block + small :], (planes, pack_rows - block - small, pack_width)
    )
    grads = jnp.concatenate([grads[:, : block + small], rest], axis=1).astype(BF16)
    kept, passed = z_halve(grads)
    if square():
        passed, up_sum, other_down, *mine_second = tie(
            passed, up_sum, theirs_sum[2 * block :], *mine_second
        )
        mine_second = send_xy(mine_second)
        down_sum = across(other_down, 2)
    else:
        tokens_near = across(jnp.concatenate([token_rows, tokens_far], axis=0), 1)
    grads = kept.astype(F32) + across(passed, 2).astype(F32)
    if square():
        ffn_grad = mine.total(mine_first, mine_second) + jnp.concatenate(
            [gate_sum, up_sum, down_sum], axis=0
        ).astype(F32)
    grad_tokens = spread_kernel(plane, (token_rows, tokens_far, tokens_near), (0, 2, 1, 3), F32)
    output_far[1:] = [jnp.concatenate(output_far[1:], axis=0)]
    output = spread_kernel(plane, (output, *output_far), (0, 1, 2, 3), BF16)
    gain_grads = grads[block + small : block + used].reshape(-1)
    return (
        output,
        grad_tokens,
        gain_grads[:block],
        gain_grads[block : 2 * block],
        gain_grads[2 * block : 3 * block],
        gain_grads[3 * block : 4 * block],
        gain_grads[4 * block : 4 * block + g_query.shape[0]],
        gain_grads[4 * block + g_query.shape[0] : gains_len],
        grads[:block, :head_width],
        grads[block : block + small, :head_width],
        grads[block : block + small, head_width:],
        grads[:block, head_width:].T,
        ffn_grad[:block],
        ffn_grad[block : 2 * block],
        ffn_grad[2 * block :].T,
    )


def solution(mesh):
    side = math.isqrt(mesh.shape["gy"] // 2)
    split = Mesh(mesh.devices.reshape(mesh.shape["gx"], side, side, 2), ("gx",) + PLANE)
    whole = ("gx",) + PLANE
    return jax.shard_map(
        body,
        mesh=split,
        in_specs=(
            P(PLANE, None),
            P(),
            P(PLANE, "gx"),
            P(whole, None),
            P(whole, None),
            P("gx", PLANE),
            P(PLANE, "gx"),
            P(PLANE, "gx"),
            P("gx", PLANE),
            P(PLANE),
            P(PLANE),
            P(PLANE),
            P(PLANE),
            P(PLANE),
            P(PLANE),
            P(PLANE, None),
        ),
        out_specs=(
            P(PLANE, None),
            P(PLANE, None),
            P(PLANE),
            P(PLANE),
            P(PLANE),
            P(PLANE),
            P(PLANE),
            P(PLANE),
            P(PLANE, "gx"),
            P(whole, None),
            P(whole, None),
            P("gx", PLANE),
            P(PLANE, "gx"),
            P(PLANE, "gx"),
            P("gx", PLANE),
        ),
        check_vma=False,
    )
```
